128 devices in a mesh: seq: 16 (over z, y_lo, core), tp: 8 (over x, y_hi).
Axes of the slice: x: 4, y: 4 (y_hi: 2, y_lo: 2; y = y_hi * 2 + y_lo), z: 4, core: 2. Of those that a mesh axis runs over, the one named last changes fastest.
Arguments:
- queries: bfloat16 [8192, 4096], P('seq', 'tp'), may hold values from -6 to 6
- audio_keys: bfloat16 [2048, 4096], P('seq', 'tp'), may hold values from -6 to 6
- audio_values: bfloat16 [2048, 4096], P('seq', 'tp'), may hold values from -12 to 12
- out_weight: bfloat16 [4096, 8192], P('tp'), may hold values from -0.09375 to 0.09375
- mix_gate: float32 [1], replicated, may hold values from 0.3 to 1.2
- block_mask: int32 [64, 16], P('seq'), may hold values from 0 to 1, as said below
- cotangent: bfloat16 [8192, 8192], P(('seq', 'tp')), may hold values from -24 to 24
Outputs:
- layer_out: bfloat16 [8192, 8192], P(('seq', 'tp'))
- grad_queries: bfloat16 [8192, 4096], P('seq', 'tp')
- grad_keys: bfloat16 [2048, 4096], P('seq', 'tp')
- grad_values: bfloat16 [2048, 4096], P('seq', 'tp')
- grad_weight: bfloat16 [4096, 8192], P('tp', 'seq')
The draws below stay inside these ranges and needn't reach their ends.
Inputs may be any that keep to these rules, and one draw needn't show every extreme that they name: Every row of block_mask holds at least one 1.
All inputs are finite; a program needn't handle non-finite values.
Results may differ from the reference program's by a relative error of at most 0.025.
Values may be sent and summed in bfloat16 or wider, within the bound.
A program may use at most 128 MiB of HBM per device.

```python
import jax
import jax.numpy as jnp
from jax import lax

D = 8192
HD = 128
HEADS = 32
BLK = 128
TXT_DEV = 512
TEXT = 8192
AUDIO = 2048
N_SEQ = 16
N_TP = 8


def draw_queries(key, part):
    key = jax.random.fold_in(key, 11)
    noise_key = jax.random.fold_in(key, 0)
    values = 1.4 * jax.random.normal(noise_key, (TEXT, HEADS * HD), jnp.float32)
    return jnp.clip(values, -6.0, 6.0).astype(jnp.bfloat16)


def draw_audio_keys(key, part):
    key = jax.random.fold_in(key, 17)
    noise_key = jax.random.fold_in(key, 0)
    values = 1.4 * jax.random.normal(noise_key, (AUDIO, HEADS * HD), jnp.float32)
    return jnp.clip(values, -6.0, 6.0).astype(jnp.bfloat16)


def draw_block_mask(key, part):
    key = jax.random.fold_in(key, 29)
    bit_key, chosen_key = jax.random.split(key, 2)
    coin_bits = jax.random.randint(bit_key, (TEXT // BLK, AUDIO // BLK), 0, 2, jnp.int32)
    chosen = jax.random.randint(chosen_key, (TEXT // BLK, 1), 0, AUDIO // BLK, jnp.int32)
    column = jnp.arange(AUDIO // BLK, dtype=jnp.int32)[None, :]
    return jnp.maximum(coin_bits, (column == chosen).astype(jnp.int32))


def strengthened(result, own_key, source, target, blocks, factor):
    def block_of(position):
        return (jnp.arange(result.shape[position]) // (result.shape[position] // blocks)).reshape((-1,) + (1,) * (result.ndim - 1 - position))

    first = jax.random.permutation(own_key, blocks)[block_of(target)]
    second = (block_of(target) + blocks // 2) % blocks
    return jnp.where((block_of(source) == first) | (block_of(source) == second), factor * result, result)


def shard_levels(rng, dims, pieces, smallest, top_value):
    loudness = 1.0
    for dim, blocks in pieces:
        heights = jax.random.uniform(jax.random.fold_in(jax.random.fold_in(rng, 6), dim), (blocks,), jnp.float32, smallest / len(pieces), top_value / len(pieces))
        loudness = loudness * jnp.repeat(jnp.exp(heights), dims[dim] // blocks).reshape((-1,) + (1,) * (len(dims) - 1 - dim))
    return loudness


def gaussian(rng, extent, scale, reach, cuts=(), held_as=jnp.bfloat16):
    drawn = jax.random.normal(rng, extent, jnp.float32) * scale
    if len(cuts) > 0:
        drawn = shard_levels(rng, extent, cuts, -0.22, 0.18) * drawn
    return jnp.clip(drawn, min=-reach, max=reach).astype(held_as)


def gaussian_with(key, dims, width, bound, cuts, heavy, held_as=jnp.bfloat16):
    values = width * jax.random.normal(key, dims, jnp.float32)
    if cuts:
        values = values * shard_levels(key, dims, cuts, -0.22, 0.18)
    return jnp.clip(strengthened(values, jax.random.fold_in(key, 3), *heavy), -bound, bound).astype(held_as)


def setup_inputs(seed: int = 0) -> dict:
    arg_keys = jax.random.split(jax.random.key(seed), 8)
    queries = draw_queries(jax.random.fold_in(arg_keys[7], 71), 0)
    audio_keys = draw_audio_keys(jax.random.fold_in(arg_keys[7], 71), 0)
    audio_values = gaussian(arg_keys[2], (AUDIO, HEADS * HD), 3.0, 12.0, ((0, 16), (1, 8)))
    out_weight = gaussian(arg_keys[3], (HEADS * HD, D), (HEADS * HD) ** -0.5, 0.09375, ((0, 8),))
    mix_gate = jnp.clip(jax.random.uniform(arg_keys[4], (1,), jnp.float32, 0.3, 1.2), 0.3, 1.2)
    block_mask = draw_block_mask(jax.random.fold_in(arg_keys[7], 71), 0)
    cotangent = gaussian_with(arg_keys[6], (TEXT, D), 1.0, 24.0, ((0, 128),), (0, 1, 128, 5.5))
    return {"queries": queries, "audio_keys": audio_keys, "audio_values": audio_values, "out_weight": out_weight, "mix_gate": mix_gate, "block_mask": block_mask, "cotangent": cotangent}


negative_fill = -1e30


def rounded(values):
    return lax.optimization_barrier(values.astype(jnp.bfloat16)).astype(jnp.float32)


def reference(queries, audio_keys, audio_values, out_weight, mix_gate, block_mask, cotangent):
    score_scale = HD ** -0.5
    gate_value = jnp.tanh(mix_gate[0])
    feature_count = HEADS * HD
    group_width = feature_count // N_TP
    mask_columns = jnp.repeat(block_mask, BLK, axis=1)
    key_heads = audio_keys.astype(jnp.float32).reshape(AUDIO, HEADS, HD)
    value_heads = audio_values.astype(jnp.float32).reshape(AUDIO, HEADS, HD)
    weight_groups = out_weight.astype(jnp.float32).reshape(N_TP, group_width, D)

    def group_step(sums, group_index):
        proj_sum, kv_sum = sums
        first_row = (group_index * TXT_DEV).astype(jnp.int32)
        query_rows = lax.dynamic_slice_in_dim(queries, first_row, TXT_DEV, 0)
        grad_rows = lax.dynamic_slice_in_dim(cotangent, first_row, TXT_DEV, 0)
        mask_rows = lax.dynamic_slice_in_dim(mask_columns, (group_index * (TXT_DEV // BLK)).astype(jnp.int32), TXT_DEV // BLK, 0)
        allowed = (jnp.repeat(mask_rows, BLK, axis=0) > 0)[None, :, :]
        query_heads = query_rows.astype(jnp.float32).reshape(TXT_DEV, HEADS, HD)
        scores = jnp.einsum("thd,ahd->hta", query_heads, key_heads) * score_scale
        row_best = jnp.max(jnp.where(allowed, scores, negative_fill), axis=2)
        weights = jnp.where(allowed, jnp.exp(scores - row_best[:, :, None]), 0.0)
        row_total = jnp.sum(weights, axis=2)
        weighted = jnp.einsum("hta,ahd->htd", rounded(weights), value_heads)
        heads_out = jnp.transpose(weighted / row_total[:, :, None], (1, 0, 2)).reshape(TXT_DEV, feature_count).astype(jnp.bfloat16)
        log_total = row_best + jnp.log(row_total)
        head_groups = heads_out.astype(jnp.float32).reshape(TXT_DEV, N_TP, group_width)
        parts = jnp.einsum("tgk,gkd->gtd", head_groups, weight_groups)
        layer_rows = (gate_value * jnp.sum(rounded(parts), axis=0)).astype(jnp.bfloat16)
        grad_heads = (gate_value * jnp.dot(grad_rows, out_weight.T, preferred_element_type=jnp.float32)).astype(jnp.bfloat16)
        weight_part = gate_value * jnp.dot(heads_out.T, grad_rows, preferred_element_type=jnp.float32)
        probs = jnp.where(allowed, jnp.exp(scores - log_total[:, :, None]), 0.0)
        grad_heads3 = grad_heads.astype(jnp.float32).reshape(TXT_DEV, HEADS, HD)
        out_heads3 = heads_out.astype(jnp.float32).reshape(TXT_DEV, HEADS, HD)
        grad_probs = jnp.einsum("thd,ahd->hta", grad_heads3, value_heads)
        delta_rows = jnp.einsum("thd,thd->ht", grad_heads3, out_heads3)
        grad_scores = rounded(probs * (grad_probs - delta_rows[:, :, None]))
        grad_query = (score_scale * jnp.einsum("hta,ahd->thd", grad_scores, key_heads)).reshape(TXT_DEV, feature_count).astype(jnp.bfloat16)
        key_term = score_scale * jnp.einsum("hta,thd->ahd", grad_scores, query_heads)
        value_term = jnp.einsum("hta,thd->ahd", rounded(probs), grad_heads3)
        kv_term = jnp.concatenate([key_term.reshape(AUDIO, feature_count), value_term.reshape(AUDIO, feature_count)], axis=1)
        return (proj_sum + rounded(weight_part), kv_sum + rounded(kv_term)), (layer_rows, grad_query)

    start_sums = (jnp.zeros((feature_count, D), jnp.float32), jnp.zeros((AUDIO, 2 * feature_count), jnp.float32))
    (proj_sum, kv_sum), (layer_blocks, query_blocks) = lax.scan(group_step, start_sums, jnp.arange(N_SEQ, dtype=jnp.int32))
    layer_out = layer_blocks.reshape(TEXT, D)
    grad_queries = query_blocks.reshape(TEXT, feature_count)
    grad_keys = kv_sum[:, :feature_count].astype(jnp.bfloat16)
    grad_values = kv_sum[:, feature_count:].astype(jnp.bfloat16)
    grad_weight = proj_sum.astype(jnp.bfloat16)
    return (layer_out, grad_queries, grad_keys, grad_values, grad_weight)
```

```python
import jax
import jax.numpy as jnp
from jax import lax
from jax.experimental import pallas as pl
from jax.experimental.pallas import tpu as pltpu
from jax.sharding import PartitionSpec as P

HD = 128
BLK = 128
CH = 8
WC = 1024
HALF = 512
TOK = 512
AUD = 2048
SCALE = HD ** (-0.5)
C2 = SCALE * 1.4426950408889634
NEG = -1e30
BF = jnp.bfloat16
F32 = jnp.float32
MESH = pl.DeviceIdType.MESH

NT = (((1,), (1,)), ((), ()))
NN = (((1,), (0,)), ((), ()))
TN = (((0,), (0,)), ((), ()))

AGY, AGP, AGM, AFP, AFM, SIB, GW, F1, F2, R1, R2, YX = range(12)


def dot(a, b, dims):
    return lax.dot_general(a, b, dims, preferred_element_type=F32)


def kernel(
    q_hbm, k_hbm, v_hbm, w_hbm, gate_ref, mask_ref, cot_hbm,
    layer_ref, dq_ref, dk_ref, dv_ref, gw_ref,
    w, cot, cot_sib, kb, vb, q2, mask2, ht, hrow, gh_acc, gh_own, gh2,
    sc, pb, lse, delta, dq_acc, dq_out, dq_in, f1b, f2b, r1b, r2b, ys, yr, gw_out, gw_in, kv_out, kv_in,
    ss, rs, ks, kr, vs, vr, ds_, dr, es, er, ls,
):
    s = lax.axis_index("seq")
    t = lax.axis_index("tp")
    core = s % 2
    chip = s // 2
    x = t // 2
    yh = t % 2
    xn, xb, xf = (x + 1) % 4, (x + 3) % 4, (x + 2) % 4
    sib = (s + 1 - 2 * core, t)
    nxt = (s, xn * 2 + yh)
    prv = (s, xb * 2 + yh)
    par = (s, x * 2 + 1 - yh)

    def rows(start, size):
        return pl.ds(pl.multiple_of(start, size), size)

    def cols(start, size):
        return pl.ds(pl.multiple_of(start, 128), size)

    def chunk(i):
        return (chip + i) % CH

    def copy(kind, i, src, dst, dev):
        return pltpu.make_async_remote_copy(
            src_ref=src, dst_ref=dst, send_sem=ss.at[kind, i], recv_sem=rs.at[kind, i],
            device_id=dev, device_id_type=MESH,
        )

    def got(kind, i, dst):
        copy(kind, i, dst, dst, nxt).wait_recv()

    def sent(kind, i, src):
        copy(kind, i, src, src, nxt).wait_send()

    barrier = pltpu.get_barrier_semaphore()
    for dev in (nxt, prv, par):
        pl.semaphore_signal(barrier, inc=1, device_id=dev, device_id_type=MESH)

    def greet(j, c):
        pl.semaphore_signal(barrier, inc=1, device_id=((s + j) % 16, t), device_id_type=MESH)
        return c

    lax.fori_loop(1, 16, greet, 0)

    def own_piece(i):
        return pltpu.make_async_copy(
            cot_hbm.at[:, cols(chunk(i) * WC, WC)], cot.at[i, rows(t * 64, 64), :], ls.at[i]
        )

    def start_piece(i, c):
        own_piece(i).start()
        return c

    lax.fori_loop(0, CH, start_piece, 0)
    w_copy = pltpu.make_async_copy(w_hbm, w, ls.at[CH])
    my_heads = cols(core * 256, 256)
    k_copy = pltpu.make_async_copy(k_hbm.at[:, my_heads], kb.at[rows(s * 128, 128), :], ls.at[CH + 1])
    v_copy = pltpu.make_async_copy(v_hbm.at[:, my_heads], vb.at[rows(s * 128, 128), :], ls.at[CH + 2])
    q_copy = pltpu.make_async_copy(q_hbm.at[:, my_heads], q2.at[rows(core * TOK, TOK), :], ls.at[CH + 3])
    m_copy = pltpu.make_async_copy(mask_ref, mask2.at[:, cols(core * TOK, TOK)], ls.at[CH + 4])
    for c in (w_copy, k_copy, v_copy, q_copy, m_copy):
        c.start()

    pl.semaphore_wait(barrier, 18)

    def stage_a(i):
        copy(AGY, i, cot_hbm.at[:, cols(chunk(i) * WC, WC)], cot.at[i, rows(t * 64, 64), :], par).start()

    stage_a(0)
    stage_a(1)

    def extra(n, src, dst):
        return pltpu.make_async_remote_copy(
            src_ref=src, dst_ref=dst, send_sem=es.at[n], recv_sem=er.at[n], device_id=sib, device_id_type=MESH
        )

    other_heads = cols((1 - core) * 256, 256)
    q_send = extra(0, q_hbm.at[:, other_heads], q2.at[rows(core * TOK, TOK), :])
    q_send.start()
    m_send = extra(1, mask_ref, mask2.at[:, cols(core * TOK, TOK)])
    m_send.start()

    def kv_copies(j, dst_rows):
        d = (s + j) % 16
        heads = cols((d % 2) * 256, 256)
        return (
            pltpu.make_async_remote_copy(
                src_ref=k_hbm.at[:, heads], dst_ref=kb.at[dst_rows, :], send_sem=ks.at[j], recv_sem=kr.at[j],
                device_id=(d, t), device_id_type=MESH),
            pltpu.make_async_remote_copy(
                src_ref=v_hbm.at[:, heads], dst_ref=vb.at[dst_rows, :], send_sem=vs.at[j], recv_sem=vr.at[j],
                device_id=(d, t), device_id_type=MESH),
        )

    def kv_start(j, c):
        for copy_ in kv_copies(j, rows(s * 128, 128)):
            copy_.start()
        return c

    lax.fori_loop(1, 16, kv_start, 0)

    gate = jnp.tanh(gate_ref[...])

    def stage_b(i):
        own_piece(i).wait()
        got(AGY, i, cot.at[i, rows((x * 2 + 1 - yh) * 64, 64), :])
        block = cot.at[i, rows(x * 128, 128), :]
        copy(AGP, i, block, block, nxt).start()
        copy(AGM, i, block, block, prv).start()

    def stage_c(i):
        got(AGP, i, cot.at[i, rows(xb * 128, 128), :])
        top = cot.at[i, rows(xb * 128, 64), :]
        copy(AFP, i, top, top, nxt).start()
        got(AGM, i, cot.at[i, rows(xn * 128, 128), :])
        low = cot.at[i, rows(xn * 128 + 64, 64), :]
        copy(AFM, i, low, low, prv).start()

    def stage_d(i):
        got(AFP, i, cot.at[i, rows(xf * 128, 64), :])
        got(AFM, i, cot.at[i, rows(xf * 128 + 64, 64), :])
        copy(SIB, i, cot.at[i, :, cols((1 - core) * HALF, HALF)], cot_sib.at[i], sib).start()

    def stage_e(i):
        cc = cols(chunk(i) * WC, WC)
        for part in range(2):
            rr = pl.ds(part * 256, 256)
            gh_acc[rr, :] += dot(w[rr, cc], cot[i], NT)

    def stage_f(i):
        got(SIB, i, cot_sib.at[i])
        mine = cols(core * TOK, TOK)
        theirs = cols((1 - core) * TOK, TOK)
        for part in range(2):
            rr = pl.ds(part * 256, 256)
            val = dot(ht[rr, mine], cot[i, :, cols(core * HALF, HALF)], NN) + dot(ht[rr, theirs], cot_sib[i], NN)
            gw_out[i, rr, :] = val.astype(BF)

        @pl.when(i > 0)
        def _():
            copy(GW, i, gw_out.at[i], gw_in.at[i - 1], (chunk(i) * 2 + core, t)).start()

    def stage_la(i):
        block = cot.at[i, rows(x * 128, 128), :]
        half = cot.at[i, rows(x * 128, 64), :]
        sent(AGP, i, block)
        sent(AGM, i, block)
        sent(AFP, i, half)
        sent(AFM, i, half)
        sent(SIB, i, cot_sib.at[i])
        for part in range(2):
            cc = cols(chunk(i) * WC + part * HALF, HALF)
            cot[i, :, pl.ds(part * HALF, HALF)] = dot(hrow[...], w[:, cc], NN).astype(BF)
        copy(F1, i, cot.at[i, rows(xf * 128, 64), :], f1b.at[i], nxt).start()
        copy(F2, i, cot.at[i, rows(xf * 128 + 64, 64), :], f2b.at[i], prv).start()

    def stage_lb(i):
        got(F1, i, f1b.at[i])
        rr = rows(xn * 128, 64)
        cot[i, rr, :] = (cot[i, rr, :].astype(F32) + f1b[i].astype(F32)).astype(BF)
        copy(R1, i, cot.at[i, rows(xn * 128, 128), :], r1b.at[i], nxt).start()
        got(F2, i, f2b.at[i])
        rr = rows(xb * 128 + 64, 64)
        cot[i, rr, :] = (cot[i, rr, :].astype(F32) + f2b[i].astype(F32)).astype(BF)
        copy(R2, i, cot.at[i, rows(xb * 128, 128), :], r2b.at[i], prv).start()

    def reduced(i, which):
        rr = rows(which * 64, 64)
        return (
            cot[i, rows(x * 128 + which * 64, 64), :].astype(F32)
            + r1b[i, rr, :].astype(F32)
            + r2b[i, rr, :].astype(F32)
        )

    def stage_lc(i):
        got(R1, i, r1b.at[i])
        got(R2, i, r2b.at[i])
        ys[i] = reduced(i, 1 - yh).astype(BF)
        copy(YX, i, ys.at[i], yr.at[i], par).start()

    def stage_ld(i):
        got(YX, i, yr.at[i])
        total = reduced(i, yh) + yr[i].astype(F32)
        layer_ref[:, cols(chunk(i) * WC, WC)] = (gate * total).astype(BF)

    def masked(score, row, tok):
        return jnp.where(mask2[pl.ds(row, 1), tok] > 0, score, NEG)

    def forward(j):
        hh, u = j // 2, j % 2
        hc = cols(hh * HD, HD)
        tok = cols(u * TOK, TOK)
        qv = q2[rows(u * TOK, TOK), hc]

        def scores(ab, best):
            part = dot(kb[rows(ab * 256, 256), hc], qv, NT)
            for b in range(2):
                val = masked(part[b * 128 : (b + 1) * 128], ab * 2 + b, tok)
                sc[rows(ab * 256 + b * 128, 128), :] = val
                best = jnp.maximum(best, jnp.max(val, axis=0, keepdims=True))
            return best

        best = lax.fori_loop(0, AUD // 256, scores, jnp.full((1, TOK), NEG, F32))

        def weigh(ab, total):
            rr = rows(ab * 256, 256)
            val = jnp.exp2((sc[rr, :] - best) * C2)
            pb[rr, :] = val.astype(BF)
            return total + jnp.sum(val, axis=0, keepdims=True)

        total = lax.fori_loop(0, AUD // 256, weigh, jnp.zeros((1, TOK), F32))
        out = dot(vb[:, hc], pb[...], TN)
        ht[rows(core * 256 + hh * HD, HD), tok] = (out / total).astype(BF)
        lse[hh, :, tok] = best * C2 + jnp.log2(total)

    def kv_send(hh, d):
        return pltpu.make_async_remote_copy(
            src_ref=kv_out.at[hh, rows(d * 128, 128), :], dst_ref=kv_in.at[hh, (d - s + 16) % 16],
            send_sem=ds_.at[hh, (d - s + 16) % 16], recv_sem=dr.at[hh, (d - s + 16) % 16],
            device_id=(d, t), device_id_type=MESH,
        )

    def backward(j):
        hh = j // 2
        ah = (j + chip // 4) % 2
        hc = cols(hh * HD, HD)
        hr = rows(hh * HD, HD)
        first = j % 2 == 0

        @pl.when(first)
        def _():
            dq_acc[...] = jnp.zeros_like(dq_acc)
            own = ht[rows(core * 256 + hh * HD, HD), :].astype(F32)
            delta[...] = jnp.sum(gh2[hr, :].astype(F32) * own, axis=0, keepdims=True)

        def step(b, c):
            rr = rows(ah * 1024 + b * 256, 256)
            kk = kb[rr, hc]
            vv = vb[rr, hc]
            qv = q2[:, hc]
            gv = gh2[hr, :]
            score = dot(kk, qv, NT)
            logs = lse[hh]
            probs = []
            for m in range(2):
                row = ah * 8 + b * 2 + m
                val = masked(score[m * 128 : (m + 1) * 128], row, slice(None))
                probs.append(jnp.exp2(val * C2 - logs))
            prob = jnp.concatenate(probs, axis=0)
            dp = dot(vv, gv, NN)
            dsc = (prob * (dp - delta[...])).astype(BF)
            kv_out[hh, rr, pl.ds(HD, HD)] = dot(prob.astype(BF), gv, NT).astype(BF)
            kv_out[hh, rr, pl.ds(0, HD)] = (SCALE * dot(dsc, qv, NN)).astype(BF)
            dq_acc[...] += dot(kk, dsc, TN)
            return c

        lax.fori_loop(0, 4, step, 0)

        def send(d, c):
            @pl.when(ah * 8 + d != s)
            def _():
                kv_send(hh, ah * 8 + d).start()

            return c

        lax.fori_loop(0, 8, send, 0)

        @pl.when(j % 2 == 1)
        def _():
            full = SCALE * dq_acc[...]
            for u in range(2):
                piece = full[:, u * TOK : (u + 1) * TOK].T.astype(BF)

                @pl.when(core == u)
                def _():
                    dq_ref[:, cols(core * 256 + hh * HD, HD)] = piece

                @pl.when(core != u)
                def _():
                    dq_out[:, hc] = piece

    mine_rows = rows(core * 256, 256)
    ht_send = extra(2, ht.at[mine_rows, :], ht.at[mine_rows, :])
    their_rows = rows((1 - core) * 256, 256)
    gh_send = extra(3, gh_own.at[their_rows, :], gh2.at[:, cols(core * TOK, TOK)])
    dq_send = extra(4, dq_out, dq_in)

    gh_acc[...] = jnp.zeros_like(gh_acc)
    w_copy.wait()

    def f_low(g):
        return jnp.minimum(2 * (g - 5), g - 2)

    def tick(g, c):
        def stage(low, n, fn, idx):
            @pl.when((g >= low) & (g < low + n))
            def _():
                fn(idx)

        stage(0, CH - 2, stage_a, g + 2)
        stage(0, CH, stage_b, g)
        stage(1, CH, stage_c, g - 1)
        stage(2, CH, stage_d, g - 2)
        stage(6, CH, stage_lb, g - 6)
        stage(7, CH, stage_lc, g - 7)
        stage(8, CH, stage_ld, g - 8)
        stage(2, CH, stage_e, g - 2)

        @pl.when(g == 3)
        def _():
            k_copy.wait()
            v_copy.wait()
            q_copy.wait()
            m_copy.wait()
            extra(0, q2.at[rows((1 - core) * TOK, TOK), :], q2.at[rows((1 - core) * TOK, TOK), :]).wait_recv()
            other = mask2.at[:, cols((1 - core) * TOK, TOK)]
            extra(1, other, other).wait_recv()

            def kv_got(j, c2):
                for copy_ in kv_copies(j, rows(((s - j + 16) % 16) * 128, 128)):
                    copy_.wait_recv()
                return c2

            lax.fori_loop(1, 16, kv_got, 0)

        @pl.when((g >= 3) & (g < 5))
        def _():
            def unit(j, c2):
                forward((g - 3) * 2 + j)
                return c2

            lax.fori_loop(0, 2, unit, 0)

        @pl.when(g == 4)
        def _():
            ht_send.start()

        @pl.when(g == 5)
        def _():
            extra(2, ht.at[their_rows, :], ht.at[their_rows, :]).wait_recv()
            hrow[...] = ht[:, cols(core * TOK, TOK)].astype(F32).T.astype(BF)

        @pl.when((g >= 5) & (g < 10))
        def _():
            def unit(i, c2):
                stage_f(i)
                return c2

            lax.fori_loop(f_low(g), f_low(g + 1), unit, 0)

        stage(5, CH, stage_la, g - 5)

        @pl.when(g == 9)
        def _():
            gh_own[...] = (gate * gh_acc[...]).astype(BF)
            gh2[:, cols(core * TOK, TOK)] = gh_own[mine_rows, :]
            gh_send.start()

        @pl.when(g == 10)
        def _():
            other = gh2.at[:, cols((1 - core) * TOK, TOK)]
            extra(3, other, other).wait_recv()

        stage(10, 4, backward, g - 10)

        @pl.when(g == 13)
        def _():
            dq_send.start()

        return c

    lax.fori_loop(0, 16, tick, 0)

    def gw_got(i, c):
        got(GW, i, gw_in.at[i - 1])
        return c

    lax.fori_loop(1, CH, gw_got, 0)

    def gw_sum(b, c):
        rr = rows(b * 64, 64)
        total = gw_out[0, rr, :].astype(F32)
        for i in range(CH - 1):
            total += gw_in[i, rr, :].astype(F32)
        gw_ref[rr, :] = (gate * total).astype(BF)
        return c

    lax.fori_loop(0, 8, gw_sum, 0)

    dq_send.wait_recv()
    dq_ref[:, cols((1 - core) * 256, 256)] = dq_in[...]

    def kv_got2(j, c):
        for hh in range(2):
            slot = kv_in.at[hh, j]
            pltpu.make_async_remote_copy(
                src_ref=slot, dst_ref=slot, send_sem=ds_.at[hh, j], recv_sem=dr.at[hh, j],
                device_id=sib, device_id_type=MESH,
            ).wait_recv()
        return c

    lax.fori_loop(1, 16, kv_got2, 0)
    for hh in range(2):
        same = kv_out[hh, rows(s * 128, 128), :].astype(F32)
        for j in range(2, 16, 2):
            same += kv_in[hh, j].astype(F32)
        other = kv_in[hh, 1].astype(F32)
        for j in range(3, 16, 2):
            other += kv_in[hh, j].astype(F32)
        hc = cols(core * 256 + hh * HD, HD)
        dk_ref[:, hc] = same[:, :HD].astype(BF)
        dv_ref[:, hc] = same[:, HD:].astype(BF)
        hc = cols((1 - core) * 256 + hh * HD, HD)
        dk_ref[:, hc] = other[:, :HD].astype(BF)
        dv_ref[:, hc] = other[:, HD:].astype(BF)

    def all_sent(i, c):
        sent(AGY, i, cot.at[i, rows(x * 128, 64), :])
        sent(F1, i, f1b.at[i])
        sent(F2, i, f2b.at[i])
        sent(R1, i, r1b.at[i])
        sent(R2, i, r2b.at[i])
        sent(YX, i, ys.at[i])

        @pl.when(i > 0)
        def _():
            sent(GW, i, gw_out.at[i])

        return c

    lax.fori_loop(0, CH, all_sent, 0)

    def kv_sent(j, c):
        for copy_ in kv_copies(j, rows(s * 128, 128)):
            copy_.wait_send()
        for hh in range(2):
            slot = kv_in.at[hh, j]
            pltpu.make_async_remote_copy(
                src_ref=slot, dst_ref=slot, send_sem=ds_.at[hh, j], recv_sem=dr.at[hh, j],
                device_id=sib, device_id_type=MESH,
            ).wait_send()
        return c

    lax.fori_loop(1, 16, kv_sent, 0)
    for c in (q_send, m_send, ht_send, gh_send, dq_send):
        c.wait_send()


def per_device(queries, audio_keys, audio_values, out_weight, mix_gate, block_mask, cotangent):
    mask_rows = jnp.repeat(block_mask.T.astype(F32), BLK, axis=1)
    hbm = pl.BlockSpec(memory_space=pl.ANY)
    vmem = pl.BlockSpec(memory_space=pltpu.VMEM)
    dma = pltpu.SemaphoreType.DMA
    return pl.pallas_call(
        kernel,
        out_shape=(
            jax.ShapeDtypeStruct((64, 8192), BF),
            jax.ShapeDtypeStruct((TOK, 512), BF),
            jax.ShapeDtypeStruct((128, 512), BF),
            jax.ShapeDtypeStruct((128, 512), BF),
            jax.ShapeDtypeStruct((512, 512), BF),
        ),
        in_specs=[hbm, hbm, hbm, hbm, vmem, vmem, hbm],
        out_specs=[vmem] * 5,
        scratch_shapes=[
            pltpu.VMEM((512, 8192), BF),
            pltpu.VMEM((CH, TOK, WC), BF),
            pltpu.VMEM((CH, TOK, HALF), BF),
            pltpu.VMEM((AUD, 256), BF),
            pltpu.VMEM((AUD, 256), BF),
            pltpu.VMEM((2 * TOK, 256), BF),
            pltpu.VMEM((16, 2 * TOK), F32),
            pltpu.VMEM((512, 2 * TOK), BF),
            pltpu.VMEM((TOK, 512), BF),
            pltpu.VMEM((512, TOK), F32),
            pltpu.VMEM((512, TOK), BF),
            pltpu.VMEM((256, 2 * TOK), BF),
            pltpu.VMEM((AUD, TOK), F32),
            pltpu.VMEM((AUD, TOK), BF),
            pltpu.VMEM((2, 1, 2 * TOK), F32),
            pltpu.VMEM((1, 2 * TOK), F32),
            pltpu.VMEM((HD, 2 * TOK), F32),
            pltpu.VMEM((TOK, 256), BF),
            pltpu.VMEM((TOK, 256), BF),
            pltpu.VMEM((CH, 64, WC), BF),
            pltpu.VMEM((CH, 64, WC), BF),
            pltpu.VMEM((CH, 128, WC), BF),
            pltpu.VMEM((CH, 128, WC), BF),
            pltpu.VMEM((CH, 64, WC), BF),
            pltpu.VMEM((CH, 64, WC), BF),
            pltpu.VMEM((CH, 512, HALF), BF),
            pltpu.VMEM((CH - 1, 512, HALF), BF),
            pltpu.VMEM((2, AUD, 256), BF),
            pltpu.VMEM((2, 16, 128, 256), BF),
            dma((12, CH)), dma((12, CH)),
            dma((16,)), dma((16,)), dma((16,)), dma((16,)),
            dma((2, 16)), dma((2, 16)),
            dma((5,)), dma((5,)),
            dma((CH + 5,)),
        ],
        compiler_params=pltpu.CompilerParams(
            collective_id=0, has_side_effects=True, vmem_limit_bytes=62 * 2**20
        ),
        cost_estimate=pl.CostEstimate(flops=20 * 10**9, bytes_accessed=16 * 2**20, transcendentals=8 * 2**20),
    )(queries, audio_keys, audio_values, out_weight, mix_gate.reshape(1, 1), mask_rows, cotangent)


def solution(mesh):
    in_specs = (
        P("seq", "tp"),
        P("seq", "tp"),
        P("seq", "tp"),
        P("tp", None),
        P(),
        P("seq", None),
        P(("seq", "tp"), None),
    )
    out_specs = (
        P(("seq", "tp"), None),
        P("seq", "tp"),
        P("seq", "tp"),
        P("seq", "tp"),
        P("tp", "seq"),
    )
    return jax.shard_map(
        per_device, mesh=mesh, in_specs=in_specs, out_specs=out_specs, check_vma=False
    )
```

```python
import jax
import jax.numpy as jnp
from jax import lax
from jax.experimental import pallas as pl
from jax.experimental.pallas import tpu as pltpu
from jax.sharding import PartitionSpec as P

HD = 128
BLK = 128
CH = 8
WC = 1024
HALF = 512
TOK = 512
AUD = 2048
SCALE = HD ** (-0.5)
C2 = SCALE * 1.4426950408889634
NEG = -1e30
BF = jnp.bfloat16
F32 = jnp.float32
MESH = pl.DeviceIdType.MESH

NT = (((1,), (1,)), ((), ()))
NN = (((1,), (0,)), ((), ()))
TN = (((0,), (0,)), ((), ()))

AGY, AGP, AGM, AFP, AFM, SIB, GW, F1, F2, R1, R2, YX, YP, YM, YF, P0 = range(16)
KINDS = P0 + 4
GATHER_X = (0, 3, 5)
SCATTER_Y = (2, 4, 6)


def dot(a, b, dims):
    return lax.dot_general(a, b, dims, preferred_element_type=F32)


def kernel(
    q_hbm, k_hbm, v_hbm, w_hbm, gate_ref, mask_ref, cot_hbm,
    layer_ref, dq_ref, dk_ref, dv_ref, gw_ref,
    w, cot, cot_sib, kvb, q2, mask2, ht, hrow, gh_acc, gh_own, gh2,
    sc, pb, lse, delta, dq_acc, dq_out, dq_in, f1b, f2b, r1b, r2b, ys, yr, p4b, gw_out, gw_in, gw_sum, gw_par, kv_out, kv_in, kv_red, kv_fin,
    ss, rs, ps, pr, zs, zr, ds_, dr, fs, fr, es, er, ls,
):
    s = lax.axis_index("seq")
    t = lax.axis_index("tp")
    core = s % 2
    z = s // 4
    yl = (s // 2) % 2
    x = t // 2
    yh = t % 2
    xn, xb, xf = (x + 1) % 4, (x + 3) % 4, (x + 2) % 4
    sib = (s + 1 - 2 * core, t)
    nxt = (s, xn * 2 + yh)
    prv = (s, xb * 2 + yh)
    par = (s, x * 2 + 1 - yh)

    def zdev(dz):
        return (((z + dz) % 4) * 4 + yl * 2 + core, t)

    def near(n):
        return (z * 4 + ((yl + n // 2) % 2) * 2 + (core + n) % 2, t)

    def rows(start, size):
        return pl.ds(pl.multiple_of(start, size), size)

    def cols(start, size):
        return pl.ds(pl.multiple_of(start, 128), size)

    def chunk(i):
        m = i // 2
        zz = ((z // 2 + m // 2) % 2) * 2 + (z + m) % 2
        return zz * 2 + (yl + i) % 2

    def copy(kind, i, src, dst, dev):
        return pltpu.make_async_remote_copy(
            src_ref=src, dst_ref=dst, send_sem=ss.at[kind, i], recv_sem=rs.at[kind, i],
            device_id=dev, device_id_type=MESH,
        )

    def got(kind, i, dst):
        copy(kind, i, dst, dst, nxt).wait_recv()

    def sent(kind, i, src):
        copy(kind, i, src, src, nxt).wait_send()

    barrier = pltpu.get_barrier_semaphore()
    for dev in (nxt, prv, par):
        pl.semaphore_signal(barrier, inc=1, device_id=dev, device_id_type=MESH)

    for n in range(1, 4):
        pl.semaphore_signal(barrier, inc=1, device_id=near(n), device_id_type=MESH)
        pl.semaphore_signal(barrier, inc=1, device_id=zdev(n), device_id_type=MESH)

    def own_piece(i):
        return pltpu.make_async_copy(
            cot_hbm.at[:, cols(chunk(i) * WC, WC)], cot.at[i, rows(t * 64, 64), :], ls.at[i]
        )

    def start_piece(i, c):
        own_piece(i).start()
        return c

    lax.fori_loop(0, CH, start_piece, 0)
    w_copy = pltpu.make_async_copy(w_hbm, w, ls.at[CH])
    my_heads = cols(core * 256, 256)
    k_copy = pltpu.make_async_copy(k_hbm.at[:, my_heads], kvb.at[rows(s * 128, 128), pl.ds(0, 256)], ls.at[CH + 1])
    v_copy = pltpu.make_async_copy(v_hbm.at[:, my_heads], kvb.at[rows(s * 128, 128), pl.ds(256, 256)], ls.at[CH + 2])
    q_copy = pltpu.make_async_copy(q_hbm.at[:, my_heads], q2.at[rows(core * TOK, TOK), :], ls.at[CH + 3])
    m_copy = pltpu.make_async_copy(mask_ref, mask2.at[:, cols(core * TOK, TOK)], ls.at[CH + 4])
    for c in (w_copy, k_copy, v_copy, q_copy, m_copy):
        c.start()

    pl.semaphore_wait(barrier, 9)

    def stage_a(i):
        copy(AGY, i, cot_hbm.at[:, cols(chunk(i) * WC, WC)], cot.at[i, rows(t * 64, 64), :], par).start()

    def piece_x(i):
        src = cot_hbm.at[:, cols(chunk(i) * WC, WC)]
        dst = cot.at[i, rows(t * 64, 64), :]
        copy(AGP, i, src, dst, nxt).start()
        copy(AGM, i, src, dst, prv).start()

    piece_x(0)
    stage_a(1)

    def extra(n, src, dst):
        return pltpu.make_async_remote_copy(
            src_ref=src, dst_ref=dst, send_sem=es.at[n], recv_sem=er.at[n], device_id=sib, device_id_type=MESH
        )

    other_heads = cols((1 - core) * 256, 256)
    q_send = extra(0, q_hbm.at[:, other_heads], q2.at[rows(core * TOK, TOK), :])
    q_send.start()
    m_send = extra(1, mask_ref, mask2.at[:, cols(core * TOK, TOK)])
    m_send.start()

    def kv_near(n, src_rows):
        heads = cols(((core + n) % 2) * 256, 256)
        return [
            pltpu.make_async_remote_copy(
                src_ref=src.at[:, heads], dst_ref=kvb.at[src_rows, pl.ds(part * 256, 256)],
                send_sem=ps.at[n, part], recv_sem=pr.at[n, part], device_id=near(n), device_id_type=MESH)
            for part, src in enumerate((k_hbm, v_hbm))
        ]

    def kv_far(dz, zz):
        block = kvb.at[rows(zz * 512, 512), :]
        return pltpu.make_async_remote_copy(
            src_ref=block, dst_ref=block, send_sem=zs.at[dz], recv_sem=zr.at[dz],
            device_id=zdev(dz), device_id_type=MESH)

    for n in range(1, 4):
        for copy_ in kv_near(n, rows(s * 128, 128)):
            copy_.start()
    stage_a(2)
    stage_a(0)

    def kv_spread():
        k_copy.wait()
        v_copy.wait()
        for n in range(1, 4):
            src = z * 4 + ((yl + n // 2) % 2) * 2 + (core + n) % 2
            for copy_ in kv_near(n, rows(src * 128, 128)):
                copy_.wait_recv()
        for dz in (1, 3, 2):
            kv_far(dz, z).start()

    gate = jnp.tanh(gate_ref[...])

    def stage_b1(i):
        own_piece(i).wait()
        got(AGY, i, cot.at[i, rows((x * 2 + 1 - yh) * 64, 64), :])
        block = cot.at[i, rows(x * 128, 128), :]
        copy(AGP, i, block, block, nxt).start()
        copy(AGM, i, block, block, prv).start()

    def stage_c1(i):
        got(AGP, i, cot.at[i, rows(xb * 128, 128), :])
        top = cot.at[i, rows(xb * 128, 64), :]
        copy(AFP, i, top, top, nxt).start()
        got(AGM, i, cot.at[i, rows(xn * 128, 128), :])
        low = cot.at[i, rows(xn * 128 + 64, 64), :]
        copy(AFM, i, low, low, prv).start()

    def stage_d1(i):
        got(AFP, i, cot.at[i, rows(xf * 128, 64), :])
        got(AFM, i, cot.at[i, rows(xf * 128 + 64, 64), :])
        share(i)

    def share(i):
        copy(SIB, i, cot.at[i, :, cols((1 - core) * HALF, HALF)], cot_sib.at[i], sib).start()

    def to_partner(kind, i, xx):
        block = cot.at[i, rows(xx * 128 + yh * 64, 64), :]
        copy(kind, i, block, block, par).start()

    def stage_c2(i):
        got(AGP, i, cot.at[i, rows(xb * 128 + yh * 64, 64), :])
        top = cot.at[i, rows(xb * 128 + yh * 64, 32), :]
        copy(AFP, i, top, top, nxt).start()
        got(AGM, i, cot.at[i, rows(xn * 128 + yh * 64, 64), :])
        low = cot.at[i, rows(xn * 128 + yh * 64 + 32, 32), :]
        copy(AFM, i, low, low, prv).start()
        to_partner(YP, i, xb)
        to_partner(YM, i, xn)

    def stage_d2(i):
        got(AFP, i, cot.at[i, rows(xf * 128 + yh * 64, 32), :])
        got(AFM, i, cot.at[i, rows(xf * 128 + yh * 64 + 32, 32), :])
        to_partner(YF, i, xf)

    def stage_x2(i):
        own_piece(i).wait()
        for kind, xx in ((AGY, x), (YP, xb), (YM, xn), (YF, xf)):
            got(kind, i, cot.at[i, rows(xx * 128 + (1 - yh) * 64, 64), :])
        share(i)

    def either(first, second, cond):
        def stage(i):
            @pl.when(cond(i))
            def _():
                first(i)

            @pl.when(jnp.logical_not(cond(i)))
            def _():
                second(i)

        return stage

    def member(i, chosen):
        hit = i < 0
        for n in chosen:
            hit = jnp.logical_or(hit, i == n)
        return hit

    def gathers_x(i):
        return member(i, GATHER_X)

    stage_b = either(piece_x, stage_b1, gathers_x)
    stage_c = either(stage_c2, stage_c1, gathers_x)
    stage_d = either(stage_d2, stage_d1, gathers_x)

    def gather_sent(i):
        @pl.when(gathers_x(i))
        def _():
            for kind in (AGP, AGM, YP, YM, YF):
                sent(kind, i, cot.at[i, rows(x * 128, 64), :])
            for kind in (AFP, AFM):
                sent(kind, i, cot.at[i, rows(x * 128, 32), :])

        @pl.when(jnp.logical_not(gathers_x(i)))
        def _():
            for kind in (AGP, AGM):
                sent(kind, i, cot.at[i, rows(x * 128, 128), :])
            for kind in (AFP, AFM):
                sent(kind, i, cot.at[i, rows(x * 128, 64), :])

    def stage_e(i):
        cc = cols(chunk(i) * WC, WC)
        for part in range(2):
            rr = pl.ds(part * 256, 256)
            gh_acc[rr, :] += dot(w[rr, cc], cot[i], NT)

    def stage_f(i):
        got(SIB, i, cot_sib.at[i])
        mine = cols(core * TOK, TOK)
        theirs = cols((1 - core) * TOK, TOK)
        for part in range(2):
            rr = pl.ds(part * 256, 256)
            val = dot(ht[rr, mine], cot[i, :, cols(core * HALF, HALF)], NN) + dot(ht[rr, theirs], cot_sib[i], NN)
            gw_out[i, rr, :] = val.astype(BF)

        @pl.when(i > 1)
        def _():
            zz = chunk(i) // 2
            copy(GW, i, gw_out.at[i], gw_in.at[i - 2], (zz * 4 + yl * 2 + core, t)).start()

    def product(i):
        gather_sent(i)
        sent(SIB, i, cot_sib.at[i])
        for part in range(2):
            cc = cols(chunk(i) * WC + part * HALF, HALF)
            cot[i, :, pl.ds(part * HALF, HALF)] = dot(hrow[...], w[:, cc], NN).astype(BF)

    def stage_la1(i):
        product(i)
        copy(F1, i, cot.at[i, rows(xf * 128, 64), :], f1b.at[i], nxt).start()
        copy(F2, i, cot.at[i, rows(xf * 128 + 64, 64), :], f2b.at[i], prv).start()

    def stage_lb1(i):
        got(F1, i, f1b.at[i])
        rr = rows(xn * 128, 64)
        cot[i, rr, :] = (cot[i, rr, :].astype(F32) + f1b[i].astype(F32)).astype(BF)
        copy(R1, i, cot.at[i, rows(xn * 128, 128), :], r1b.at[i], nxt).start()
        got(F2, i, f2b.at[i])
        rr = rows(xb * 128 + 64, 64)
        cot[i, rr, :] = (cot[i, rr, :].astype(F32) + f2b[i].astype(F32)).astype(BF)
        copy(R2, i, cot.at[i, rows(xb * 128, 128), :], r2b.at[i], prv).start()

    def reduced(i, which):
        rr = rows(which * 64, 64)
        return (
            cot[i, rows(x * 128 + which * 64, 64), :].astype(F32)
            + r1b[i, rr, :].astype(F32)
            + r2b[i, rr, :].astype(F32)
        )

    def stage_lc1(i):
        got(R1, i, r1b.at[i])
        got(R2, i, r2b.at[i])
        ys[i] = reduced(i, 1 - yh).astype(BF)
        copy(YX, i, ys.at[i], yr.at[i], par).start()

    def stage_ld1(i):
        got(YX, i, yr.at[i])
        total = reduced(i, yh) + yr[i].astype(F32)
        layer_ref[:, cols(chunk(i) * WC, WC)] = (gate * total).astype(BF)

    def slot(i):
        return i // 2 - 1

    def stage_la2(i):
        product(i)
        for n in range(4):
            copy(P0 + n, i, cot.at[i, rows(n * 128 + (1 - yh) * 64, 64), :], p4b.at[slot(i), n], par).start()

    def add_partner(i, xx):
        rr = rows(xx * 128 + yh * 64, 64)
        return cot[i, rr, :].astype(F32) + p4b[slot(i), xx].astype(F32)

    def stage_lb2(i):
        for n in range(4):
            got(P0 + n, i, p4b.at[slot(i), n])
        rr = rows(xf * 128 + yh * 64, 64)
        cot[i, rr, :] = add_partner(i, xf).astype(BF)
        copy(F1, i, cot.at[i, rows(xf * 128 + yh * 64, 32), :], f1b.at[i, pl.ds(0, 32), :], nxt).start()
        copy(F2, i, cot.at[i, rows(xf * 128 + yh * 64 + 32, 32), :], f2b.at[i, pl.ds(0, 32), :], prv).start()

    def stage_lc2(i):
        top, low = pl.ds(0, 32), pl.ds(0, 64)
        got(F1, i, f1b.at[i, top, :])
        val = add_partner(i, xn)
        cot[i, rows(xn * 128 + yh * 64, 32), :] = (val[:32] + f1b[i, top, :].astype(F32)).astype(BF)
        cot[i, rows(xn * 128 + yh * 64 + 32, 32), :] = val[32:].astype(BF)
        copy(R1, i, cot.at[i, rows(xn * 128 + yh * 64, 64), :], r1b.at[i, low, :], nxt).start()
        got(F2, i, f2b.at[i, top, :])
        val = add_partner(i, xb)
        cot[i, rows(xb * 128 + yh * 64, 32), :] = val[:32].astype(BF)
        cot[i, rows(xb * 128 + yh * 64 + 32, 32), :] = (val[32:] + f2b[i, top, :].astype(F32)).astype(BF)
        copy(R2, i, cot.at[i, rows(xb * 128 + yh * 64, 64), :], r2b.at[i, low, :], prv).start()

    def stage_ld2(i):
        low = pl.ds(0, 64)
        got(R1, i, r1b.at[i, low, :])
        got(R2, i, r2b.at[i, low, :])
        total = add_partner(i, x) + r1b[i, low, :].astype(F32) + r2b[i, low, :].astype(F32)
        layer_ref[:, cols(chunk(i) * WC, WC)] = (gate * total).astype(BF)

    def scatters_y(i):
        return member(i, SCATTER_Y)

    stage_la = either(stage_la2, stage_la1, scatters_y)
    stage_lb = either(stage_lb2, stage_lb1, scatters_y)
    stage_lc = either(stage_lc2, stage_lc1, scatters_y)
    stage_ld = either(stage_ld2, stage_ld1, scatters_y)

    def masked(score, row, tok):
        return jnp.where(mask2[pl.ds(row, 1), tok] > 0, score, NEG)

    def forward(j):
        hh, u = j // 2, j % 2
        hc = cols(hh * HD, HD)
        vc = cols(256 + hh * HD, HD)
        tok = cols(u * TOK, TOK)
        qv = q2[rows(u * TOK, TOK), hc]

        def scores(ab, best):
            part = dot(kvb[rows(ab * 256, 256), hc], qv, NT)
            for b in range(2):
                val = masked(part[b * 128 : (b + 1) * 128], ab * 2 + b, tok)
                sc[rows(ab * 256 + b * 128, 128), :] = val
                best = jnp.maximum(best, jnp.max(val, axis=0, keepdims=True))
            return best

        best = lax.fori_loop(0, AUD // 256, scores, jnp.full((1, TOK), NEG, F32))

        def weigh(ab, total):
            rr = rows(ab * 256, 256)
            val = jnp.exp2((sc[rr, :] - best) * C2)
            pb[rr, :] = val.astype(BF)
            return total + jnp.sum(val, axis=0, keepdims=True)

        total = lax.fori_loop(0, AUD // 256, weigh, jnp.zeros((1, TOK), F32))
        out = dot(kvb[:, vc], pb[...], TN)
        ht[rows(core * 256 + hh * HD, HD), tok] = (out / total).astype(BF)
        lse[hh, :, tok] = best * C2 + jnp.log2(total)

    def kv_z(hh, dz):
        return pltpu.make_async_remote_copy(
            src_ref=kv_out.at[hh, rows(((z + dz) % 4) * 512, 512), :], dst_ref=kv_in.at[hh, dz - 1],
            send_sem=ds_.at[hh, dz], recv_sem=dr.at[hh, dz], device_id=zdev(dz), device_id_type=MESH)

    def kv_y(hh, n):
        src = ((yl + n // 2) % 2) * 2 + (core + n) % 2
        return pltpu.make_async_remote_copy(
            src_ref=kv_red.at[hh, src], dst_ref=kv_fin.at[hh, n],
            send_sem=fs.at[hh, n], recv_sem=fr.at[hh, n], device_id=near(n), device_id_type=MESH)

    def kv_reduce(hh):
        for dz in range(1, 4):
            kv_z(hh, dz).wait_recv()
        for b in range(4):
            total = kv_out[hh, rows(z * 512 + b * 128, 128), :].astype(F32)
            for dz in range(3):
                total += kv_in[hh, dz, b * 128 : (b + 1) * 128, :].astype(F32)
            kv_red[hh, b] = total.astype(BF)
        for n in range(1, 4):
            kv_y(hh, n).start()

    def kv_finish(hh):
        for n in range(1, 4):
            kv_y(hh, n).wait_recv()
        same = kv_red[hh, yl * 2 + core].astype(F32) + kv_fin[hh, 2].astype(F32)
        other = kv_fin[hh, 1].astype(F32) + kv_fin[hh, 3].astype(F32)
        hc = cols(core * 256 + hh * HD, HD)
        dk_ref[:, hc] = same[:, :HD].astype(BF)
        dv_ref[:, hc] = same[:, HD:].astype(BF)
        hc = cols((1 - core) * 256 + hh * HD, HD)
        dk_ref[:, hc] = other[:, :HD].astype(BF)
        dv_ref[:, hc] = other[:, HD:].astype(BF)

    gw_send = pltpu.make_async_remote_copy(
        src_ref=gw_sum, dst_ref=gw_par, send_sem=fs.at[0, 0], recv_sem=fr.at[0, 0],
        device_id=near(2), device_id_type=MESH)

    def gw_reduce(which, write):
        def got_one(i, c):
            got(GW, 2 * i + which, gw_in.at[2 * i + which - 2])
            return c

        lax.fori_loop(1, 4, got_one, 0)

        def add(b, c):
            rr = rows(b * 64, 64)
            total = gw_out[which, rr, :].astype(F32)
            for i in range(3):
                total += gw_in[2 * i + which, rr, :].astype(F32)
            write(rr, total)
            return c

        lax.fori_loop(0, 8, add, 0)

    def gw_part():
        def write(rr, total):
            gw_sum[rr, :] = total.astype(BF)

        gw_reduce(1, write)
        gw_send.start()

    def gw_finish():
        gw_send.wait_recv()

        def write(rr, total):
            gw_ref[rr, :] = (gate * (total + gw_par[rr, :].astype(F32))).astype(BF)

        gw_reduce(0, write)

    def backward(j):
        hh = j // 2
        ah = (j + 1 + z // 2) % 2
        hc = cols(hh * HD, HD)
        hr = rows(hh * HD, HD)
        first = j % 2 == 0

        @pl.when(first)
        def _():
            dq_acc[...] = jnp.zeros_like(dq_acc)
            own = ht[rows(core * 256 + hh * HD, HD), :].astype(F32)
            delta[...] = jnp.sum(gh2[hr, :].astype(F32) * own, axis=0, keepdims=True)

        def step(b, c):
            rr = rows(ah * 1024 + b * 256, 256)
            kk = kvb[rr, hc]
            vv = kvb[rr, cols(256 + hh * HD, HD)]
            qv = q2[:, hc]
            gv = gh2[hr, :]
            score = dot(kk, qv, NT)
            logs = lse[hh]
            probs = []
            for m in range(2):
                row = ah * 8 + b * 2 + m
                val = masked(score[m * 128 : (m + 1) * 128], row, slice(None))
                probs.append(jnp.exp2(val * C2 - logs))
            prob = jnp.concatenate(probs, axis=0)
            dp = dot(vv, gv, NN)
            dsc = (prob * (dp - delta[...])).astype(BF)
            kv_out[hh, rr, pl.ds(HD, HD)] = dot(prob.astype(BF), gv, NT).astype(BF)
            kv_out[hh, rr, pl.ds(0, HD)] = (SCALE * dot(dsc, qv, NN)).astype(BF)
            dq_acc[...] += dot(kk, dsc, TN)
            return c

        lax.fori_loop(0, 4, step, 0)

        for b in range(2):
            dz = (ah * 2 + b - z + 4) % 4

            @pl.when(dz > 0)
            def _():
                kv_z(hh, dz).start()

        @pl.when(j % 2 == 1)
        def _():
            full = SCALE * dq_acc[...]
            for u in range(2):
                piece = full[:, u * TOK : (u + 1) * TOK].T.astype(BF)

                @pl.when(core == u)
                def _():
                    dq_ref[:, cols(core * 256 + hh * HD, HD)] = piece

                @pl.when(core != u)
                def _():
                    dq_out[:, hc] = piece

    mine_rows = rows(core * 256, 256)
    ht_send = extra(2, ht.at[mine_rows, :], ht.at[mine_rows, :])
    their_rows = rows((1 - core) * 256, 256)
    gh_send = extra(3, gh_own.at[their_rows, :], gh2.at[:, cols(core * TOK, TOK)])
    dq_send = extra(4, dq_out, dq_in)

    gh_acc[...] = jnp.zeros_like(gh_acc)
    w_copy.wait()

    def tick(g, c):
        def stage(low, n, fn, idx):
            @pl.when((g >= low) & (g < low + n))
            def _():
                fn(idx)

        stage(0, CH - 3, stage_a, g + 3)
        stage(0, CH - 1, stage_b, g + 1)
        stage(0, CH, stage_c, g)

        @pl.when(g == 0)
        def _():
            kv_spread()

        stage(1, CH, stage_d, g - 1)

        def stage_ready(i):
            @pl.when(gathers_x(i))
            def _():
                stage_x2(i)
                stage_e(i)

        stage(3, CH, stage_ready, g - 3)

        def stage_ready1(i):
            @pl.when(jnp.logical_not(gathers_x(i)))
            def _():
                stage_e(i)

        stage(1, CH, stage_ready1, g - 1)

        @pl.when(g == 3)
        def _():
            q_copy.wait()
            m_copy.wait()
            extra(0, q2.at[rows((1 - core) * TOK, TOK), :], q2.at[rows((1 - core) * TOK, TOK), :]).wait_recv()
            other = mask2.at[:, cols((1 - core) * TOK, TOK)]
            extra(1, other, other).wait_recv()
            for dz in range(1, 4):
                kv_far(dz, (z - dz + 4) % 4).wait_recv()

        @pl.when((g >= 3) & (g < 5))
        def _():
            def unit(j, c2):
                forward((g - 3) * 2 + j)
                return c2

            lax.fori_loop(0, 2, unit, 0)

        @pl.when(g == 4)
        def _():
            ht_send.start()

        @pl.when(g == 5)
        def _():
            extra(2, ht.at[their_rows, :], ht.at[their_rows, :]).wait_recv()
            hrow[...] = ht[:, cols(core * TOK, TOK)].astype(F32).T.astype(BF)

        @pl.when((g >= 5) & (g < 9))
        def _():
            def unit(i, c2):
                ready = i + 1 + 2 * gathers_x(i).astype(jnp.int32)

                @pl.when(jnp.maximum(ready, 5) == g)
                def _():
                    stage_f(i)

                return c2

            lax.fori_loop(0, CH, unit, 0)

        @pl.when(g == 8)
        def _():
            gh_own[...] = (gate * gh_acc[...]).astype(BF)
            gh2[:, cols(core * TOK, TOK)] = gh_own[mine_rows, :]
            gh_send.start()

        stage(5, CH, stage_la, g - 5)
        stage(7, CH, stage_lb, g - 7)
        stage(8, CH, stage_lc, g - 8)
        stage(9, CH, stage_ld, g - 9)

        @pl.when(g == 9)
        def _():
            other = gh2.at[:, cols((1 - core) * TOK, TOK)]
            extra(3, other, other).wait_recv()

        stage(9, 4, backward, g - 9)

        @pl.when(g == 11)
        def _():
            gw_part()

        @pl.when(g == 12)
        def _():
            dq_send.start()
            kv_reduce(0)

        @pl.when(g == 13)
        def _():
            gw_finish()

        @pl.when(g == 14)
        def _():
            kv_reduce(1)
            kv_finish(0)

        return c

    lax.fori_loop(0, 17, tick, 0)

    dq_send.wait_recv()
    dq_ref[:, cols((1 - core) * 256, 256)] = dq_in[...]
    kv_finish(1)

    def all_sent(i, c):
        sent(AGY, i, cot.at[i, rows(x * 128, 64), :])

        @pl.when(scatters_y(i))
        def _():
            for n in range(4):
                sent(P0 + n, i, p4b.at[slot(i), n])
            for kind in (F1, F2):
                sent(kind, i, cot.at[i, rows(x * 128, 32), :])
            for kind in (R1, R2):
                sent(kind, i, cot.at[i, rows(x * 128, 64), :])

        @pl.when(jnp.logical_not(scatters_y(i)))
        def _():
            sent(F1, i, f1b.at[i])
            sent(F2, i, f2b.at[i])
            sent(R1, i, r1b.at[i])
            sent(R2, i, r2b.at[i])
            sent(YX, i, ys.at[i])

        @pl.when(i > 1)
        def _():
            sent(GW, i, gw_out.at[i])

        return c

    lax.fori_loop(0, CH, all_sent, 0)
    for n in range(1, 4):
        for copy_ in kv_near(n, rows(s * 128, 128)):
            copy_.wait_send()
        kv_far(n, z).wait_send()
        for hh in range(2):
            kv_z(hh, n).wait_send()
            kv_y(hh, n).wait_send()
    gw_send.wait_send()
    for c in (q_send, m_send, ht_send, gh_send, dq_send):
        c.wait_send()


def hand_over(*refs):
    sems = refs[10]
    copies = [pltpu.make_async_copy(refs[n], refs[5 + n], sems.at[n]) for n in range(5)]
    for c in copies:
        c.start()
    for c in copies:
        c.wait()


def per_device(queries, audio_keys, audio_values, out_weight, mix_gate, block_mask, cotangent):
    mask_rows = jnp.repeat(block_mask.T.astype(F32), BLK, axis=1)
    hbm = pl.BlockSpec(memory_space=pl.ANY)
    vmem = pl.BlockSpec(memory_space=pltpu.VMEM)
    dma = pltpu.SemaphoreType.DMA
    results = pl.pallas_call(
        kernel,
        out_shape=(
            jax.ShapeDtypeStruct((64, 8192), BF),
            jax.ShapeDtypeStruct((TOK, 512), BF),
            jax.ShapeDtypeStruct((128, 512), BF),
            jax.ShapeDtypeStruct((128, 512), BF),
            jax.ShapeDtypeStruct((512, 512), BF),
        ),
        in_specs=[hbm, hbm, hbm, hbm, vmem, vmem, hbm],
        out_specs=[vmem] * 5,
        scratch_shapes=[
            pltpu.VMEM((512, 8192), BF),
            pltpu.VMEM((CH, TOK, WC), BF),
            pltpu.VMEM((CH, TOK, HALF), BF),
            pltpu.VMEM((AUD, 512), BF),
            pltpu.VMEM((2 * TOK, 256), BF),
            pltpu.VMEM((16, 2 * TOK), F32),
            pltpu.VMEM((512, 2 * TOK), BF),
            pltpu.VMEM((TOK, 512), BF),
            pltpu.VMEM((512, TOK), F32),
            pltpu.VMEM((512, TOK), BF),
            pltpu.VMEM((256, 2 * TOK), BF),
            pltpu.VMEM((AUD, TOK), F32),
            pltpu.VMEM((AUD, TOK), BF),
            pltpu.VMEM((2, 1, 2 * TOK), F32),
            pltpu.VMEM((1, 2 * TOK), F32),
            pltpu.VMEM((HD, 2 * TOK), F32),
            pltpu.VMEM((TOK, 256), BF),
            pltpu.VMEM((TOK, 256), BF),
            pltpu.VMEM((CH, 64, WC), BF),
            pltpu.VMEM((CH, 64, WC), BF),
            pltpu.VMEM((CH, 128, WC), BF),
            pltpu.VMEM((CH, 128, WC), BF),
            pltpu.VMEM((CH, 64, WC), BF),
            pltpu.VMEM((CH, 64, WC), BF),
            pltpu.VMEM((3, 4, 64, WC), BF),
            pltpu.VMEM((CH, 512, HALF), BF),
            pltpu.VMEM((CH - 2, 512, HALF), BF),
            pltpu.VMEM((512, HALF), BF),
            pltpu.VMEM((512, HALF), BF),
            pltpu.VMEM((2, AUD, 256), BF),
            pltpu.VMEM((2, 3, 512, 256), BF),
            pltpu.VMEM((2, 4, 128, 256), BF),
            pltpu.VMEM((2, 4, 128, 256), BF),
            dma((KINDS, CH)), dma((KINDS, CH)),
            dma((4, 2)), dma((4, 2)),
            dma((4,)), dma((4,)),
            dma((2, 4)), dma((2, 4)),
            dma((2, 4)), dma((2, 4)),
            dma((5,)), dma((5,)),
            dma((CH + 5,)),
        ],
        compiler_params=pltpu.CompilerParams(
            collective_id=0, has_side_effects=True, vmem_limit_bytes=62 * 2**20
        ),
        cost_estimate=pl.CostEstimate(flops=20 * 10**9, bytes_accessed=16 * 2**20, transcendentals=8 * 2**20),
    )(queries, audio_keys, audio_values, out_weight, mix_gate.reshape(1, 1), mask_rows, cotangent)
    return pl.pallas_call(
        hand_over,
        out_shape=tuple(jax.ShapeDtypeStruct(r.shape, r.dtype) for r in results),
        in_specs=[vmem] * 5,
        out_specs=[hbm] * 5,
        scratch_shapes=[dma((5,))],
    )(*results)


def solution(mesh):
    in_specs = (
        P("seq", "tp"),
        P("seq", "tp"),
        P("seq", "tp"),
        P("tp", None),
        P(),
        P("seq", None),
        P(("seq", "tp"), None),
    )
    out_specs = (
        P(("seq", "tp"), None),
        P("seq", "tp"),
        P("seq", "tp"),
        P("seq", "tp"),
        P("tp", "seq"),
    )
    return jax.shard_map(
        per_device, mesh=mesh, in_specs=in_specs, out_specs=out_specs, check_vma=False
    )
```

```python
import jax
import jax.numpy as jnp
from jax import lax
from jax.experimental import pallas as pl
from jax.experimental.pallas import tpu as pltpu
from jax.sharding import PartitionSpec as P

HD = 128
BLK = 128
CH = 8
WC = 1024
HALF = 512
TOK = 512
AUD = 2048
SCALE = HD ** (-0.5)
C2 = SCALE * 1.4426950408889634
NEG = -1e30
BF = jnp.bfloat16
F32 = jnp.float32
MESH = pl.DeviceIdType.MESH

NT = (((1,), (1,)), ((), ()))
NN = (((1,), (0,)), ((), ()))
TN = (((0,), (0,)), ((), ()))

AGY, AGP, AGM, AFP, AFM, SIB, GW, F1, F2, R1, R2, YX, YP, YM, YF, P0 = range(16)
KINDS = P0 + 4
GATHER_X = (3, 5)
SCATTER_Y = (1, 3, 5)
TICKS = 48
PLAN = (
    ('BW', (31, 32, 33, 34), (0, 1, 2, 3)),
    ('DQ', (38,), (0,)),
    ('LB', (29, 30, 32, 34, 35, 38, 41, 42), (7, 5, 2, 0, 3, 1, 4, 6)),
    ('LC', (35, 36, 37, 38, 39, 42, 45, 46), (5, 7, 2, 0, 3, 1, 4, 6)),
    ('K0', (0,), (0,)),
    ('GP', (36,), (0,)),
    ('B', (0, 1, 10, 11, 12, 13, 14, 15), (3, 5, 4, 7, 1, 0, 2, 6)),
    ('FW', (15, 16, 17, 18), (0, 1, 2, 3)),
    ('A', (1, 2, 3, 4, 5, 6, 7, 8), (4, 5, 7, 1, 3, 0, 2, 6)),
    ('C', (8, 9, 11, 12, 17, 20, 21, 22), (3, 5, 4, 7, 0, 2, 1, 6)),
    ('K1', (8,), (0,)),
    ('KR', (41, 45), (0, 1)),
    ('D', (9, 10, 13, 17, 24, 25, 27, 28), (3, 5, 4, 7, 0, 2, 1, 6)),
    ('HR', (21,), (0,)),
    ('X', (18, 19), (3, 5)),
    ('E', (13, 17, 18, 19, 24, 25, 27, 28), (4, 7, 3, 5, 0, 2, 1, 6)),
    ('GH', (28,), (0,)),
    ('F', (21, 23, 24, 25, 26, 28, 36, 37), (5, 7, 3, 0, 2, 1, 4, 6)),
    ('KF', (45, 46), (0, 1)),
    ('LD', (39, 40, 42, 43, 44, 45, 46, 47), (7, 5, 3, 2, 0, 4, 1, 6)),
    ('DF', (38,), (0,)),
    ('GF', (47,), (0,)),
    ('LA', (22, 23, 24, 25, 26, 30, 36, 37), (5, 7, 3, 0, 2, 1, 4, 6)),
    ('HX', (19,), (0,)),
)


def dot(a, b, dims):
    return lax.dot_general(a, b, dims, preferred_element_type=F32)


def kernel(
    q_hbm, k_hbm, v_hbm, w_hbm, gate_ref, mask_ref, cot_hbm,
    layer_ref, dq_ref, dk_ref, dv_ref, gw_ref,
    w, cot, cot_sib, kvb, q2, mask2, ht, hrow, gh_acc, gh_own, gh2,
    sc, pb, lse, delta, dq_acc, dq_out, dq_in, f1b, f2b, r1b, r2b, ys, yr, p4b, gw_out, gw_in, gw_sum, gw_par, kv_out, kv_in, kv_red, kv_fin,
    ss, rs, ps, pr, zs, zr, ds_, dr, fs, fr, es, er, ls,
):
    s = lax.axis_index("seq")
    t = lax.axis_index("tp")
    core = s % 2
    z = s // 4
    yl = (s // 2) % 2
    x = t // 2
    yh = t % 2
    xn, xb, xf = (x + 1) % 4, (x + 3) % 4, (x + 2) % 4
    sib = (s + 1 - 2 * core, t)
    nxt = (s, xn * 2 + yh)
    prv = (s, xb * 2 + yh)
    par = (s, x * 2 + 1 - yh)

    def zdev(dz):
        return (((z + dz) % 4) * 4 + yl * 2 + core, t)

    def near(n):
        return (z * 4 + ((yl + n // 2) % 2) * 2 + (core + n) % 2, t)

    def rows(start, size):
        return pl.ds(pl.multiple_of(start, size), size)

    def cols(start, size):
        return pl.ds(pl.multiple_of(start, 128), size)

    def chunk(i):
        m = i // 2
        zz = ((z // 2 + m // 2) % 2) * 2 + (z + m) % 2
        return zz * 2 + (yl + i) % 2

    def copy(kind, i, src, dst, dev):
        return pltpu.make_async_remote_copy(
            src_ref=src, dst_ref=dst, send_sem=ss.at[kind, i], recv_sem=rs.at[kind, i],
            device_id=dev, device_id_type=MESH,
        )

    def got(kind, i, dst):
        copy(kind, i, dst, dst, nxt).wait_recv()

    def sent(kind, i, src):
        copy(kind, i, src, src, nxt).wait_send()

    barrier = pltpu.get_barrier_semaphore()
    for dev in (nxt, prv, par):
        pl.semaphore_signal(barrier, inc=1, device_id=dev, device_id_type=MESH)

    for n in range(1, 4):
        pl.semaphore_signal(barrier, inc=1, device_id=near(n), device_id_type=MESH)
        pl.semaphore_signal(barrier, inc=1, device_id=zdev(n), device_id_type=MESH)

    def own_piece(i):
        return pltpu.make_async_copy(
            cot_hbm.at[:, cols(chunk(i) * WC, WC)], cot.at[i, rows(t * 64, 64), :], ls.at[i]
        )

    def start_piece(i, c):
        own_piece(i).start()
        return c

    lax.fori_loop(0, CH, start_piece, 0)
    w_copy = pltpu.make_async_copy(w_hbm, w, ls.at[CH])
    my_heads = cols(core * 256, 256)
    k_copy = pltpu.make_async_copy(k_hbm.at[:, my_heads], kvb.at[rows(s * 128, 128), pl.ds(0, 256)], ls.at[CH + 1])
    v_copy = pltpu.make_async_copy(v_hbm.at[:, my_heads], kvb.at[rows(s * 128, 128), pl.ds(256, 256)], ls.at[CH + 2])
    q_copy = pltpu.make_async_copy(q_hbm.at[:, my_heads], q2.at[rows(core * TOK, TOK), :], ls.at[CH + 3])
    m_copy = pltpu.make_async_copy(mask_ref, mask2.at[:, cols(core * TOK, TOK)], ls.at[CH + 4])
    for c in (w_copy, k_copy, v_copy, q_copy, m_copy):
        c.start()

    pl.semaphore_wait(barrier, 9)

    def stage_a(i):
        copy(AGY, i, cot_hbm.at[:, cols(chunk(i) * WC, WC)], cot.at[i, rows(t * 64, 64), :], par).start()

    def piece_x(i):
        src = cot_hbm.at[:, cols(chunk(i) * WC, WC)]
        dst = cot.at[i, rows(t * 64, 64), :]
        copy(AGP, i, src, dst, nxt).start()
        copy(AGM, i, src, dst, prv).start()


    def extra(n, src, dst):
        return pltpu.make_async_remote_copy(
            src_ref=src, dst_ref=dst, send_sem=es.at[n], recv_sem=er.at[n], device_id=sib, device_id_type=MESH
        )

    other_heads = cols((1 - core) * 256, 256)
    q_send = extra(0, q_hbm.at[:, other_heads], q2.at[rows(core * TOK, TOK), :])
    q_send.start()
    m_send = extra(1, mask_ref, mask2.at[:, cols(core * TOK, TOK)])
    m_send.start()

    def kv_near(n, src_rows):
        heads = cols(((core + n) % 2) * 256, 256)
        return [
            pltpu.make_async_remote_copy(
                src_ref=src.at[:, heads], dst_ref=kvb.at[src_rows, pl.ds(part * 256, 256)],
                send_sem=ps.at[n, part], recv_sem=pr.at[n, part], device_id=near(n), device_id_type=MESH)
            for part, src in enumerate((k_hbm, v_hbm))
        ]

    def kv_far(dz, zz):
        block = kvb.at[rows(zz * 512, 512), :]
        return pltpu.make_async_remote_copy(
            src_ref=block, dst_ref=block, send_sem=zs.at[dz], recv_sem=zr.at[dz],
            device_id=zdev(dz), device_id_type=MESH)

    def kv_share():
        for n in range(1, 4):
            for copy_ in kv_near(n, rows(s * 128, 128)):
                copy_.start()

    def kv_spread():
        k_copy.wait()
        v_copy.wait()
        for n in range(1, 4):
            src = z * 4 + ((yl + n // 2) % 2) * 2 + (core + n) % 2
            for copy_ in kv_near(n, rows(src * 128, 128)):
                copy_.wait_recv()
        for dz in (1, 3, 2):
            kv_far(dz, z).start()

    gate = jnp.tanh(gate_ref[...])

    def stage_b1(i):
        own_piece(i).wait()
        got(AGY, i, cot.at[i, rows((x * 2 + 1 - yh) * 64, 64), :])
        block = cot.at[i, rows(x * 128, 128), :]
        copy(AGP, i, block, block, nxt).start()
        copy(AGM, i, block, block, prv).start()

    def stage_c1(i):
        got(AGP, i, cot.at[i, rows(xb * 128, 128), :])
        top = cot.at[i, rows(xb * 128, 64), :]
        copy(AFP, i, top, top, nxt).start()
        got(AGM, i, cot.at[i, rows(xn * 128, 128), :])
        low = cot.at[i, rows(xn * 128 + 64, 64), :]
        copy(AFM, i, low, low, prv).start()

    def stage_d1(i):
        got(AFP, i, cot.at[i, rows(xf * 128, 64), :])
        got(AFM, i, cot.at[i, rows(xf * 128 + 64, 64), :])
        share(i)

    def share(i):
        copy(SIB, i, cot.at[i, :, cols((1 - core) * HALF, HALF)], cot_sib.at[i], sib).start()

    def to_partner(kind, i, xx):
        block = cot.at[i, rows(xx * 128 + yh * 64, 64), :]
        copy(kind, i, block, block, par).start()

    def stage_c2(i):
        got(AGP, i, cot.at[i, rows(xb * 128 + yh * 64, 64), :])
        top = cot.at[i, rows(xb * 128 + yh * 64, 32), :]
        copy(AFP, i, top, top, nxt).start()
        got(AGM, i, cot.at[i, rows(xn * 128 + yh * 64, 64), :])
        low = cot.at[i, rows(xn * 128 + yh * 64 + 32, 32), :]
        copy(AFM, i, low, low, prv).start()
        to_partner(YP, i, xb)
        to_partner(YM, i, xn)

    def stage_d2(i):
        got(AFP, i, cot.at[i, rows(xf * 128 + yh * 64, 32), :])
        got(AFM, i, cot.at[i, rows(xf * 128 + yh * 64 + 32, 32), :])
        to_partner(YF, i, xf)

    def stage_x2(i):
        own_piece(i).wait()
        for kind, xx in ((AGY, x), (YP, xb), (YM, xn), (YF, xf)):
            got(kind, i, cot.at[i, rows(xx * 128 + (1 - yh) * 64, 64), :])
        share(i)

    def either(first, second, cond):
        def stage(i):
            @pl.when(cond(i))
            def _():
                first(i)

            @pl.when(jnp.logical_not(cond(i)))
            def _():
                second(i)

        return stage

    def member(i, chosen):
        hit = i < 0
        for n in chosen:
            hit = jnp.logical_or(hit, i == n)
        return hit

    def gathers_x(i):
        return member(i, GATHER_X)

    stage_b = either(piece_x, stage_b1, gathers_x)
    stage_c = either(stage_c2, stage_c1, gathers_x)
    stage_d = either(stage_d2, stage_d1, gathers_x)

    def gather_sent(i):
        @pl.when(gathers_x(i))
        def _():
            for kind in (AGP, AGM, YP, YM, YF):
                sent(kind, i, cot.at[i, rows(x * 128, 64), :])
            for kind in (AFP, AFM):
                sent(kind, i, cot.at[i, rows(x * 128, 32), :])

        @pl.when(jnp.logical_not(gathers_x(i)))
        def _():
            for kind in (AGP, AGM):
                sent(kind, i, cot.at[i, rows(x * 128, 128), :])
            for kind in (AFP, AFM):
                sent(kind, i, cot.at[i, rows(x * 128, 64), :])

    def stage_e(i):
        cc = cols(chunk(i) * WC, WC)
        for part in range(2):
            rr = pl.ds(part * 256, 256)
            gh_acc[rr, :] += dot(w[rr, cc], cot[i], NT)

    def stage_f(i):
        got(SIB, i, cot_sib.at[i])
        mine = cols(core * TOK, TOK)
        theirs = cols((1 - core) * TOK, TOK)
        for part in range(2):
            rr = pl.ds(part * 256, 256)
            val = dot(ht[rr, mine], cot[i, :, cols(core * HALF, HALF)], NN) + dot(ht[rr, theirs], cot_sib[i], NN)
            gw_out[i, rr, :] = val.astype(BF)

        @pl.when(i > 1)
        def _():
            zz = chunk(i) // 2
            copy(GW, i, gw_out.at[i], gw_in.at[i - 2], (zz * 4 + yl * 2 + core, t)).start()

    def product(i):
        gather_sent(i)
        sent(SIB, i, cot_sib.at[i])
        for part in range(2):
            cc = cols(chunk(i) * WC + part * HALF, HALF)
            cot[i, :, pl.ds(part * HALF, HALF)] = dot(hrow[...], w[:, cc], NN).astype(BF)

    def stage_la1(i):
        product(i)
        copy(F1, i, cot.at[i, rows(xf * 128, 64), :], f1b.at[i], nxt).start()
        copy(F2, i, cot.at[i, rows(xf * 128 + 64, 64), :], f2b.at[i], prv).start()

    def stage_lb1(i):
        got(F1, i, f1b.at[i])
        rr = rows(xn * 128, 64)
        cot[i, rr, :] = (cot[i, rr, :].astype(F32) + f1b[i].astype(F32)).astype(BF)
        copy(R1, i, cot.at[i, rows(xn * 128, 128), :], r1b.at[i], nxt).start()
        got(F2, i, f2b.at[i])
        rr = rows(xb * 128 + 64, 64)
        cot[i, rr, :] = (cot[i, rr, :].astype(F32) + f2b[i].astype(F32)).astype(BF)
        copy(R2, i, cot.at[i, rows(xb * 128, 128), :], r2b.at[i], prv).start()

    def reduced(i, which):
        rr = rows(which * 64, 64)
        return (
            cot[i, rows(x * 128 + which * 64, 64), :].astype(F32)
            + r1b[i, rr, :].astype(F32)
            + r2b[i, rr, :].astype(F32)
        )

    def stage_lc1(i):
        got(R1, i, r1b.at[i])
        got(R2, i, r2b.at[i])
        ys[i] = reduced(i, 1 - yh).astype(BF)
        copy(YX, i, ys.at[i], yr.at[i], par).start()

    def stage_ld1(i):
        got(YX, i, yr.at[i])
        total = reduced(i, yh) + yr[i].astype(F32)
        layer_ref[:, cols(chunk(i) * WC, WC)] = (gate * total).astype(BF)

    def slot(i):
        return sum((i > n).astype(jnp.int32) for n in SCATTER_Y)

    def stage_la2(i):
        product(i)
        for n in range(4):
            copy(P0 + n, i, cot.at[i, rows(n * 128 + (1 - yh) * 64, 64), :], p4b.at[slot(i), n], par).start()

    def add_partner(i, xx):
        rr = rows(xx * 128 + yh * 64, 64)
        return cot[i, rr, :].astype(F32) + p4b[slot(i), xx].astype(F32)

    def stage_lb2(i):
        for n in range(4):
            got(P0 + n, i, p4b.at[slot(i), n])
        rr = rows(xf * 128 + yh * 64, 64)
        cot[i, rr, :] = add_partner(i, xf).astype(BF)
        copy(F1, i, cot.at[i, rows(xf * 128 + yh * 64, 32), :], f1b.at[i, pl.ds(0, 32), :], nxt).start()
        copy(F2, i, cot.at[i, rows(xf * 128 + yh * 64 + 32, 32), :], f2b.at[i, pl.ds(0, 32), :], prv).start()

    def stage_lc2(i):
        top, low = pl.ds(0, 32), pl.ds(0, 64)
        got(F1, i, f1b.at[i, top, :])
        val = add_partner(i, xn)
        cot[i, rows(xn * 128 + yh * 64, 32), :] = (val[:32] + f1b[i, top, :].astype(F32)).astype(BF)
        cot[i, rows(xn * 128 + yh * 64 + 32, 32), :] = val[32:].astype(BF)
        copy(R1, i, cot.at[i, rows(xn * 128 + yh * 64, 64), :], r1b.at[i, low, :], nxt).start()
        got(F2, i, f2b.at[i, top, :])
        val = add_partner(i, xb)
        cot[i, rows(xb * 128 + yh * 64, 32), :] = val[:32].astype(BF)
        cot[i, rows(xb * 128 + yh * 64 + 32, 32), :] = (val[32:] + f2b[i, top, :].astype(F32)).astype(BF)
        copy(R2, i, cot.at[i, rows(xb * 128 + yh * 64, 64), :], r2b.at[i, low, :], prv).start()

    def stage_ld2(i):
        low = pl.ds(0, 64)
        got(R1, i, r1b.at[i, low, :])
        got(R2, i, r2b.at[i, low, :])
        total = add_partner(i, x) + r1b[i, low, :].astype(F32) + r2b[i, low, :].astype(F32)
        layer_ref[:, cols(chunk(i) * WC, WC)] = (gate * total).astype(BF)

    def scatters_y(i):
        return member(i, SCATTER_Y)

    stage_la = either(stage_la2, stage_la1, scatters_y)
    stage_lb = either(stage_lb2, stage_lb1, scatters_y)
    stage_lc = either(stage_lc2, stage_lc1, scatters_y)
    stage_ld = either(stage_ld2, stage_ld1, scatters_y)

    def masked(score, row, tok):
        return jnp.where(mask2[pl.ds(row, 1), tok] > 0, score, NEG)

    def forward(j):
        hh, u = j // 2, j % 2
        hc = cols(hh * HD, HD)
        vc = cols(256 + hh * HD, HD)
        tok = cols(u * TOK, TOK)
        qv = q2[rows(u * TOK, TOK), hc]

        def scores(ab, best):
            part = dot(kvb[rows(ab * 256, 256), hc], qv, NT)
            for b in range(2):
                val = masked(part[b * 128 : (b + 1) * 128], ab * 2 + b, tok)
                sc[rows(ab * 256 + b * 128, 128), :] = val
                best = jnp.maximum(best, jnp.max(val, axis=0, keepdims=True))
            return best

        best = lax.fori_loop(0, AUD // 256, scores, jnp.full((1, TOK), NEG, F32))

        def weigh(ab, total):
            rr = rows(ab * 256, 256)
            val = jnp.exp2((sc[rr, :] - best) * C2)
            pb[rr, :] = val.astype(BF)
            return total + jnp.sum(val, axis=0, keepdims=True)

        total = lax.fori_loop(0, AUD // 256, weigh, jnp.zeros((1, TOK), F32))
        out = dot(kvb[:, vc], pb[...], TN)
        ht[rows(core * 256 + hh * HD, HD), tok] = (out / total).astype(BF)
        lse[hh, :, tok] = best * C2 + jnp.log2(total)

    def kv_z(hh, dz):
        return pltpu.make_async_remote_copy(
            src_ref=kv_out.at[hh, rows(((z + dz) % 4) * 512, 512), :], dst_ref=kv_in.at[hh, dz - 1],
            send_sem=ds_.at[hh, dz], recv_sem=dr.at[hh, dz], device_id=zdev(dz), device_id_type=MESH)

    def kv_y(hh, n):
        src = ((yl + n // 2) % 2) * 2 + (core + n) % 2
        return pltpu.make_async_remote_copy(
            src_ref=kv_red.at[hh, src], dst_ref=kv_fin.at[hh, n],
            send_sem=fs.at[hh, n], recv_sem=fr.at[hh, n], device_id=near(n), device_id_type=MESH)

    def kv_reduce(hh):
        for dz in range(1, 4):
            kv_z(hh, dz).wait_recv()
        for b in range(4):
            total = kv_out[hh, rows(z * 512 + b * 128, 128), :].astype(F32)
            for dz in range(3):
                total += kv_in[hh, dz, b * 128 : (b + 1) * 128, :].astype(F32)
            kv_red[hh, b] = total.astype(BF)
        for n in range(1, 4):
            kv_y(hh, n).start()

    def kv_finish(hh):
        for n in range(1, 4):
            kv_y(hh, n).wait_recv()
        same = kv_red[hh, yl * 2 + core].astype(F32) + kv_fin[hh, 2].astype(F32)
        other = kv_fin[hh, 1].astype(F32) + kv_fin[hh, 3].astype(F32)
        hc = cols(core * 256 + hh * HD, HD)
        dk_ref[:, hc] = same[:, :HD].astype(BF)
        dv_ref[:, hc] = same[:, HD:].astype(BF)
        hc = cols((1 - core) * 256 + hh * HD, HD)
        dk_ref[:, hc] = other[:, :HD].astype(BF)
        dv_ref[:, hc] = other[:, HD:].astype(BF)

    gw_send = pltpu.make_async_remote_copy(
        src_ref=gw_sum, dst_ref=gw_par, send_sem=fs.at[0, 0], recv_sem=fr.at[0, 0],
        device_id=near(2), device_id_type=MESH)

    def gw_reduce(which, write):
        def got_one(i, c):
            got(GW, 2 * i + which, gw_in.at[2 * i + which - 2])
            return c

        lax.fori_loop(1, 4, got_one, 0)

        def add(b, c):
            rr = rows(b * 64, 64)
            total = gw_out[which, rr, :].astype(F32)
            for i in range(3):
                total += gw_in[2 * i + which, rr, :].astype(F32)
            write(rr, total)
            return c

        lax.fori_loop(0, 8, add, 0)

    def gw_part():
        def write(rr, total):
            gw_sum[rr, :] = total.astype(BF)

        gw_reduce(1, write)
        gw_send.start()

    def gw_finish():
        gw_send.wait_recv()

        def write(rr, total):
            gw_ref[rr, :] = (gate * (total + gw_par[rr, :].astype(F32))).astype(BF)

        gw_reduce(0, write)

    def backward(j):
        hh = j // 2
        ah = (j + 1 + z // 2) % 2
        hc = cols(hh * HD, HD)
        hr = rows(hh * HD, HD)
        first = j % 2 == 0

        @pl.when(first)
        def _():
            dq_acc[...] = jnp.zeros_like(dq_acc)
            own = ht[rows(core * 256 + hh * HD, HD), :].astype(F32)
            delta[...] = jnp.sum(gh2[hr, :].astype(F32) * own, axis=0, keepdims=True)

        def step(b, c):
            rr = rows(ah * 1024 + b * 256, 256)
            kk = kvb[rr, hc]
            vv = kvb[rr, cols(256 + hh * HD, HD)]
            qv = q2[:, hc]
            gv = gh2[hr, :]
            score = dot(kk, qv, NT)
            logs = lse[hh]
            probs = []
            for m in range(2):
                row = ah * 8 + b * 2 + m
                val = masked(score[m * 128 : (m + 1) * 128], row, slice(None))
                probs.append(jnp.exp2(val * C2 - logs))
            prob = jnp.concatenate(probs, axis=0)
            dp = dot(vv, gv, NN)
            dsc = (prob * (dp - delta[...])).astype(BF)
            kv_out[hh, rr, pl.ds(HD, HD)] = dot(prob.astype(BF), gv, NT).astype(BF)
            kv_out[hh, rr, pl.ds(0, HD)] = (SCALE * dot(dsc, qv, NN)).astype(BF)
            dq_acc[...] += dot(kk, dsc, TN)
            return c

        lax.fori_loop(0, 4, step, 0)

        for b in range(2):
            dz = (ah * 2 + b - z + 4) % 4

            @pl.when(dz > 0)
            def _():
                kv_z(hh, dz).start()

        @pl.when(j % 2 == 1)
        def _():
            full = SCALE * dq_acc[...]
            for u in range(2):
                piece = full[:, u * TOK : (u + 1) * TOK].T.astype(BF)

                @pl.when(core == u)
                def _():
                    dq_ref[:, cols(core * 256 + hh * HD, HD)] = piece

                @pl.when(core != u)
                def _():
                    dq_out[:, hc] = piece

    mine_rows = rows(core * 256, 256)
    ht_send = extra(2, ht.at[mine_rows, :], ht.at[mine_rows, :])
    their_rows = rows((1 - core) * 256, 256)
    gh_send = extra(3, gh_own.at[their_rows, :], gh2.at[:, cols(core * TOK, TOK)])
    dq_send = extra(4, dq_out, dq_in)

    gh_acc[...] = jnp.zeros_like(gh_acc)

    def heads_first():
        q_copy.wait()
        m_copy.wait()
        other_q = q2.at[rows((1 - core) * TOK, TOK), :]
        extra(0, other_q, other_q).wait_recv()
        other_m = mask2.at[:, cols((1 - core) * TOK, TOK)]
        extra(1, other_m, other_m).wait_recv()
        for dz in range(1, 4):
            kv_far(dz, (z - dz + 4) % 4).wait_recv()

    def on_first(i, fn):
        @pl.when(i == 0)
        def _():
            fn()

    def stage_fw(j):
        on_first(j, heads_first)
        forward(j)

    def gh_got():
        other = gh2.at[:, cols((1 - core) * TOK, TOK)]
        extra(3, other, other).wait_recv()

    def stage_bw(j):
        on_first(j, gh_got)
        backward(j)

    def stage_hr():
        extra(2, ht.at[their_rows, :], ht.at[their_rows, :]).wait_recv()
        hrow[...] = ht[:, cols(core * TOK, TOK)].astype(F32).T.astype(BF)

    def stage_gh():
        gh_own[...] = (gate * gh_acc[...]).astype(BF)
        gh2[:, cols(core * TOK, TOK)] = gh_own[mine_rows, :]
        gh_send.start()

    def stage_df():
        dq_send.wait_recv()
        dq_ref[:, cols((1 - core) * 256, 256)] = dq_in[...]

    once = {
        "K0": kv_share, "K1": kv_spread, "HX": ht_send.start, "HR": stage_hr, "GH": stage_gh,
        "GP": gw_part, "GF": gw_finish, "DQ": dq_send.start, "DF": stage_df,
    }
    each = {
        "A": stage_a, "B": stage_b, "C": stage_c, "D": stage_d, "X": stage_x2, "E": stage_e, "F": stage_f,
        "LA": stage_la, "LB": stage_lb, "LC": stage_lc, "LD": stage_ld,
        "FW": stage_fw, "BW": stage_bw, "KR": kv_reduce, "KF": kv_finish,
    }
    w_tick = min(ticks[0] for name, ticks, _ in PLAN if name == "E")

    def packed(ticks, low):
        return jnp.int32(sum(1 << (n - low) for n in ticks if low <= n < low + 30))

    def tick(g, state):
        after = []
        for (name, ticks, idx), (bits, order) in zip(PLAN, state):
            for low in range(30, TICKS, 30):
                bits = jnp.where(g == low, packed(ticks, low), bits)
            hit = bits % 2 == 1
            if name == "E":

                @pl.when(g == w_tick)
                def _():
                    w_copy.wait()

            @pl.when(hit)
            def _():
                if name in once:
                    once[name]()
                else:
                    each[name](order % 8)

            after.append((bits // 2, jnp.where(hit, order // 8, order)))
        return tuple(after)

    start = tuple(
        (packed(ticks, 0), jnp.int32(sum(i << (3 * n) for n, i in enumerate(idx)))) for _, ticks, idx in PLAN
    )
    lax.fori_loop(0, TICKS, tick, start)

    def all_sent(i, c):
        sent(AGY, i, cot.at[i, rows(x * 128, 64), :])

        @pl.when(scatters_y(i))
        def _():
            for n in range(4):
                sent(P0 + n, i, p4b.at[slot(i), n])
            for kind in (F1, F2):
                sent(kind, i, cot.at[i, rows(x * 128, 32), :])
            for kind in (R1, R2):
                sent(kind, i, cot.at[i, rows(x * 128, 64), :])

        @pl.when(jnp.logical_not(scatters_y(i)))
        def _():
            sent(F1, i, f1b.at[i])
            sent(F2, i, f2b.at[i])
            sent(R1, i, r1b.at[i])
            sent(R2, i, r2b.at[i])
            sent(YX, i, ys.at[i])

        @pl.when(i > 1)
        def _():
            sent(GW, i, gw_out.at[i])

        return c

    lax.fori_loop(0, CH, all_sent, 0)
    for n in range(1, 4):
        for copy_ in kv_near(n, rows(s * 128, 128)):
            copy_.wait_send()
        kv_far(n, z).wait_send()
        for hh in range(2):
            kv_z(hh, n).wait_send()
            kv_y(hh, n).wait_send()
    gw_send.wait_send()
    for c in (q_send, m_send, ht_send, gh_send, dq_send):
        c.wait_send()


def hand_over(*refs):
    sems = refs[10]
    copies = [pltpu.make_async_copy(refs[n], refs[5 + n], sems.at[n]) for n in range(5)]
    for c in copies:
        c.start()
    for c in copies:
        c.wait()


def per_device(queries, audio_keys, audio_values, out_weight, mix_gate, block_mask, cotangent):
    mask_rows = jnp.repeat(block_mask.T.astype(F32), BLK, axis=1)
    hbm = pl.BlockSpec(memory_space=pl.ANY)
    vmem = pl.BlockSpec(memory_space=pltpu.VMEM)
    dma = pltpu.SemaphoreType.DMA
    results = pl.pallas_call(
        kernel,
        out_shape=(
            jax.ShapeDtypeStruct((64, 8192), BF),
            jax.ShapeDtypeStruct((TOK, 512), BF),
            jax.ShapeDtypeStruct((128, 512), BF),
            jax.ShapeDtypeStruct((128, 512), BF),
            jax.ShapeDtypeStruct((512, 512), BF),
        ),
        in_specs=[hbm, hbm, hbm, hbm, vmem, vmem, hbm],
        out_specs=[vmem] * 5,
        scratch_shapes=[
            pltpu.VMEM((512, 8192), BF),
            pltpu.VMEM((CH, TOK, WC), BF),
            pltpu.VMEM((CH, TOK, HALF), BF),
            pltpu.VMEM((AUD, 512), BF),
            pltpu.VMEM((2 * TOK, 256), BF),
            pltpu.VMEM((16, 2 * TOK), F32),
            pltpu.VMEM((512, 2 * TOK), BF),
            pltpu.VMEM((TOK, 512), BF),
            pltpu.VMEM((512, TOK), F32),
            pltpu.VMEM((512, TOK), BF),
            pltpu.VMEM((256, 2 * TOK), BF),
            pltpu.VMEM((AUD, TOK), F32),
            pltpu.VMEM((AUD, TOK), BF),
            pltpu.VMEM((2, 1, 2 * TOK), F32),
            pltpu.VMEM((1, 2 * TOK), F32),
            pltpu.VMEM((HD, 2 * TOK), F32),
            pltpu.VMEM((TOK, 256), BF),
            pltpu.VMEM((TOK, 256), BF),
            pltpu.VMEM((CH, 64, WC), BF),
            pltpu.VMEM((CH, 64, WC), BF),
            pltpu.VMEM((CH, 128, WC), BF),
            pltpu.VMEM((CH, 128, WC), BF),
            pltpu.VMEM((CH, 64, WC), BF),
            pltpu.VMEM((CH, 64, WC), BF),
            pltpu.VMEM((3, 4, 64, WC), BF),
            pltpu.VMEM((CH, 512, HALF), BF),
            pltpu.VMEM((CH - 2, 512, HALF), BF),
            pltpu.VMEM((512, HALF), BF),
            pltpu.VMEM((512, HALF), BF),
            pltpu.VMEM((2, AUD, 256), BF),
            pltpu.VMEM((2, 3, 512, 256), BF),
            pltpu.VMEM((2, 4, 128, 256), BF),
            pltpu.VMEM((2, 4, 128, 256), BF),
            dma((KINDS, CH)), dma((KINDS, CH)),
            dma((4, 2)), dma((4, 2)),
            dma((4,)), dma((4,)),
            dma((2, 4)), dma((2, 4)),
            dma((2, 4)), dma((2, 4)),
            dma((5,)), dma((5,)),
            dma((CH + 5,)),
        ],
        compiler_params=pltpu.CompilerParams(
            collective_id=0, has_side_effects=True, vmem_limit_bytes=62 * 2**20
        ),
        cost_estimate=pl.CostEstimate(flops=20 * 10**9, bytes_accessed=16 * 2**20, transcendentals=8 * 2**20),
    )(queries, audio_keys, audio_values, out_weight, mix_gate.reshape(1, 1), mask_rows, cotangent)
    return pl.pallas_call(
        hand_over,
        out_shape=tuple(jax.ShapeDtypeStruct(r.shape, r.dtype) for r in results),
        in_specs=[vmem] * 5,
        out_specs=[hbm] * 5,
        scratch_shapes=[dma((5,))],
    )(*results)


def solution(mesh):
    in_specs = (
        P("seq", "tp"),
        P("seq", "tp"),
        P("seq", "tp"),
        P("tp", None),
        P(),
        P("seq", None),
        P(("seq", "tp"), None),
    )
    out_specs = (
        P(("seq", "tp"), None),
        P("seq", "tp"),
        P("seq", "tp"),
        P("seq", "tp"),
        P("tp", "seq"),
    )
    return jax.shard_map(
        per_device, mesh=mesh, in_specs=in_specs, out_specs=out_specs, check_vma=False
    )
```

```python
import jax
import jax.numpy as jnp
from jax import lax
from jax.experimental import pallas as pl
from jax.experimental.pallas import tpu as pltpu
from jax.sharding import PartitionSpec as P

HD = 128
BLK = 128
CH = 8
WC = 1024
HALF = 512
TOK = 512
AUD = 2048
SCALE = HD ** (-0.5)
C2 = SCALE * 1.4426950408889634
NEG = -1e30
BF = jnp.bfloat16
F32 = jnp.float32
MESH = pl.DeviceIdType.MESH

NT = (((1,), (1,)), ((), ()))
NN = (((1,), (0,)), ((), ()))
TN = (((0,), (0,)), ((), ()))

AGY, AGP, AGM, AFP, AFM, SIB, GW, F1, F2, R1, R2, YX, YP, YM, YF, P0 = range(16)
KINDS = P0 + 4
GATHER_X = (3, 5)
SCATTER_Y = (1, 3, 5)
TICKS = 51
PLAN = (
    ('HR', (18,), (0,)),
    ('K0', (0,), (0,)),
    ('A', (0, 2, 3, 4, 5, 6, 9, 10), (4, 2, 0, 7, 1, 3, 5, 6)),
    ('GP', (32,), (0,)),
    ('F', (18, 19, 22, 24, 27, 29, 30, 36), (5, 7, 3, 2, 0, 6, 1, 4)),
    ('GH', (29,), (0,)),
    ('B', (0, 1, 7, 8, 9, 10, 11, 15), (3, 5, 4, 2, 7, 0, 1, 6)),
    ('X', (15, 17), (5, 3)),
    ('LC', (32, 36, 40, 41, 42, 43, 44, 45), (5, 7, 0, 2, 1, 6, 3, 4)),
    ('E', (15, 19, 20, 22, 24, 25, 26, 28), (5, 7, 2, 3, 0, 4, 6, 1)),
    ('LB', (30, 31, 32, 33, 36, 37, 38, 39), (5, 2, 7, 0, 3, 6, 1, 4)),
    ('D', (9, 10, 15, 16, 20, 23, 25, 27), (5, 3, 2, 7, 4, 0, 6, 1)),
    ('LA', (18, 22, 23, 25, 28, 29, 31, 36), (5, 7, 3, 2, 0, 6, 1, 4)),
    ('KF', (45, 47), (1, 0)),
    ('KR', (38, 44), (0, 1)),
    ('K1', (6,), (0,)),
    ('DQ', (39,), (0,)),
    ('LD', (43, 44, 45, 46, 47, 48, 49, 50), (5, 0, 1, 6, 7, 2, 4, 3)),
    ('C', (4, 6, 9, 10, 11, 16, 20, 21), (3, 5, 2, 7, 4, 0, 6, 1)),
    ('GF', (50,), (0,)),
    ('FW', (11, 12, 13, 14), (0, 1, 2, 3)),
    ('HX', (14,), (0,)),
    ('L0', (7,), (0,)),
    ('DF', (42,), (0,)),
    ('BW', (31, 33, 34, 35), (0, 1, 2, 3)),
)


def dot(a, b, dims):
    return lax.dot_general(a, b, dims, preferred_element_type=F32)


def kernel(
    q_hbm, k_hbm, v_hbm, w_hbm, gate_ref, mask_ref, cot_hbm,
    layer_hbm, dq_hbm, dk_hbm, dv_hbm, gw_hbm,
    layer_ref, dq_ref, dk_ref, dv_ref, gw_ref,
    w, cot, cot_sib, kvb, q2, mask2, ht, hrow, gh_acc, gh_own, gh2,
    sc, pb, lse, delta, dq_acc, dq_out, dq_in, f1b, f2b, r1b, r2b, ys, yr, p4b, gw_out, gw_in, gw_sum, gw_par, kv_out, kv_in, kv_red, kv_fin,
    ss, rs, ps, pr, zs, zr, ds_, dr, fs, fr, es, er, ls, os_,
):
    s = lax.axis_index("seq")
    t = lax.axis_index("tp")
    core = s % 2
    z = s // 4
    yl = (s // 2) % 2
    x = t // 2
    yh = t % 2
    xn, xb, xf = (x + 1) % 4, (x + 3) % 4, (x + 2) % 4
    sib = (s + 1 - 2 * core, t)
    nxt = (s, xn * 2 + yh)
    prv = (s, xb * 2 + yh)
    par = (s, x * 2 + 1 - yh)

    def zdev(dz):
        return (((z + dz) % 4) * 4 + yl * 2 + core, t)

    def near(n):
        return (z * 4 + ((yl + n // 2) % 2) * 2 + (core + n) % 2, t)

    def rows(start, size):
        return pl.ds(pl.multiple_of(start, size), size)

    def cols(start, size):
        return pl.ds(pl.multiple_of(start, 128), size)

    def chunk(i):
        m = i // 2
        zz = ((z // 2 + m // 2) % 2) * 2 + (z + m) % 2
        return zz * 2 + (yl + i) % 2

    def copy(kind, i, src, dst, dev):
        return pltpu.make_async_remote_copy(
            src_ref=src, dst_ref=dst, send_sem=ss.at[kind, i], recv_sem=rs.at[kind, i],
            device_id=dev, device_id_type=MESH,
        )

    def got(kind, i, dst):
        copy(kind, i, dst, dst, nxt).wait_recv()

    def sent(kind, i, src):
        copy(kind, i, src, src, nxt).wait_send()

    barrier = pltpu.get_barrier_semaphore()
    for dev in (nxt, prv, par):
        pl.semaphore_signal(barrier, inc=1, device_id=dev, device_id_type=MESH)

    for n in range(1, 4):
        pl.semaphore_signal(barrier, inc=1, device_id=near(n), device_id_type=MESH)
        pl.semaphore_signal(barrier, inc=1, device_id=zdev(n), device_id_type=MESH)

    def own_piece(i):
        return pltpu.make_async_copy(
            cot_hbm.at[:, cols(chunk(i) * WC, WC)], cot.at[i, rows(t * 64, 64), :], ls.at[i]
        )

    def start_piece(i, c):
        own_piece(i).start()
        return c

    lax.fori_loop(0, CH, start_piece, 0)
    w_copy = pltpu.make_async_copy(w_hbm, w, ls.at[CH])
    my_heads = cols(core * 256, 256)
    k_copy = pltpu.make_async_copy(k_hbm.at[:, my_heads], kvb.at[rows(s * 128, 128), pl.ds(0, 256)], ls.at[CH + 1])
    v_copy = pltpu.make_async_copy(v_hbm.at[:, my_heads], kvb.at[rows(s * 128, 128), pl.ds(256, 256)], ls.at[CH + 2])
    q_copy = pltpu.make_async_copy(q_hbm.at[:, my_heads], q2.at[rows(core * TOK, TOK), :], ls.at[CH + 3])
    for c in (w_copy, k_copy, v_copy, q_copy):
        c.start()

    pl.semaphore_wait(barrier, 9)

    def out_copy(n, src, dst):
        return pltpu.make_async_copy(src, dst, os_.at[n])

    def layer_copy(i):
        cc = cols(chunk(i) * WC, WC)
        return out_copy(i, layer_ref.at[:, cc], layer_hbm.at[:, cc])

    dq_copy = out_copy(CH, dq_ref, dq_hbm)
    gw_copy = out_copy(CH + 1, gw_ref, gw_hbm)
    dk_copy = out_copy(CH + 2, dk_ref, dk_hbm)
    dv_copy = out_copy(CH + 3, dv_ref, dv_hbm)

    def stage_a(i):
        copy(AGY, i, cot_hbm.at[:, cols(chunk(i) * WC, WC)], cot.at[i, rows(t * 64, 64), :], par).start()

    def piece_x(i):
        src = cot_hbm.at[:, cols(chunk(i) * WC, WC)]
        dst = cot.at[i, rows(t * 64, 64), :]
        copy(AGP, i, src, dst, nxt).start()
        copy(AGM, i, src, dst, prv).start()


    def extra(n, src, dst):
        return pltpu.make_async_remote_copy(
            src_ref=src, dst_ref=dst, send_sem=es.at[n], recv_sem=er.at[n], device_id=sib, device_id_type=MESH
        )

    other_heads = cols((1 - core) * 256, 256)
    q_send = extra(0, q_hbm.at[:, other_heads], q2.at[rows(core * TOK, TOK), :])
    my_mask = mask2.at[:, cols(core * TOK, TOK)]
    m_send = extra(1, my_mask, my_mask)

    def prepare():
        gh_acc[...] = jnp.zeros_like(gh_acc)
        for tb in range(TOK // BLK):
            for ab in range(AUD // BLK):
                seen = jnp.full((1, BLK), mask_ref[tb, ab].astype(F32))
                mask2[pl.ds(ab, 1), cols(core * TOK + tb * BLK, BLK)] = seen
        q_send.start()
        m_send.start()

    def kv_near(n, src_rows):
        heads = cols(((core + n) % 2) * 256, 256)
        return [
            pltpu.make_async_remote_copy(
                src_ref=src.at[:, heads], dst_ref=kvb.at[src_rows, pl.ds(part * 256, 256)],
                send_sem=ps.at[n, part], recv_sem=pr.at[n, part], device_id=near(n), device_id_type=MESH)
            for part, src in enumerate((k_hbm, v_hbm))
        ]

    def kv_far(dz, zz):
        block = kvb.at[rows(zz * 512, 512), :]
        return pltpu.make_async_remote_copy(
            src_ref=block, dst_ref=block, send_sem=zs.at[dz], recv_sem=zr.at[dz],
            device_id=zdev(dz), device_id_type=MESH)

    def kv_share():
        for n in range(1, 4):
            for copy_ in kv_near(n, rows(s * 128, 128)):
                copy_.start()

    def kv_spread():
        k_copy.wait()
        v_copy.wait()
        for n in range(1, 4):
            src = z * 4 + ((yl + n // 2) % 2) * 2 + (core + n) % 2
            for copy_ in kv_near(n, rows(src * 128, 128)):
                copy_.wait_recv()
        for dz in (1, 3, 2):
            kv_far(dz, z).start()

    gate = jnp.tanh(gate_ref[...])

    def stage_b1(i):
        own_piece(i).wait()
        got(AGY, i, cot.at[i, rows((x * 2 + 1 - yh) * 64, 64), :])
        block = cot.at[i, rows(x * 128, 128), :]
        copy(AGP, i, block, block, nxt).start()
        copy(AGM, i, block, block, prv).start()

    def stage_c1(i):
        got(AGP, i, cot.at[i, rows(xb * 128, 128), :])
        top = cot.at[i, rows(xb * 128, 64), :]
        copy(AFP, i, top, top, nxt).start()
        got(AGM, i, cot.at[i, rows(xn * 128, 128), :])
        low = cot.at[i, rows(xn * 128 + 64, 64), :]
        copy(AFM, i, low, low, prv).start()

    def stage_d1(i):
        got(AFP, i, cot.at[i, rows(xf * 128, 64), :])
        got(AFM, i, cot.at[i, rows(xf * 128 + 64, 64), :])
        share(i)

    def share(i):
        copy(SIB, i, cot.at[i, :, cols((1 - core) * HALF, HALF)], cot_sib.at[i], sib).start()

    def to_partner(kind, i, xx):
        block = cot.at[i, rows(xx * 128 + yh * 64, 64), :]
        copy(kind, i, block, block, par).start()

    def stage_c2(i):
        got(AGP, i, cot.at[i, rows(xb * 128 + yh * 64, 64), :])
        top = cot.at[i, rows(xb * 128 + yh * 64, 32), :]
        copy(AFP, i, top, top, nxt).start()
        got(AGM, i, cot.at[i, rows(xn * 128 + yh * 64, 64), :])
        low = cot.at[i, rows(xn * 128 + yh * 64 + 32, 32), :]
        copy(AFM, i, low, low, prv).start()
        to_partner(YP, i, xb)
        to_partner(YM, i, xn)

    def stage_d2(i):
        got(AFP, i, cot.at[i, rows(xf * 128 + yh * 64, 32), :])
        got(AFM, i, cot.at[i, rows(xf * 128 + yh * 64 + 32, 32), :])
        to_partner(YF, i, xf)

    def stage_x2(i):
        own_piece(i).wait()
        for kind, xx in ((AGY, x), (YP, xb), (YM, xn), (YF, xf)):
            got(kind, i, cot.at[i, rows(xx * 128 + (1 - yh) * 64, 64), :])
        share(i)

    def either(first, second, cond):
        def stage(i):
            @pl.when(cond(i))
            def _():
                first(i)

            @pl.when(jnp.logical_not(cond(i)))
            def _():
                second(i)

        return stage

    def member(i, chosen):
        hit = i < 0
        for n in chosen:
            hit = jnp.logical_or(hit, i == n)
        return hit

    def gathers_x(i):
        return member(i, GATHER_X)

    stage_b = either(piece_x, stage_b1, gathers_x)
    stage_c = either(stage_c2, stage_c1, gathers_x)
    stage_d = either(stage_d2, stage_d1, gathers_x)

    def gather_sent(i):
        @pl.when(gathers_x(i))
        def _():
            for kind in (AGP, AGM, YP, YM, YF):
                sent(kind, i, cot.at[i, rows(x * 128, 64), :])
            for kind in (AFP, AFM):
                sent(kind, i, cot.at[i, rows(x * 128, 32), :])

        @pl.when(jnp.logical_not(gathers_x(i)))
        def _():
            for kind in (AGP, AGM):
                sent(kind, i, cot.at[i, rows(x * 128, 128), :])
            for kind in (AFP, AFM):
                sent(kind, i, cot.at[i, rows(x * 128, 64), :])

    def stage_e(i):
        cc = cols(chunk(i) * WC, WC)
        for part in range(2):
            rr = pl.ds(part * 256, 256)
            gh_acc[rr, :] += dot(w[rr, cc], cot[i], NT)

    def stage_f(i):
        got(SIB, i, cot_sib.at[i])
        mine = cols(core * TOK, TOK)
        theirs = cols((1 - core) * TOK, TOK)
        for part in range(2):
            rr = pl.ds(part * 256, 256)
            val = dot(ht[rr, mine], cot[i, :, cols(core * HALF, HALF)], NN) + dot(ht[rr, theirs], cot_sib[i], NN)
            gw_out[i, rr, :] = val.astype(BF)

        @pl.when(i > 1)
        def _():
            zz = chunk(i) // 2
            copy(GW, i, gw_out.at[i], gw_in.at[i - 2], (zz * 4 + yl * 2 + core, t)).start()

    def product(i):
        gather_sent(i)
        sent(SIB, i, cot_sib.at[i])
        for part in range(2):
            cc = cols(chunk(i) * WC + part * HALF, HALF)
            cot[i, :, pl.ds(part * HALF, HALF)] = dot(hrow[...], w[:, cc], NN).astype(BF)

    def stage_la1(i):
        product(i)
        copy(F1, i, cot.at[i, rows(xf * 128, 64), :], f1b.at[i], nxt).start()
        copy(F2, i, cot.at[i, rows(xf * 128 + 64, 64), :], f2b.at[i], prv).start()

    def stage_lb1(i):
        got(F1, i, f1b.at[i])
        rr = rows(xn * 128, 64)
        cot[i, rr, :] = (cot[i, rr, :].astype(F32) + f1b[i].astype(F32)).astype(BF)
        copy(R1, i, cot.at[i, rows(xn * 128, 128), :], r1b.at[i], nxt).start()
        got(F2, i, f2b.at[i])
        rr = rows(xb * 128 + 64, 64)
        cot[i, rr, :] = (cot[i, rr, :].astype(F32) + f2b[i].astype(F32)).astype(BF)
        copy(R2, i, cot.at[i, rows(xb * 128, 128), :], r2b.at[i], prv).start()

    def reduced(i, which):
        rr = rows(which * 64, 64)
        return (
            cot[i, rows(x * 128 + which * 64, 64), :].astype(F32)
            + r1b[i, rr, :].astype(F32)
            + r2b[i, rr, :].astype(F32)
        )

    def stage_lc1(i):
        got(R1, i, r1b.at[i])
        got(R2, i, r2b.at[i])
        ys[i] = reduced(i, 1 - yh).astype(BF)
        copy(YX, i, ys.at[i], yr.at[i], par).start()

    def stage_ld1(i):
        got(YX, i, yr.at[i])
        total = reduced(i, yh) + yr[i].astype(F32)
        layer_ref[:, cols(chunk(i) * WC, WC)] = (gate * total).astype(BF)
        layer_copy(i).start()

    def slot(i):
        return sum((i > n).astype(jnp.int32) for n in SCATTER_Y)

    def stage_la2(i):
        product(i)
        for n in range(4):
            copy(P0 + n, i, cot.at[i, rows(n * 128 + (1 - yh) * 64, 64), :], p4b.at[slot(i), n], par).start()

    def add_partner(i, xx):
        rr = rows(xx * 128 + yh * 64, 64)
        return cot[i, rr, :].astype(F32) + p4b[slot(i), xx].astype(F32)

    def stage_lb2(i):
        for n in range(4):
            got(P0 + n, i, p4b.at[slot(i), n])
        rr = rows(xf * 128 + yh * 64, 64)
        cot[i, rr, :] = add_partner(i, xf).astype(BF)
        copy(F1, i, cot.at[i, rows(xf * 128 + yh * 64, 32), :], f1b.at[i, pl.ds(0, 32), :], nxt).start()
        copy(F2, i, cot.at[i, rows(xf * 128 + yh * 64 + 32, 32), :], f2b.at[i, pl.ds(0, 32), :], prv).start()

    def stage_lc2(i):
        top, low = pl.ds(0, 32), pl.ds(0, 64)
        got(F1, i, f1b.at[i, top, :])
        val = add_partner(i, xn)
        cot[i, rows(xn * 128 + yh * 64, 32), :] = (val[:32] + f1b[i, top, :].astype(F32)).astype(BF)
        cot[i, rows(xn * 128 + yh * 64 + 32, 32), :] = val[32:].astype(BF)
        copy(R1, i, cot.at[i, rows(xn * 128 + yh * 64, 64), :], r1b.at[i, low, :], nxt).start()
        got(F2, i, f2b.at[i, top, :])
        val = add_partner(i, xb)
        cot[i, rows(xb * 128 + yh * 64, 32), :] = val[:32].astype(BF)
        cot[i, rows(xb * 128 + yh * 64 + 32, 32), :] = (val[32:] + f2b[i, top, :].astype(F32)).astype(BF)
        copy(R2, i, cot.at[i, rows(xb * 128 + yh * 64, 64), :], r2b.at[i, low, :], prv).start()

    def stage_ld2(i):
        low = pl.ds(0, 64)
        got(R1, i, r1b.at[i, low, :])
        got(R2, i, r2b.at[i, low, :])
        total = add_partner(i, x) + r1b[i, low, :].astype(F32) + r2b[i, low, :].astype(F32)
        layer_ref[:, cols(chunk(i) * WC, WC)] = (gate * total).astype(BF)
        layer_copy(i).start()

    def chunk_sent(i):
        sent(AGY, i, cot.at[i, rows(x * 128, 64), :])

        @pl.when(scatters_y(i))
        def _():
            for n in range(4):
                sent(P0 + n, i, p4b.at[slot(i), n])
            for kind in (F1, F2):
                sent(kind, i, cot.at[i, rows(x * 128, 32), :])
            for kind in (R1, R2):
                sent(kind, i, cot.at[i, rows(x * 128, 64), :])

        @pl.when(jnp.logical_not(scatters_y(i)))
        def _():
            sent(F1, i, f1b.at[i])
            sent(F2, i, f2b.at[i])
            sent(R1, i, r1b.at[i])
            sent(R2, i, r2b.at[i])
            sent(YX, i, ys.at[i])

    def scatters_y(i):
        return member(i, SCATTER_Y)

    stage_la = either(stage_la2, stage_la1, scatters_y)
    stage_lb = either(stage_lb2, stage_lb1, scatters_y)
    stage_lc = either(stage_lc2, stage_lc1, scatters_y)
    stage_ld_ = either(stage_ld2, stage_ld1, scatters_y)

    def stage_ld(i):
        stage_ld_(i)
        chunk_sent(i)

    def masked(score, row, tok):
        return jnp.where(mask2[pl.ds(row, 1), tok] > 0, score, NEG)

    def forward(j):
        hh, u = j // 2, j % 2
        hc = cols(hh * HD, HD)
        vc = cols(256 + hh * HD, HD)
        tok = cols(u * TOK, TOK)
        qv = q2[rows(u * TOK, TOK), hc]

        def scores(ab, best):
            part = dot(kvb[rows(ab * 256, 256), hc], qv, NT)
            for b in range(2):
                val = masked(part[b * 128 : (b + 1) * 128], ab * 2 + b, tok)
                sc[rows(ab * 256 + b * 128, 128), :] = val
                best = jnp.maximum(best, jnp.max(val, axis=0, keepdims=True))
            return best

        best = lax.fori_loop(0, AUD // 256, scores, jnp.full((1, TOK), NEG, F32))

        def weigh(ab, total):
            rr = rows(ab * 256, 256)
            val = jnp.exp2((sc[rr, :] - best) * C2)
            pb[rr, :] = val.astype(BF)
            return total + jnp.sum(val, axis=0, keepdims=True)

        total = lax.fori_loop(0, AUD // 256, weigh, jnp.zeros((1, TOK), F32))
        out = dot(kvb[:, vc], pb[...], TN)
        ht[rows(core * 256 + hh * HD, HD), tok] = (out / total).astype(BF)
        lse[hh, :, tok] = best * C2 + jnp.log2(total)

    def kv_z(hh, dz):
        return pltpu.make_async_remote_copy(
            src_ref=kv_out.at[hh, rows(((z + dz) % 4) * 512, 512), :], dst_ref=kv_in.at[hh, dz - 1],
            send_sem=ds_.at[hh, dz], recv_sem=dr.at[hh, dz], device_id=zdev(dz), device_id_type=MESH)

    def kv_y(hh, n):
        src = ((yl + n // 2) % 2) * 2 + (core + n) % 2
        return pltpu.make_async_remote_copy(
            src_ref=kv_red.at[hh, src], dst_ref=kv_fin.at[hh, n],
            send_sem=fs.at[hh, n], recv_sem=fr.at[hh, n], device_id=near(n), device_id_type=MESH)

    def kv_reduce(hh):
        for dz in range(1, 4):
            kv_z(hh, dz).wait_recv()
        for b in range(4):
            total = kv_out[hh, rows(z * 512 + b * 128, 128), :].astype(F32)
            for dz in range(3):
                total += kv_in[hh, dz, b * 128 : (b + 1) * 128, :].astype(F32)
            kv_red[hh, b] = total.astype(BF)
        for n in range(1, 4):
            kv_y(hh, n).start()
        for dz in range(1, 4):
            kv_z(hh, dz).wait_send()

    kv_last = [idx for name, _, idx in PLAN if name == "KF"][0][-1]

    def kv_finish(hh):
        for n in range(1, 4):
            kv_y(hh, n).wait_recv()
        same = kv_red[hh, yl * 2 + core].astype(F32) + kv_fin[hh, 2].astype(F32)
        other = kv_fin[hh, 1].astype(F32) + kv_fin[hh, 3].astype(F32)
        hc = cols(core * 256 + hh * HD, HD)
        dk_ref[:, hc] = same[:, :HD].astype(BF)
        dv_ref[:, hc] = same[:, HD:].astype(BF)
        hc = cols((1 - core) * 256 + hh * HD, HD)
        dk_ref[:, hc] = other[:, :HD].astype(BF)
        dv_ref[:, hc] = other[:, HD:].astype(BF)
        for n in range(1, 4):
            kv_y(hh, n).wait_send()

        @pl.when(hh == kv_last)
        def _():
            dk_copy.start()
            dv_copy.start()

    gw_send = pltpu.make_async_remote_copy(
        src_ref=gw_sum, dst_ref=gw_par, send_sem=fs.at[0, 0], recv_sem=fr.at[0, 0],
        device_id=near(2), device_id_type=MESH)

    def gw_reduce(which, write):
        def got_one(i, c):
            got(GW, 2 * i + which, gw_in.at[2 * i + which - 2])
            return c

        lax.fori_loop(1, 4, got_one, 0)

        def add(b, c):
            rr = rows(b * 64, 64)
            total = gw_out[which, rr, :].astype(F32)
            for i in range(3):
                total += gw_in[2 * i + which, rr, :].astype(F32)
            write(rr, total)
            return c

        lax.fori_loop(0, 8, add, 0)

    def gw_part():
        def write(rr, total):
            gw_sum[rr, :] = total.astype(BF)

        gw_reduce(1, write)
        gw_send.start()

    def gw_finish():
        gw_send.wait_recv()

        def write(rr, total):
            gw_ref[rr, :] = (gate * (total + gw_par[rr, :].astype(F32))).astype(BF)

        gw_reduce(0, write)
        gw_copy.start()
        gw_send.wait_send()

        def gw_left(i, c):
            sent(GW, i, gw_out.at[i])
            return c

        lax.fori_loop(2, CH, gw_left, 0)

    def backward(j):
        hh = j // 2
        ah = (j + 1 + z // 2) % 2
        hc = cols(hh * HD, HD)
        hr = rows(hh * HD, HD)
        first = j % 2 == 0

        @pl.when(first)
        def _():
            dq_acc[...] = jnp.zeros_like(dq_acc)
            own = ht[rows(core * 256 + hh * HD, HD), :].astype(F32)
            delta[...] = jnp.sum(gh2[hr, :].astype(F32) * own, axis=0, keepdims=True)

        def step(b, c):
            rr = rows(ah * 1024 + b * 256, 256)
            kk = kvb[rr, hc]
            vv = kvb[rr, cols(256 + hh * HD, HD)]
            qv = q2[:, hc]
            gv = gh2[hr, :]
            score = dot(kk, qv, NT)
            logs = lse[hh]
            probs = []
            for m in range(2):
                row = ah * 8 + b * 2 + m
                val = masked(score[m * 128 : (m + 1) * 128], row, slice(None))
                probs.append(jnp.exp2(val * C2 - logs))
            prob = jnp.concatenate(probs, axis=0)
            dp = dot(vv, gv, NN)
            dsc = (prob * (dp - delta[...])).astype(BF)
            kv_out[hh, rr, pl.ds(HD, HD)] = dot(prob.astype(BF), gv, NT).astype(BF)
            kv_out[hh, rr, pl.ds(0, HD)] = (SCALE * dot(dsc, qv, NN)).astype(BF)
            dq_acc[...] += dot(kk, dsc, TN)
            return c

        lax.fori_loop(0, 4, step, 0)

        for b in range(2):
            dz = (ah * 2 + b - z + 4) % 4

            @pl.when(dz > 0)
            def _():
                kv_z(hh, dz).start()

        @pl.when(j % 2 == 1)
        def _():
            full = SCALE * dq_acc[...]
            for u in range(2):
                piece = full[:, u * TOK : (u + 1) * TOK].T.astype(BF)

                @pl.when(core == u)
                def _():
                    dq_ref[:, cols(core * 256 + hh * HD, HD)] = piece

                @pl.when(core != u)
                def _():
                    dq_out[:, hc] = piece

    mine_rows = rows(core * 256, 256)
    ht_send = extra(2, ht.at[mine_rows, :], ht.at[mine_rows, :])
    their_rows = rows((1 - core) * 256, 256)
    gh_send = extra(3, gh_own.at[their_rows, :], gh2.at[:, cols(core * TOK, TOK)])
    dq_send = extra(4, dq_out, dq_in)

    def heads_first():
        q_copy.wait()
        other_q = q2.at[rows((1 - core) * TOK, TOK), :]
        extra(0, other_q, other_q).wait_recv()
        other_m = mask2.at[:, cols((1 - core) * TOK, TOK)]
        extra(1, other_m, other_m).wait_recv()
        for dz in range(1, 4):
            kv_far(dz, (z - dz + 4) % 4).wait_recv()

    def on_first(i, fn):
        @pl.when(i == 0)
        def _():
            fn()

    def stage_fw(j):
        on_first(j, heads_first)
        forward(j)

    def gh_got():
        other = gh2.at[:, cols((1 - core) * TOK, TOK)]
        extra(3, other, other).wait_recv()

    def stage_bw(j):
        on_first(j, gh_got)
        backward(j)

    def stage_hr():
        extra(2, ht.at[their_rows, :], ht.at[their_rows, :]).wait_recv()
        hrow[...] = ht[:, cols(core * TOK, TOK)].astype(F32).T.astype(BF)
        q_send.wait_send()
        m_send.wait_send()
        ht_send.wait_send()
        for n in range(1, 4):
            for copy_ in kv_near(n, rows(s * 128, 128)):
                copy_.wait_send()
            kv_far(n, z).wait_send()

    def stage_gh():
        gh_own[...] = (gate * gh_acc[...]).astype(BF)
        gh2[:, cols(core * TOK, TOK)] = gh_own[mine_rows, :]
        gh_send.start()

    def stage_df():
        dq_send.wait_recv()
        dq_ref[:, cols((1 - core) * 256, 256)] = dq_in[...]
        dq_copy.start()
        dq_send.wait_send()
        gh_send.wait_send()

    once = {
        "L0": prepare, "K0": kv_share, "K1": kv_spread, "HX": ht_send.start, "HR": stage_hr, "GH": stage_gh,
        "GP": gw_part, "GF": gw_finish, "DQ": dq_send.start, "DF": stage_df,
    }
    each = {
        "A": stage_a, "B": stage_b, "C": stage_c, "D": stage_d, "X": stage_x2, "E": stage_e, "F": stage_f,
        "LA": stage_la, "LB": stage_lb, "LC": stage_lc, "LD": stage_ld,
        "FW": stage_fw, "BW": stage_bw, "KR": kv_reduce, "KF": kv_finish,
    }
    w_tick = min(ticks[0] for name, ticks, _ in PLAN if name == "E")

    def packed(ticks, low):
        return jnp.int32(sum(1 << (n - low) for n in ticks if low <= n < low + 30))

    def tick(g, state):
        after = []
        for (name, ticks, idx), (bits, order) in zip(PLAN, state):
            for low in range(30, TICKS, 30):
                bits = jnp.where(g == low, packed(ticks, low), bits)
            hit = bits % 2 == 1
            if name == "E":

                @pl.when(g == w_tick)
                def _():
                    w_copy.wait()

            @pl.when(hit)
            def _():
                if name in once:
                    once[name]()
                else:
                    each[name](order % 8)

            after.append((bits // 2, jnp.where(hit, order // 8, order)))
        return tuple(after)

    start = tuple(
        (packed(ticks, 0), jnp.int32(sum(i << (3 * n) for n, i in enumerate(idx)))) for _, ticks, idx in PLAN
    )
    lax.fori_loop(0, TICKS, tick, start)

    def written(i, c):
        layer_copy(i).wait()
        return c

    lax.fori_loop(0, CH, written, 0)
    for c in (dq_copy, gw_copy, dk_copy, dv_copy):
        c.wait()


def hand_over(*refs):
    given, results, held, sems = refs[:5], refs[5:10], refs[10:15], refs[15]
    ins = [pltpu.make_async_copy(given[n], held[n], sems.at[0, n]) for n in range(5)]
    outs = [pltpu.make_async_copy(held[n], results[n], sems.at[1, n]) for n in range(5)]
    for c in ins:
        c.start()
    for c, d in zip(ins, outs):
        c.wait()
        d.start()
    for d in outs:
        d.wait()


def per_device(queries, audio_keys, audio_values, out_weight, mix_gate, block_mask, cotangent):
    hbm = pl.BlockSpec(memory_space=pl.ANY)
    vmem = pl.BlockSpec(memory_space=pltpu.VMEM)
    dma = pltpu.SemaphoreType.DMA
    results = pl.pallas_call(
        kernel,
        out_shape=(
            jax.ShapeDtypeStruct((64, 8192), BF),
            jax.ShapeDtypeStruct((TOK, 512), BF),
            jax.ShapeDtypeStruct((128, 512), BF),
            jax.ShapeDtypeStruct((128, 512), BF),
            jax.ShapeDtypeStruct((512, 512), BF),
        ),
        in_specs=[hbm, hbm, hbm, hbm, vmem, pl.BlockSpec(memory_space=pltpu.SMEM), hbm],
        out_specs=[hbm] * 5,
        scratch_shapes=[
            pltpu.VMEM((64, 8192), BF),
            pltpu.VMEM((TOK, 512), BF),
            pltpu.VMEM((128, 512), BF),
            pltpu.VMEM((128, 512), BF),
            pltpu.VMEM((512, 512), BF),
            pltpu.VMEM((512, 8192), BF),
            pltpu.VMEM((CH, TOK, WC), BF),
            pltpu.VMEM((CH, TOK, HALF), BF),
            pltpu.VMEM((AUD, 512), BF),
            pltpu.VMEM((2 * TOK, 256), BF),
            pltpu.VMEM((16, 2 * TOK), F32),
            pltpu.VMEM((512, 2 * TOK), BF),
            pltpu.VMEM((TOK, 512), BF),
            pltpu.VMEM((512, TOK), F32),
            pltpu.VMEM((512, TOK), BF),
            pltpu.VMEM((256, 2 * TOK), BF),
            pltpu.VMEM((AUD, TOK), F32),
            pltpu.VMEM((AUD, TOK), BF),
            pltpu.VMEM((2, 1, 2 * TOK), F32),
            pltpu.VMEM((1, 2 * TOK), F32),
            pltpu.VMEM((HD, 2 * TOK), F32),
            pltpu.VMEM((TOK, 256), BF),
            pltpu.VMEM((TOK, 256), BF),
            pltpu.VMEM((CH, 64, WC), BF),
            pltpu.VMEM((CH, 64, WC), BF),
            pltpu.VMEM((CH, 128, WC), BF),
            pltpu.VMEM((CH, 128, WC), BF),
            pltpu.VMEM((CH, 64, WC), BF),
            pltpu.VMEM((CH, 64, WC), BF),
            pltpu.VMEM((3, 4, 64, WC), BF),
            pltpu.VMEM((CH, 512, HALF), BF),
            pltpu.VMEM((CH - 2, 512, HALF), BF),
            pltpu.VMEM((512, HALF), BF),
            pltpu.VMEM((512, HALF), BF),
            pltpu.VMEM((2, AUD, 256), BF),
            pltpu.VMEM((2, 3, 512, 256), BF),
            pltpu.VMEM((2, 4, 128, 256), BF),
            pltpu.VMEM((2, 4, 128, 256), BF),
            dma((KINDS, CH)), dma((KINDS, CH)),
            dma((4, 2)), dma((4, 2)),
            dma((4,)), dma((4,)),
            dma((2, 4)), dma((2, 4)),
            dma((2, 4)), dma((2, 4)),
            dma((5,)), dma((5,)),
            dma((CH + 4,)),
            dma((CH + 4,)),
        ],
        compiler_params=pltpu.CompilerParams(
            collective_id=0, has_side_effects=True, vmem_limit_bytes=62 * 2**20
        ),
        cost_estimate=pl.CostEstimate(flops=20 * 10**9, bytes_accessed=16 * 2**20, transcendentals=8 * 2**20),
    )(queries, audio_keys, audio_values, out_weight, mix_gate.reshape(1, 1), block_mask, cotangent)
    return pl.pallas_call(
        hand_over,
        out_shape=tuple(jax.ShapeDtypeStruct(r.shape, r.dtype) for r in results),
        in_specs=[hbm] * 5,
        out_specs=[hbm] * 5,
        scratch_shapes=[pltpu.VMEM(r.shape, r.dtype) for r in results] + [dma((2, 5))],
    )(*results)


def solution(mesh):
    in_specs = (
        P("seq", "tp"),
        P("seq", "tp"),
        P("seq", "tp"),
        P("tp", None),
        P(),
        P("seq", None),
        P(("seq", "tp"), None),
    )
    out_specs = (
        P(("seq", "tp"), None),
        P("seq", "tp"),
        P("seq", "tp"),
        P("seq", "tp"),
        P("tp", "seq"),
    )
    return jax.shard_map(
        per_device, mesh=mesh, in_specs=in_specs, out_specs=out_specs, check_vma=False
    )
```

```python
import jax
import jax.numpy as jnp
from jax import lax
from jax.experimental import pallas as pl
from jax.experimental.pallas import tpu as pltpu
from jax.sharding import PartitionSpec as P

HD = 128
BLK = 128
CH = 8
WC = 1024
HALF = 512
TOK = 512
AUD = 2048
SCALE = HD ** (-0.5)
C2 = SCALE * 1.4426950408889634
NEG = -1e30
BF = jnp.bfloat16
F32 = jnp.float32
MESH = pl.DeviceIdType.MESH

NT = (((1,), (1,)), ((), ()))
NN = (((1,), (0,)), ((), ()))
TN = (((0,), (0,)), ((), ()))

AGY, AGP, AGM, AFP, AFM, SIB, GW, F1, F2, R1, R2, YX, YP, YM, YF, P0 = range(16)
KINDS = P0 + 4
GATHER_X = (3, 5)
SCATTER_Y = (1, 3, 5)
TICKS = 51
PLAN = (
    ('HR', (18,), (0,)),
    ('K0', (0,), (0,)),
    ('A', (0, 2, 3, 4, 5, 6, 9, 10), (4, 2, 0, 7, 1, 3, 5, 6)),
    ('GP', (32,), (0,)),
    ('F', (18, 19, 22, 24, 27, 29, 30, 36), (5, 7, 3, 2, 0, 6, 1, 4)),
    ('GH', (29,), (0,)),
    ('B', (0, 1, 7, 8, 9, 10, 11, 15), (3, 5, 4, 2, 7, 0, 1, 6)),
    ('X', (15, 17), (5, 3)),
    ('LC', (32, 36, 40, 41, 42, 43, 44, 45), (5, 7, 0, 2, 1, 6, 3, 4)),
    ('E', (15, 19, 20, 22, 24, 25, 26, 28), (5, 7, 2, 3, 0, 4, 6, 1)),
    ('LB', (30, 31, 32, 33, 36, 37, 38, 39), (5, 2, 7, 0, 3, 6, 1, 4)),
    ('D', (9, 10, 15, 16, 20, 23, 25, 27), (5, 3, 2, 7, 4, 0, 6, 1)),
    ('LA', (18, 22, 23, 25, 28, 29, 31, 36), (5, 7, 3, 2, 0, 6, 1, 4)),
    ('KF', (45, 47), (1, 0)),
    ('KR', (38, 44), (0, 1)),
    ('K1', (6,), (0,)),
    ('DQ', (39,), (0,)),
    ('LD', (43, 44, 45, 46, 47, 48, 49, 50), (5, 0, 1, 6, 7, 2, 4, 3)),
    ('C', (4, 6, 9, 10, 11, 16, 20, 21), (3, 5, 2, 7, 4, 0, 6, 1)),
    ('GF', (50,), (0,)),
    ('FW', (11, 12, 13, 14), (0, 1, 2, 3)),
    ('HX', (14,), (0,)),
    ('L0', (7,), (0,)),
    ('DF', (42,), (0,)),
    ('BW', (31, 33, 34, 35), (0, 1, 2, 3)),
)


def dot(a, b, dims):
    return lax.dot_general(a, b, dims, preferred_element_type=F32)


def kernel(
    q_hbm, k_hbm, v_hbm, w_hbm, gate_ref, mask_ref, cot_hbm,
    layer_ref, dq_ref, dk_ref, dv_ref, gw_ref,
    w, cot, cot_sib, kvb, q2, mask2, ht, hrow, gh_acc, gh_own, gh2,
    sc, pb, lse, delta, dq_acc, dq_out, dq_in, f1b, f2b, r1b, r2b, yr, p4b, gw_out, gw_in, gw_par, kv_out, kv_in, kv_fin,
    ss, rs, ps, pr, zs, zr, ds_, dr, fs, fr, es, er, ls,
):
    s = lax.axis_index("seq")
    t = lax.axis_index("tp")
    core = s % 2
    z = s // 4
    yl = (s // 2) % 2
    x = t // 2
    yh = t % 2
    xn, xb, xf = (x + 1) % 4, (x + 3) % 4, (x + 2) % 4
    sib = (s + 1 - 2 * core, t)
    nxt = (s, xn * 2 + yh)
    prv = (s, xb * 2 + yh)
    par = (s, x * 2 + 1 - yh)

    def zdev(dz):
        return (((z + dz) % 4) * 4 + yl * 2 + core, t)

    def near(n):
        return (z * 4 + ((yl + n // 2) % 2) * 2 + (core + n) % 2, t)

    def rows(start, size):
        return pl.ds(pl.multiple_of(start, size), size)

    def cols(start, size):
        return pl.ds(pl.multiple_of(start, 128), size)

    def chunk(i):
        m = i // 2
        zz = ((z // 2 + m // 2) % 2) * 2 + (z + m) % 2
        return zz * 2 + (yl + i) % 2

    def copy(kind, i, src, dst, dev):
        return pltpu.make_async_remote_copy(
            src_ref=src, dst_ref=dst, send_sem=ss.at[kind, i], recv_sem=rs.at[kind, i],
            device_id=dev, device_id_type=MESH,
        )

    def got(kind, i, dst):
        copy(kind, i, dst, dst, nxt).wait_recv()

    def sent(kind, i, src):
        copy(kind, i, src, src, nxt).wait_send()

    barrier = pltpu.get_barrier_semaphore()
    for dev in (nxt, prv, par):
        pl.semaphore_signal(barrier, inc=1, device_id=dev, device_id_type=MESH)

    for n in range(1, 4):
        pl.semaphore_signal(barrier, inc=1, device_id=near(n), device_id_type=MESH)
        pl.semaphore_signal(barrier, inc=1, device_id=zdev(n), device_id_type=MESH)

    def own_piece(i):
        return pltpu.make_async_copy(
            cot_hbm.at[:, cols(chunk(i) * WC, WC)], cot.at[i, rows(t * 64, 64), :], ls.at[i]
        )

    def start_piece(i, c):
        own_piece(i).start()
        return c

    lax.fori_loop(0, CH, start_piece, 0)
    w_copy = pltpu.make_async_copy(w_hbm, w, ls.at[CH])
    my_heads = cols(core * 256, 256)
    k_copy = pltpu.make_async_copy(k_hbm.at[:, my_heads], kvb.at[rows(s * 128, 128), pl.ds(0, 256)], ls.at[CH + 1])
    v_copy = pltpu.make_async_copy(v_hbm.at[:, my_heads], kvb.at[rows(s * 128, 128), pl.ds(256, 256)], ls.at[CH + 2])
    q_copy = pltpu.make_async_copy(q_hbm.at[:, my_heads], q2.at[rows(core * TOK, TOK), :], ls.at[CH + 3])
    for c in (w_copy, k_copy, v_copy, q_copy):
        c.start()

    pl.semaphore_wait(barrier, 9)

    def stage_a(i):
        copy(AGY, i, cot_hbm.at[:, cols(chunk(i) * WC, WC)], cot.at[i, rows(t * 64, 64), :], par).start()

    def piece_x(i):
        src = cot_hbm.at[:, cols(chunk(i) * WC, WC)]
        dst = cot.at[i, rows(t * 64, 64), :]
        copy(AGP, i, src, dst, nxt).start()
        copy(AGM, i, src, dst, prv).start()


    def extra(n, src, dst):
        return pltpu.make_async_remote_copy(
            src_ref=src, dst_ref=dst, send_sem=es.at[n], recv_sem=er.at[n], device_id=sib, device_id_type=MESH
        )

    other_heads = cols((1 - core) * 256, 256)
    q_send = extra(0, q_hbm.at[:, other_heads], q2.at[rows(core * TOK, TOK), :])
    my_mask = mask2.at[:, cols(core * TOK, TOK)]
    m_send = extra(1, my_mask, my_mask)

    def prepare():
        gh_acc[...] = jnp.zeros_like(gh_acc)
        for tb in range(TOK // BLK):
            for ab in range(AUD // BLK):
                seen = jnp.full((1, BLK), mask_ref[tb, ab].astype(F32))
                mask2[pl.ds(ab, 1), cols(core * TOK + tb * BLK, BLK)] = seen
        q_send.start()
        m_send.start()

    def kv_near(n, src_rows):
        heads = cols(((core + n) % 2) * 256, 256)
        return [
            pltpu.make_async_remote_copy(
                src_ref=src.at[:, heads], dst_ref=kvb.at[src_rows, pl.ds(part * 256, 256)],
                send_sem=ps.at[n, part], recv_sem=pr.at[n, part], device_id=near(n), device_id_type=MESH)
            for part, src in enumerate((k_hbm, v_hbm))
        ]

    def kv_far(dz, zz):
        block = kvb.at[rows(zz * 512, 512), :]
        return pltpu.make_async_remote_copy(
            src_ref=block, dst_ref=block, send_sem=zs.at[dz], recv_sem=zr.at[dz],
            device_id=zdev(dz), device_id_type=MESH)

    def kv_share():
        for n in range(1, 4):
            for copy_ in kv_near(n, rows(s * 128, 128)):
                copy_.start()

    def kv_spread():
        k_copy.wait()
        v_copy.wait()
        for n in range(1, 4):
            src = z * 4 + ((yl + n // 2) % 2) * 2 + (core + n) % 2
            for copy_ in kv_near(n, rows(src * 128, 128)):
                copy_.wait_recv()
        for dz in (1, 3, 2):
            kv_far(dz, z).start()

    gate = jnp.tanh(gate_ref[...])

    def stage_b1(i):
        own_piece(i).wait()
        got(AGY, i, cot.at[i, rows((x * 2 + 1 - yh) * 64, 64), :])
        block = cot.at[i, rows(x * 128, 128), :]
        copy(AGP, i, block, block, nxt).start()
        copy(AGM, i, block, block, prv).start()

    def stage_c1(i):
        got(AGP, i, cot.at[i, rows(xb * 128, 128), :])
        top = cot.at[i, rows(xb * 128, 64), :]
        copy(AFP, i, top, top, nxt).start()
        got(AGM, i, cot.at[i, rows(xn * 128, 128), :])
        low = cot.at[i, rows(xn * 128 + 64, 64), :]
        copy(AFM, i, low, low, prv).start()

    def stage_d1(i):
        got(AFP, i, cot.at[i, rows(xf * 128, 64), :])
        got(AFM, i, cot.at[i, rows(xf * 128 + 64, 64), :])
        share(i)

    def share(i):
        copy(SIB, i, cot.at[i, :, cols((1 - core) * HALF, HALF)], cot_sib.at[i], sib).start()

    def to_partner(kind, i, xx):
        block = cot.at[i, rows(xx * 128 + yh * 64, 64), :]
        copy(kind, i, block, block, par).start()

    def stage_c2(i):
        got(AGP, i, cot.at[i, rows(xb * 128 + yh * 64, 64), :])
        top = cot.at[i, rows(xb * 128 + yh * 64, 32), :]
        copy(AFP, i, top, top, nxt).start()
        got(AGM, i, cot.at[i, rows(xn * 128 + yh * 64, 64), :])
        low = cot.at[i, rows(xn * 128 + yh * 64 + 32, 32), :]
        copy(AFM, i, low, low, prv).start()
        to_partner(YP, i, xb)
        to_partner(YM, i, xn)

    def stage_d2(i):
        got(AFP, i, cot.at[i, rows(xf * 128 + yh * 64, 32), :])
        got(AFM, i, cot.at[i, rows(xf * 128 + yh * 64 + 32, 32), :])
        to_partner(YF, i, xf)

    def stage_x2(i):
        own_piece(i).wait()
        for kind, xx in ((AGY, x), (YP, xb), (YM, xn), (YF, xf)):
            got(kind, i, cot.at[i, rows(xx * 128 + (1 - yh) * 64, 64), :])
        share(i)

    def either(first, second, cond):
        def stage(i):
            @pl.when(cond(i))
            def _():
                first(i)

            @pl.when(jnp.logical_not(cond(i)))
            def _():
                second(i)

        return stage

    def member(i, chosen):
        hit = i < 0
        for n in chosen:
            hit = jnp.logical_or(hit, i == n)
        return hit

    def gathers_x(i):
        return member(i, GATHER_X)

    stage_b = either(piece_x, stage_b1, gathers_x)
    stage_c = either(stage_c2, stage_c1, gathers_x)
    stage_d = either(stage_d2, stage_d1, gathers_x)

    def gather_sent(i):
        @pl.when(gathers_x(i))
        def _():
            for kind in (AGP, AGM, YP, YM, YF):
                sent(kind, i, cot.at[i, rows(x * 128, 64), :])
            for kind in (AFP, AFM):
                sent(kind, i, cot.at[i, rows(x * 128, 32), :])

        @pl.when(jnp.logical_not(gathers_x(i)))
        def _():
            for kind in (AGP, AGM):
                sent(kind, i, cot.at[i, rows(x * 128, 128), :])
            for kind in (AFP, AFM):
                sent(kind, i, cot.at[i, rows(x * 128, 64), :])

    def stage_e(i):
        cc = cols(chunk(i) * WC, WC)
        for part in range(2):
            rr = pl.ds(part * 256, 256)
            gh_acc[rr, :] += dot(w[rr, cc], cot[i], NT)

    def stage_f(i):
        got(SIB, i, cot_sib.at[i])
        mine = cols(core * TOK, TOK)
        theirs = cols((1 - core) * TOK, TOK)
        for part in range(2):
            rr = pl.ds(part * 256, 256)
            val = dot(ht[rr, mine], cot[i, :, cols(core * HALF, HALF)], NN) + dot(ht[rr, theirs], cot_sib[i], NN)
            gw_out[i, rr, :] = val.astype(BF)

        @pl.when(i > 1)
        def _():
            zz = chunk(i) // 2
            copy(GW, i, gw_out.at[i], gw_in.at[i - 2], (zz * 4 + yl * 2 + core, t)).start()

    def product(i):
        gather_sent(i)
        sent(SIB, i, cot_sib.at[i])
        for part in range(2):
            cc = cols(chunk(i) * WC + part * HALF, HALF)
            cot[i, :, pl.ds(part * HALF, HALF)] = dot(hrow[...], w[:, cc], NN).astype(BF)

    def stage_la1(i):
        product(i)
        copy(F1, i, cot.at[i, rows(xf * 128, 64), :], f1b.at[i], nxt).start()
        copy(F2, i, cot.at[i, rows(xf * 128 + 64, 64), :], f2b.at[i], prv).start()

    def stage_lb1(i):
        got(F1, i, f1b.at[i])
        rr = rows(xn * 128, 64)
        cot[i, rr, :] = (cot[i, rr, :].astype(F32) + f1b[i].astype(F32)).astype(BF)
        copy(R1, i, cot.at[i, rows(xn * 128, 128), :], r1b.at[i], nxt).start()
        got(F2, i, f2b.at[i])
        rr = rows(xb * 128 + 64, 64)
        cot[i, rr, :] = (cot[i, rr, :].astype(F32) + f2b[i].astype(F32)).astype(BF)
        copy(R2, i, cot.at[i, rows(xb * 128, 128), :], r2b.at[i], prv).start()

    def reduced(i, which):
        rr = rows(which * 64, 64)
        return (
            cot[i, rows(x * 128 + which * 64, 64), :].astype(F32)
            + r1b[i, rr, :].astype(F32)
            + r2b[i, rr, :].astype(F32)
        )

    def stage_lc1(i):
        got(R1, i, r1b.at[i])
        got(R2, i, r2b.at[i])
        rr = rows(x * 128 + (1 - yh) * 64, 64)
        cot[i, rr, :] = reduced(i, 1 - yh).astype(BF)
        copy(YX, i, cot.at[i, rr, :], yr.at[i], par).start()

    def stage_ld1(i):
        got(YX, i, yr.at[i])
        total = reduced(i, yh) + yr[i].astype(F32)
        layer_ref[:, cols(chunk(i) * WC, WC)] = (gate * total).astype(BF)

    def slot(i):
        return sum((i > n).astype(jnp.int32) for n in SCATTER_Y)

    def stage_la2(i):
        product(i)
        for n in range(4):
            copy(P0 + n, i, cot.at[i, rows(n * 128 + (1 - yh) * 64, 64), :], p4b.at[slot(i), n], par).start()

    def add_partner(i, xx):
        rr = rows(xx * 128 + yh * 64, 64)
        return cot[i, rr, :].astype(F32) + p4b[slot(i), xx].astype(F32)

    def stage_lb2(i):
        for n in range(4):
            got(P0 + n, i, p4b.at[slot(i), n])
        rr = rows(xf * 128 + yh * 64, 64)
        cot[i, rr, :] = add_partner(i, xf).astype(BF)
        copy(F1, i, cot.at[i, rows(xf * 128 + yh * 64, 32), :], f1b.at[i, pl.ds(0, 32), :], nxt).start()
        copy(F2, i, cot.at[i, rows(xf * 128 + yh * 64 + 32, 32), :], f2b.at[i, pl.ds(0, 32), :], prv).start()

    def stage_lc2(i):
        top, low = pl.ds(0, 32), pl.ds(0, 64)
        got(F1, i, f1b.at[i, top, :])
        val = add_partner(i, xn)
        cot[i, rows(xn * 128 + yh * 64, 32), :] = (val[:32] + f1b[i, top, :].astype(F32)).astype(BF)
        cot[i, rows(xn * 128 + yh * 64 + 32, 32), :] = val[32:].astype(BF)
        copy(R1, i, cot.at[i, rows(xn * 128 + yh * 64, 64), :], r1b.at[i, low, :], nxt).start()
        got(F2, i, f2b.at[i, top, :])
        val = add_partner(i, xb)
        cot[i, rows(xb * 128 + yh * 64, 32), :] = val[:32].astype(BF)
        cot[i, rows(xb * 128 + yh * 64 + 32, 32), :] = (val[32:] + f2b[i, top, :].astype(F32)).astype(BF)
        copy(R2, i, cot.at[i, rows(xb * 128 + yh * 64, 64), :], r2b.at[i, low, :], prv).start()

    def stage_ld2(i):
        low = pl.ds(0, 64)
        got(R1, i, r1b.at[i, low, :])
        got(R2, i, r2b.at[i, low, :])
        total = add_partner(i, x) + r1b[i, low, :].astype(F32) + r2b[i, low, :].astype(F32)
        layer_ref[:, cols(chunk(i) * WC, WC)] = (gate * total).astype(BF)

    def chunk_sent(i):
        sent(AGY, i, cot.at[i, rows(x * 128, 64), :])

        @pl.when(scatters_y(i))
        def _():
            for n in range(4):
                sent(P0 + n, i, p4b.at[slot(i), n])
            for kind in (F1, F2):
                sent(kind, i, cot.at[i, rows(x * 128, 32), :])
            for kind in (R1, R2):
                sent(kind, i, cot.at[i, rows(x * 128, 64), :])

        @pl.when(jnp.logical_not(scatters_y(i)))
        def _():
            sent(F1, i, f1b.at[i])
            sent(F2, i, f2b.at[i])
            sent(R1, i, r1b.at[i])
            sent(R2, i, r2b.at[i])
            sent(YX, i, yr.at[i])

    def scatters_y(i):
        return member(i, SCATTER_Y)

    stage_la = either(stage_la2, stage_la1, scatters_y)
    stage_lb = either(stage_lb2, stage_lb1, scatters_y)
    stage_lc = either(stage_lc2, stage_lc1, scatters_y)
    stage_ld_ = either(stage_ld2, stage_ld1, scatters_y)

    def stage_ld(i):
        stage_ld_(i)
        chunk_sent(i)

    def masked(score, row, tok):
        return jnp.where(mask2[pl.ds(row, 1), tok] > 0, score, NEG)

    def forward(j):
        hh, u = j // 2, j % 2
        hc = cols(hh * HD, HD)
        vc = cols(256 + hh * HD, HD)
        tok = cols(u * TOK, TOK)
        qv = q2[rows(u * TOK, TOK), hc]

        def scores(ab, best):
            part = dot(kvb[rows(ab * 256, 256), hc], qv, NT)
            for b in range(2):
                val = masked(part[b * 128 : (b + 1) * 128], ab * 2 + b, tok)
                sc[rows(ab * 256 + b * 128, 128), :] = val
                best = jnp.maximum(best, jnp.max(val, axis=0, keepdims=True))
            return best

        best = lax.fori_loop(0, AUD // 256, scores, jnp.full((1, TOK), NEG, F32))

        def weigh(ab, total):
            rr = rows(ab * 256, 256)
            val = jnp.exp2((sc[rr, :] - best) * C2)
            pb[rr, :] = val.astype(BF)
            return total + jnp.sum(val, axis=0, keepdims=True)

        total = lax.fori_loop(0, AUD // 256, weigh, jnp.zeros((1, TOK), F32))
        out = dot(kvb[:, vc], pb[...], TN)
        ht[rows(core * 256 + hh * HD, HD), tok] = (out / total).astype(BF)
        lse[hh, :, tok] = best * C2 + jnp.log2(total)

    def kv_z(hh, dz):
        return pltpu.make_async_remote_copy(
            src_ref=kv_out.at[hh, rows(((z + dz) % 4) * 512, 512), :], dst_ref=kv_in.at[hh, dz - 1],
            send_sem=ds_.at[hh, dz], recv_sem=dr.at[hh, dz], device_id=zdev(dz), device_id_type=MESH)

    def kv_y(hh, n):
        src = ((yl + n // 2) % 2) * 2 + (core + n) % 2
        return pltpu.make_async_remote_copy(
            src_ref=kv_out.at[hh, rows(z * 512 + src * 128, 128), :], dst_ref=kv_fin.at[hh, n],
            send_sem=fs.at[hh, n], recv_sem=fr.at[hh, n], device_id=near(n), device_id_type=MESH)

    def kv_reduce(hh):
        for dz in range(1, 4):
            kv_z(hh, dz).wait_recv()
        for b in range(4):
            total = kv_out[hh, rows(z * 512 + b * 128, 128), :].astype(F32)
            for dz in range(3):
                total += kv_in[hh, dz, b * 128 : (b + 1) * 128, :].astype(F32)
            kv_out[hh, rows(z * 512 + b * 128, 128), :] = total.astype(BF)
        for n in range(1, 4):
            kv_y(hh, n).start()
        for dz in range(1, 4):
            kv_z(hh, dz).wait_send()

    def kv_finish(hh):
        for n in range(1, 4):
            kv_y(hh, n).wait_recv()
        same = kv_out[hh, rows(s * 128, 128), :].astype(F32) + kv_fin[hh, 2].astype(F32)
        other = kv_fin[hh, 1].astype(F32) + kv_fin[hh, 3].astype(F32)
        hc = cols(core * 256 + hh * HD, HD)
        dk_ref[:, hc] = same[:, :HD].astype(BF)
        dv_ref[:, hc] = same[:, HD:].astype(BF)
        hc = cols((1 - core) * 256 + hh * HD, HD)
        dk_ref[:, hc] = other[:, :HD].astype(BF)
        dv_ref[:, hc] = other[:, HD:].astype(BF)
        for n in range(1, 4):
            kv_y(hh, n).wait_send()

    gw_send = pltpu.make_async_remote_copy(
        src_ref=gw_out.at[1], dst_ref=gw_par, send_sem=fs.at[0, 0], recv_sem=fr.at[0, 0],
        device_id=near(2), device_id_type=MESH)

    def gw_reduce(which, write):
        def got_one(i, c):
            got(GW, 2 * i + which, gw_in.at[2 * i + which - 2])
            return c

        lax.fori_loop(1, 4, got_one, 0)

        def add(b, c):
            rr = rows(b * 64, 64)
            total = gw_out[which, rr, :].astype(F32)
            for i in range(3):
                total += gw_in[2 * i + which, rr, :].astype(F32)
            write(rr, total)
            return c

        lax.fori_loop(0, 8, add, 0)

    def gw_part():
        def write(rr, total):
            gw_out[1, rr, :] = total.astype(BF)

        gw_reduce(1, write)
        gw_send.start()

    def gw_finish():
        gw_send.wait_recv()

        def write(rr, total):
            gw_ref[rr, :] = (gate * (total + gw_par[rr, :].astype(F32))).astype(BF)

        gw_reduce(0, write)
        gw_send.wait_send()

        def gw_left(i, c):
            sent(GW, i, gw_out.at[i])
            return c

        lax.fori_loop(2, CH, gw_left, 0)

    def backward(j):
        hh = j // 2
        ah = (j + 1 + z // 2) % 2
        hc = cols(hh * HD, HD)
        hr = rows(hh * HD, HD)
        first = j % 2 == 0

        @pl.when(first)
        def _():
            dq_acc[...] = jnp.zeros_like(dq_acc)
            own = ht[rows(core * 256 + hh * HD, HD), :].astype(F32)
            delta[...] = jnp.sum(gh2[hr, :].astype(F32) * own, axis=0, keepdims=True)

        def step(b, c):
            rr = rows(ah * 1024 + b * 256, 256)
            kk = kvb[rr, hc]
            vv = kvb[rr, cols(256 + hh * HD, HD)]
            qv = q2[:, hc]
            gv = gh2[hr, :]
            score = dot(kk, qv, NT)
            logs = lse[hh]
            probs = []
            for m in range(2):
                row = ah * 8 + b * 2 + m
                val = masked(score[m * 128 : (m + 1) * 128], row, slice(None))
                probs.append(jnp.exp2(val * C2 - logs))
            prob = jnp.concatenate(probs, axis=0)
            dp = dot(vv, gv, NN)
            dsc = (prob * (dp - delta[...])).astype(BF)
            kv_out[hh, rr, pl.ds(HD, HD)] = dot(prob.astype(BF), gv, NT).astype(BF)
            kv_out[hh, rr, pl.ds(0, HD)] = (SCALE * dot(dsc, qv, NN)).astype(BF)
            dq_acc[...] += dot(kk, dsc, TN)
            return c

        lax.fori_loop(0, 4, step, 0)

        for b in range(2):
            dz = (ah * 2 + b - z + 4) % 4

            @pl.when(dz > 0)
            def _():
                kv_z(hh, dz).start()

        @pl.when(j % 2 == 1)
        def _():
            full = SCALE * dq_acc[...]
            for u in range(2):
                piece = full[:, u * TOK : (u + 1) * TOK].T.astype(BF)

                @pl.when(core == u)
                def _():
                    dq_ref[:, cols(core * 256 + hh * HD, HD)] = piece

                @pl.when(core != u)
                def _():
                    dq_out[:, hc] = piece

    mine_rows = rows(core * 256, 256)
    ht_send = extra(2, ht.at[mine_rows, :], ht.at[mine_rows, :])
    their_rows = rows((1 - core) * 256, 256)
    gh_send = extra(3, gh_own.at[their_rows, :], gh2.at[:, cols(core * TOK, TOK)])
    dq_send = extra(4, dq_out, dq_in)

    def heads_first():
        q_copy.wait()
        other_q = q2.at[rows((1 - core) * TOK, TOK), :]
        extra(0, other_q, other_q).wait_recv()
        other_m = mask2.at[:, cols((1 - core) * TOK, TOK)]
        extra(1, other_m, other_m).wait_recv()
        for dz in range(1, 4):
            kv_far(dz, (z - dz + 4) % 4).wait_recv()

    def on_first(i, fn):
        @pl.when(i == 0)
        def _():
            fn()

    def stage_fw(j):
        on_first(j, heads_first)
        forward(j)

    def gh_got():
        other = gh2.at[:, cols((1 - core) * TOK, TOK)]
        extra(3, other, other).wait_recv()

    def stage_bw(j):
        on_first(j, gh_got)
        backward(j)

    def stage_hr():
        extra(2, ht.at[their_rows, :], ht.at[their_rows, :]).wait_recv()
        hrow[...] = ht[:, cols(core * TOK, TOK)].astype(F32).T.astype(BF)
        q_send.wait_send()
        m_send.wait_send()
        ht_send.wait_send()
        for n in range(1, 4):
            for copy_ in kv_near(n, rows(s * 128, 128)):
                copy_.wait_send()
            kv_far(n, z).wait_send()

    def stage_gh():
        gh_own[...] = (gate * gh_acc[...]).astype(BF)
        gh2[:, cols(core * TOK, TOK)] = gh_own[mine_rows, :]
        gh_send.start()

    def stage_df():
        dq_send.wait_recv()
        dq_ref[:, cols((1 - core) * 256, 256)] = dq_in[...]
        dq_send.wait_send()
        gh_send.wait_send()

    once = {
        "L0": prepare, "K0": kv_share, "K1": kv_spread, "HX": ht_send.start, "HR": stage_hr, "GH": stage_gh,
        "GP": gw_part, "GF": gw_finish, "DQ": dq_send.start, "DF": stage_df,
    }
    each = {
        "A": stage_a, "B": stage_b, "C": stage_c, "D": stage_d, "X": stage_x2, "E": stage_e, "F": stage_f,
        "LA": stage_la, "LB": stage_lb, "LC": stage_lc, "LD": stage_ld,
        "FW": stage_fw, "BW": stage_bw, "KR": kv_reduce, "KF": kv_finish,
    }
    w_tick = min(ticks[0] for name, ticks, _ in PLAN if name == "E")

    def packed(ticks, low):
        return jnp.int32(sum(1 << (n - low) for n in ticks if low <= n < low + 30))

    def tick(g, state):
        after = []
        for (name, ticks, idx), (bits, order) in zip(PLAN, state):
            for low in range(30, TICKS, 30):
                bits = jnp.where(g == low, packed(ticks, low), bits)
            hit = bits % 2 == 1
            if name == "E":

                @pl.when(g == w_tick)
                def _():
                    w_copy.wait()

            @pl.when(hit)
            def _():
                if name in once:
                    once[name]()
                else:
                    each[name](order % 8)

            after.append((bits // 2, jnp.where(hit, order // 8, order)))
        return tuple(after)

    start = tuple(
        (packed(ticks, 0), jnp.int32(sum(i << (3 * n) for n, i in enumerate(idx)))) for _, ticks, idx in PLAN
    )
    lax.fori_loop(0, TICKS, tick, start)


def hand_over(*refs):
    given, results, sems = refs[:5], refs[5:10], refs[10]
    outs = [pltpu.make_async_copy(given[n], results[n], sems.at[n]) for n in range(5)]
    for c in outs:
        c.start()
    for c in outs:
        c.wait()


def per_device(queries, audio_keys, audio_values, out_weight, mix_gate, block_mask, cotangent):
    hbm = pl.BlockSpec(memory_space=pl.ANY)
    vmem = pl.BlockSpec(memory_space=pltpu.VMEM)
    dma = pltpu.SemaphoreType.DMA
    results = pl.pallas_call(
        kernel,
        out_shape=(
            pltpu.VMEM((64, 8192), BF),
            pltpu.VMEM((TOK, 512), BF),
            pltpu.VMEM((128, 512), BF),
            pltpu.VMEM((128, 512), BF),
            pltpu.VMEM((512, 512), BF),
        ),
        in_specs=[hbm, hbm, hbm, hbm, vmem, pl.BlockSpec(memory_space=pltpu.SMEM), hbm],
        out_specs=[vmem] * 5,
        scratch_shapes=[
            pltpu.VMEM((512, 8192), BF),
            pltpu.VMEM((CH, TOK, WC), BF),
            pltpu.VMEM((CH, TOK, HALF), BF),
            pltpu.VMEM((AUD, 512), BF),
            pltpu.VMEM((2 * TOK, 256), BF),
            pltpu.VMEM((16, 2 * TOK), F32),
            pltpu.VMEM((512, 2 * TOK), BF),
            pltpu.VMEM((TOK, 512), BF),
            pltpu.VMEM((512, TOK), F32),
            pltpu.VMEM((512, TOK), BF),
            pltpu.VMEM((256, 2 * TOK), BF),
            pltpu.VMEM((AUD, TOK), F32),
            pltpu.VMEM((AUD, TOK), BF),
            pltpu.VMEM((2, 1, 2 * TOK), F32),
            pltpu.VMEM((1, 2 * TOK), F32),
            pltpu.VMEM((HD, 2 * TOK), F32),
            pltpu.VMEM((TOK, 256), BF),
            pltpu.VMEM((TOK, 256), BF),
            pltpu.VMEM((CH, 64, WC), BF),
            pltpu.VMEM((CH, 64, WC), BF),
            pltpu.VMEM((CH, 128, WC), BF),
            pltpu.VMEM((CH, 128, WC), BF),
            pltpu.VMEM((CH, 64, WC), BF),
            pltpu.VMEM((3, 4, 64, WC), BF),
            pltpu.VMEM((CH, 512, HALF), BF),
            pltpu.VMEM((CH - 2, 512, HALF), BF),
            pltpu.VMEM((512, HALF), BF),
            pltpu.VMEM((2, AUD, 256), BF),
            pltpu.VMEM((2, 3, 512, 256), BF),
            pltpu.VMEM((2, 4, 128, 256), BF),
            dma((KINDS, CH)), dma((KINDS, CH)),
            dma((4, 2)), dma((4, 2)),
            dma((4,)), dma((4,)),
            dma((2, 4)), dma((2, 4)),
            dma((2, 4)), dma((2, 4)),
            dma((5,)), dma((5,)),
            dma((CH + 4,)),
        ],
        compiler_params=pltpu.CompilerParams(
            collective_id=0, has_side_effects=True, vmem_limit_bytes=58 * 2**20
        ),
        cost_estimate=pl.CostEstimate(flops=20 * 10**9, bytes_accessed=16 * 2**20, transcendentals=8 * 2**20),
    )(queries, audio_keys, audio_values, out_weight, mix_gate.reshape(1, 1), block_mask, cotangent)
    results = [pltpu.with_memory_space_constraint(r, pltpu.VMEM) for r in results]
    return pl.pallas_call(
        hand_over,
        out_shape=tuple(jax.ShapeDtypeStruct(r.shape, r.dtype) for r in results),
        in_specs=[vmem] * 5,
        out_specs=[hbm] * 5,
        scratch_shapes=[dma((5,))],
    )(*results)


def solution(mesh):
    in_specs = (
        P("seq", "tp"),
        P("seq", "tp"),
        P("seq", "tp"),
        P("tp", None),
        P(),
        P("seq", None),
        P(("seq", "tp"), None),
    )
    out_specs = (
        P(("seq", "tp"), None),
        P("seq", "tp"),
        P("seq", "tp"),
        P("seq", "tp"),
        P("tp", "seq"),
    )
    return jax.shard_map(
        per_device, mesh=mesh, in_specs=in_specs, out_specs=out_specs, check_vma=False
    )
```

```python
import jax
import jax.numpy as jnp
from jax import lax
from jax.experimental import pallas as pl
from jax.experimental.pallas import tpu as pltpu
from jax.sharding import PartitionSpec as P

HD = 128
BLK = 128
CH = 8
WC = 1024
HALF = 512
TOK = 512
AUD = 2048
SCALE = HD ** (-0.5)
C2 = SCALE * 1.4426950408889634
NEG = -1e30
BF = jnp.bfloat16
F32 = jnp.float32
MESH = pl.DeviceIdType.MESH

NT = (((1,), (1,)), ((), ()))
NN = (((1,), (0,)), ((), ()))
TN = (((0,), (0,)), ((), ()))

AGY, AGP, AGM, AFP, AFM, SIB, GW, F1, F2, R1, R2, YX, YP, YM, YF, P0 = range(16)
KINDS = P0 + 4
GATHER_X = (3, 5)
SCATTER_Y = (1, 3, 5)
TICKS = 54
PLAN = (
    ('F', (18, 19, 22, 24, 28, 29, 30, 36), (5, 7, 3, 2, 0, 6, 1, 4)),
    ('GP', (32,), (0,)),
    ('B', (0, 1, 7, 8, 9, 10, 11, 15), (3, 5, 4, 2, 7, 0, 1, 6)),
    ('D', (9, 10, 16, 17, 23, 24, 26, 28), (5, 3, 2, 7, 0, 4, 6, 1)),
    ('GH', (29,), (0,)),
    ('KF', (47, 48), (1, 0)),
    ('X', (15, 17), (5, 3)),
    ('E', (15, 19, 20, 22, 24, 25, 27, 28), (5, 7, 2, 3, 0, 4, 6, 1)),
    ('K0', (0,), (0,)),
    ('LB', (30, 31, 32, 33, 37, 38, 39, 40), (5, 2, 7, 0, 3, 6, 1, 4)),
    ('C', (4, 6, 9, 10, 11, 18, 20, 21), (3, 5, 2, 7, 4, 0, 6, 1)),
    ('LA', (18, 22, 23, 26, 28, 29, 31, 36), (5, 7, 3, 2, 0, 6, 1, 4)),
    ('A', (0, 1, 2, 3, 4, 5, 8, 9), (4, 2, 0, 7, 1, 3, 5, 6)),
    ('BW', (31, 33, 34, 35), (0, 1, 2, 3)),
    ('DQ', (40,), (0,)),
    ('L0', (7,), (0,)),
    ('FW', (11, 12, 13, 14), (0, 1, 2, 3)),
    ('LC', (36, 40, 41, 42, 43, 44, 45, 46), (7, 0, 5, 2, 1, 6, 3, 4)),
    ('KR', (39, 45), (0, 1)),
    ('LD', (45, 46, 48, 49, 50, 51, 52, 53), (0, 5, 1, 6, 7, 2, 4, 3)),
    ('HR', (17,), (0,)),
    ('GF', (53,), (0,)),
    ('HX', (14,), (0,)),
    ('K1', (5,), (0,)),
    ('DF', (43,), (0,)),
)


def dot(a, b, dims):
    return lax.dot_general(a, b, dims, preferred_element_type=F32)


def kernel(
    q_hbm, k_hbm, v_hbm, w_hbm, gate_ref, mask_ref, cot_hbm,
    layer_ref, dq_ref, dk_ref, dv_ref, gw_ref,
    w, cot, cot_sib, kvb, q2, mask2, ht, hrow, gh_acc, gh_own, gh2,
    sc, pb, lse, delta, dq_acc, dq_out, dq_in, f1b, f2b, r1b, r2b, yr, p4b, gw_out, gw_in, gw_par, kv_out, kv_in, kv_fin,
    ss, rs, ps, pr, zs, zr, ds_, dr, fs, fr, es, er, ls,
):
    s = lax.axis_index("seq")
    t = lax.axis_index("tp")
    core = s % 2
    z = s // 4
    yl = (s // 2) % 2
    x = t // 2
    yh = t % 2
    xn, xb, xf = (x + 1) % 4, (x + 3) % 4, (x + 2) % 4
    sib = (s + 1 - 2 * core, t)
    nxt = (s, xn * 2 + yh)
    prv = (s, xb * 2 + yh)
    par = (s, x * 2 + 1 - yh)

    def zdev(dz):
        return (((z + dz) % 4) * 4 + yl * 2 + core, t)

    def near(n):
        return (z * 4 + ((yl + n // 2) % 2) * 2 + (core + n) % 2, t)

    def rows(start, size):
        return pl.ds(pl.multiple_of(start, size), size)

    def cols(start, size):
        return pl.ds(pl.multiple_of(start, 128), size)

    def chunk(i):
        m = i // 2
        zz = ((z // 2 + m // 2) % 2) * 2 + (z + m) % 2
        return zz * 2 + (yl + i) % 2

    def copy(kind, i, src, dst, dev):
        return pltpu.make_async_remote_copy(
            src_ref=src, dst_ref=dst, send_sem=ss.at[kind, i], recv_sem=rs.at[kind, i],
            device_id=dev, device_id_type=MESH,
        )

    def got(kind, i, dst):
        copy(kind, i, dst, dst, nxt).wait_recv()

    def sent(kind, i, src):
        copy(kind, i, src, src, nxt).wait_send()

    barrier = pltpu.get_barrier_semaphore()
    for dev in (nxt, prv, par):
        pl.semaphore_signal(barrier, inc=1, device_id=dev, device_id_type=MESH)

    for n in range(1, 4):
        pl.semaphore_signal(barrier, inc=1, device_id=near(n), device_id_type=MESH)
        pl.semaphore_signal(barrier, inc=1, device_id=zdev(n), device_id_type=MESH)

    def own_piece(i):
        return pltpu.make_async_copy(
            cot_hbm.at[:, cols(chunk(i) * WC, WC)], cot.at[i, rows(t * 64, 64), :], ls.at[i]
        )

    def start_piece(i, c):
        own_piece(i).start()
        return c

    w_copy = pltpu.make_async_copy(w_hbm, w, ls.at[CH])
    my_heads = cols(core * 256, 256)
    k_copy = pltpu.make_async_copy(k_hbm.at[:, my_heads], kvb.at[rows(s * 128, 128), pl.ds(0, 256)], ls.at[CH + 1])
    v_copy = pltpu.make_async_copy(v_hbm.at[:, my_heads], kvb.at[rows(s * 128, 128), pl.ds(256, 256)], ls.at[CH + 2])
    q_copy = pltpu.make_async_copy(q_hbm.at[:, my_heads], q2.at[rows(core * TOK, TOK), :], ls.at[CH + 3])

    pl.semaphore_wait(barrier, 9)

    def stage_a(i):
        copy(AGY, i, cot_hbm.at[:, cols(chunk(i) * WC, WC)], cot.at[i, rows(t * 64, 64), :], par).start()

    def piece_x(i):
        src = cot_hbm.at[:, cols(chunk(i) * WC, WC)]
        dst = cot.at[i, rows(t * 64, 64), :]
        copy(AGP, i, src, dst, nxt).start()
        copy(AGM, i, src, dst, prv).start()


    def extra(n, src, dst):
        return pltpu.make_async_remote_copy(
            src_ref=src, dst_ref=dst, send_sem=es.at[n], recv_sem=er.at[n], device_id=sib, device_id_type=MESH
        )

    other_heads = cols((1 - core) * 256, 256)
    q_send = extra(0, q_hbm.at[:, other_heads], q2.at[rows(core * TOK, TOK), :])
    my_mask = mask2.at[:, cols(core * TOK, TOK)]
    m_send = extra(1, my_mask, my_mask)

    def prepare():
        gh_acc[...] = jnp.zeros_like(gh_acc)
        for tb in range(TOK // BLK):
            for ab in range(AUD // BLK):
                seen = jnp.full((1, BLK), mask_ref[tb, ab].astype(F32))
                mask2[pl.ds(ab, 1), cols(core * TOK + tb * BLK, BLK)] = seen
        q_send.start()
        m_send.start()

    def kv_near(n, src_rows):
        heads = cols(((core + n) % 2) * 256, 256)
        return [
            pltpu.make_async_remote_copy(
                src_ref=src.at[:, heads], dst_ref=kvb.at[src_rows, pl.ds(part * 256, 256)],
                send_sem=ps.at[n, part], recv_sem=pr.at[n, part], device_id=near(n), device_id_type=MESH)
            for part, src in enumerate((k_hbm, v_hbm))
        ]

    def kv_far(dz, zz):
        block = kvb.at[rows(zz * 512, 512), :]
        return pltpu.make_async_remote_copy(
            src_ref=block, dst_ref=block, send_sem=zs.at[dz], recv_sem=zr.at[dz],
            device_id=zdev(dz), device_id_type=MESH)

    def kv_share():
        for n in range(1, 4):
            for copy_ in kv_near(n, rows(s * 128, 128)):
                copy_.start()

        for c in (k_copy, v_copy):
            c.start()
        lax.fori_loop(0, CH, start_piece, 0)
        for c in (q_copy, w_copy):
            c.start()

    def kv_spread():
        k_copy.wait()
        v_copy.wait()
        for n in range(1, 4):
            src = z * 4 + ((yl + n // 2) % 2) * 2 + (core + n) % 2
            for copy_ in kv_near(n, rows(src * 128, 128)):
                copy_.wait_recv()
        for dz in (1, 3, 2):
            kv_far(dz, z).start()

    gate = jnp.tanh(gate_ref[...])

    def stage_b1(i):
        own_piece(i).wait()
        got(AGY, i, cot.at[i, rows((x * 2 + 1 - yh) * 64, 64), :])
        block = cot.at[i, rows(x * 128, 128), :]
        copy(AGP, i, block, block, nxt).start()
        copy(AGM, i, block, block, prv).start()

    def stage_c1(i):
        got(AGP, i, cot.at[i, rows(xb * 128, 128), :])
        top = cot.at[i, rows(xb * 128, 64), :]
        copy(AFP, i, top, top, nxt).start()
        got(AGM, i, cot.at[i, rows(xn * 128, 128), :])
        low = cot.at[i, rows(xn * 128 + 64, 64), :]
        copy(AFM, i, low, low, prv).start()

    def stage_d1(i):
        got(AFP, i, cot.at[i, rows(xf * 128, 64), :])
        got(AFM, i, cot.at[i, rows(xf * 128 + 64, 64), :])
        share(i)

    def share(i):
        copy(SIB, i, cot.at[i, :, cols((1 - core) * HALF, HALF)], cot_sib.at[i], sib).start()

    def to_partner(kind, i, xx):
        block = cot.at[i, rows(xx * 128 + yh * 64, 64), :]
        copy(kind, i, block, block, par).start()

    def stage_c2(i):
        got(AGP, i, cot.at[i, rows(xb * 128 + yh * 64, 64), :])
        top = cot.at[i, rows(xb * 128 + yh * 64, 32), :]
        copy(AFP, i, top, top, nxt).start()
        got(AGM, i, cot.at[i, rows(xn * 128 + yh * 64, 64), :])
        low = cot.at[i, rows(xn * 128 + yh * 64 + 32, 32), :]
        copy(AFM, i, low, low, prv).start()
        to_partner(YP, i, xb)
        to_partner(YM, i, xn)

    def stage_d2(i):
        got(AFP, i, cot.at[i, rows(xf * 128 + yh * 64, 32), :])
        got(AFM, i, cot.at[i, rows(xf * 128 + yh * 64 + 32, 32), :])
        to_partner(YF, i, xf)

    def stage_x2(i):
        own_piece(i).wait()
        for kind, xx in ((AGY, x), (YP, xb), (YM, xn), (YF, xf)):
            got(kind, i, cot.at[i, rows(xx * 128 + (1 - yh) * 64, 64), :])
        share(i)

    def either(first, second, cond):
        def stage(i):
            @pl.when(cond(i))
            def _():
                first(i)

            @pl.when(jnp.logical_not(cond(i)))
            def _():
                second(i)

        return stage

    def member(i, chosen):
        hit = i < 0
        for n in chosen:
            hit = jnp.logical_or(hit, i == n)
        return hit

    def gathers_x(i):
        return member(i, GATHER_X)

    stage_b = either(piece_x, stage_b1, gathers_x)
    stage_c = either(stage_c2, stage_c1, gathers_x)
    stage_d = either(stage_d2, stage_d1, gathers_x)

    def gather_sent(i):
        @pl.when(gathers_x(i))
        def _():
            for kind in (AGP, AGM, YP, YM, YF):
                sent(kind, i, cot.at[i, rows(x * 128, 64), :])
            for kind in (AFP, AFM):
                sent(kind, i, cot.at[i, rows(x * 128, 32), :])

        @pl.when(jnp.logical_not(gathers_x(i)))
        def _():
            for kind in (AGP, AGM):
                sent(kind, i, cot.at[i, rows(x * 128, 128), :])
            for kind in (AFP, AFM):
                sent(kind, i, cot.at[i, rows(x * 128, 64), :])

    def stage_e(i):
        cc = cols(chunk(i) * WC, WC)
        for part in range(2):
            rr = pl.ds(part * 256, 256)
            gh_acc[rr, :] += dot(w[rr, cc], cot[i], NT)

    def stage_f(i):
        got(SIB, i, cot_sib.at[i])
        mine = cols(core * TOK, TOK)
        theirs = cols((1 - core) * TOK, TOK)
        for part in range(2):
            rr = pl.ds(part * 256, 256)
            val = dot(ht[rr, mine], cot[i, :, cols(core * HALF, HALF)], NN) + dot(ht[rr, theirs], cot_sib[i], NN)
            gw_out[i, rr, :] = val.astype(BF)

        @pl.when(i > 1)
        def _():
            zz = chunk(i) // 2
            copy(GW, i, gw_out.at[i], gw_in.at[i - 2], (zz * 4 + yl * 2 + core, t)).start()

    def product(i):
        gather_sent(i)
        sent(SIB, i, cot_sib.at[i])
        for part in range(2):
            cc = cols(chunk(i) * WC + part * HALF, HALF)
            cot[i, :, pl.ds(part * HALF, HALF)] = dot(hrow[...], w[:, cc], NN).astype(BF)

    def stage_la1(i):
        product(i)
        copy(F1, i, cot.at[i, rows(xf * 128, 64), :], f1b.at[i], nxt).start()
        copy(F2, i, cot.at[i, rows(xf * 128 + 64, 64), :], f2b.at[i], prv).start()

    def stage_lb1(i):
        got(F1, i, f1b.at[i])
        rr = rows(xn * 128, 64)
        cot[i, rr, :] = (cot[i, rr, :].astype(F32) + f1b[i].astype(F32)).astype(BF)
        copy(R1, i, cot.at[i, rows(xn * 128, 128), :], r1b.at[i], nxt).start()
        got(F2, i, f2b.at[i])
        rr = rows(xb * 128 + 64, 64)
        cot[i, rr, :] = (cot[i, rr, :].astype(F32) + f2b[i].astype(F32)).astype(BF)
        copy(R2, i, cot.at[i, rows(xb * 128, 128), :], r2b.at[i], prv).start()

    def reduced(i, which):
        rr = rows(which * 64, 64)
        return (
            cot[i, rows(x * 128 + which * 64, 64), :].astype(F32)
            + r1b[i, rr, :].astype(F32)
            + r2b[i, rr, :].astype(F32)
        )

    def stage_lc1(i):
        got(R1, i, r1b.at[i])
        got(R2, i, r2b.at[i])
        rr = rows(x * 128 + (1 - yh) * 64, 64)
        cot[i, rr, :] = reduced(i, 1 - yh).astype(BF)
        copy(YX, i, cot.at[i, rr, :], yr.at[i], par).start()

    def stage_ld1(i):
        got(YX, i, yr.at[i])
        total = reduced(i, yh) + yr[i].astype(F32)
        layer_ref[:, cols(chunk(i) * WC, WC)] = (gate * total).astype(BF)

    def slot(i):
        return sum((i > n).astype(jnp.int32) for n in SCATTER_Y)

    def stage_la2(i):
        product(i)
        for n in range(4):
            copy(P0 + n, i, cot.at[i, rows(n * 128 + (1 - yh) * 64, 64), :], p4b.at[slot(i), n], par).start()

    def add_partner(i, xx):
        rr = rows(xx * 128 + yh * 64, 64)
        return cot[i, rr, :].astype(F32) + p4b[slot(i), xx].astype(F32)

    def stage_lb2(i):
        for n in range(4):
            got(P0 + n, i, p4b.at[slot(i), n])
        rr = rows(xf * 128 + yh * 64, 64)
        cot[i, rr, :] = add_partner(i, xf).astype(BF)
        copy(F1, i, cot.at[i, rows(xf * 128 + yh * 64, 32), :], f1b.at[i, pl.ds(0, 32), :], nxt).start()
        copy(F2, i, cot.at[i, rows(xf * 128 + yh * 64 + 32, 32), :], f2b.at[i, pl.ds(0, 32), :], prv).start()

    def stage_lc2(i):
        top, low = pl.ds(0, 32), pl.ds(0, 64)
        got(F1, i, f1b.at[i, top, :])
        val = add_partner(i, xn)
        cot[i, rows(xn * 128 + yh * 64, 32), :] = (val[:32] + f1b[i, top, :].astype(F32)).astype(BF)
        cot[i, rows(xn * 128 + yh * 64 + 32, 32), :] = val[32:].astype(BF)
        copy(R1, i, cot.at[i, rows(xn * 128 + yh * 64, 64), :], r1b.at[i, low, :], nxt).start()
        got(F2, i, f2b.at[i, top, :])
        val = add_partner(i, xb)
        cot[i, rows(xb * 128 + yh * 64, 32), :] = val[:32].astype(BF)
        cot[i, rows(xb * 128 + yh * 64 + 32, 32), :] = (val[32:] + f2b[i, top, :].astype(F32)).astype(BF)
        copy(R2, i, cot.at[i, rows(xb * 128 + yh * 64, 64), :], r2b.at[i, low, :], prv).start()

    def stage_ld2(i):
        low = pl.ds(0, 64)
        got(R1, i, r1b.at[i, low, :])
        got(R2, i, r2b.at[i, low, :])
        total = add_partner(i, x) + r1b[i, low, :].astype(F32) + r2b[i, low, :].astype(F32)
        layer_ref[:, cols(chunk(i) * WC, WC)] = (gate * total).astype(BF)

    def chunk_sent(i):
        sent(AGY, i, cot.at[i, rows(x * 128, 64), :])

        @pl.when(scatters_y(i))
        def _():
            for n in range(4):
                sent(P0 + n, i, p4b.at[slot(i), n])
            for kind in (F1, F2):
                sent(kind, i, cot.at[i, rows(x * 128, 32), :])
            for kind in (R1, R2):
                sent(kind, i, cot.at[i, rows(x * 128, 64), :])

        @pl.when(jnp.logical_not(scatters_y(i)))
        def _():
            sent(F1, i, f1b.at[i])
            sent(F2, i, f2b.at[i])
            sent(R1, i, r1b.at[i])
            sent(R2, i, r2b.at[i])
            sent(YX, i, yr.at[i])

    def scatters_y(i):
        return member(i, SCATTER_Y)

    stage_la = either(stage_la2, stage_la1, scatters_y)
    stage_lb = either(stage_lb2, stage_lb1, scatters_y)
    stage_lc = either(stage_lc2, stage_lc1, scatters_y)
    stage_ld_ = either(stage_ld2, stage_ld1, scatters_y)

    def stage_ld(i):
        stage_ld_(i)
        chunk_sent(i)

    def masked(score, row, tok):
        return jnp.where(mask2[pl.ds(row, 1), tok] > 0, score, NEG)

    def forward(j):
        hh, u = j // 2, j % 2
        hc = cols(hh * HD, HD)
        vc = cols(256 + hh * HD, HD)
        tok = cols(u * TOK, TOK)
        qv = q2[rows(u * TOK, TOK), hc]

        def scores(ab, best):
            part = dot(kvb[rows(ab * 256, 256), hc], qv, NT)
            for b in range(2):
                val = masked(part[b * 128 : (b + 1) * 128], ab * 2 + b, tok)
                sc[rows(ab * 256 + b * 128, 128), :] = val
                best = jnp.maximum(best, jnp.max(val, axis=0, keepdims=True))
            return best

        best = lax.fori_loop(0, AUD // 256, scores, jnp.full((1, TOK), NEG, F32))

        def weigh(ab, total):
            rr = rows(ab * 256, 256)
            val = jnp.exp2((sc[rr, :] - best) * C2)
            pb[rr, :] = val.astype(BF)
            return total + jnp.sum(val, axis=0, keepdims=True)

        total = lax.fori_loop(0, AUD // 256, weigh, jnp.zeros((1, TOK), F32))
        out = dot(kvb[:, vc], pb[...], TN)
        ht[rows(core * 256 + hh * HD, HD), tok] = (out / total).astype(BF)
        lse[hh, :, tok] = best * C2 + jnp.log2(total)

    def kv_z(hh, dz):
        return pltpu.make_async_remote_copy(
            src_ref=kv_out.at[hh, rows(((z + dz) % 4) * 512, 512), :], dst_ref=kv_in.at[hh, dz - 1],
            send_sem=ds_.at[hh, dz], recv_sem=dr.at[hh, dz], device_id=zdev(dz), device_id_type=MESH)

    def kv_y(hh, n):
        src = ((yl + n // 2) % 2) * 2 + (core + n) % 2
        return pltpu.make_async_remote_copy(
            src_ref=kv_out.at[hh, rows(z * 512 + src * 128, 128), :], dst_ref=kv_fin.at[hh, n],
            send_sem=fs.at[hh, n], recv_sem=fr.at[hh, n], device_id=near(n), device_id_type=MESH)

    def kv_reduce(hh):
        for dz in range(1, 4):
            kv_z(hh, dz).wait_recv()
        for b in range(4):
            total = kv_out[hh, rows(z * 512 + b * 128, 128), :].astype(F32)
            for dz in range(3):
                total += kv_in[hh, dz, b * 128 : (b + 1) * 128, :].astype(F32)
            kv_out[hh, rows(z * 512 + b * 128, 128), :] = total.astype(BF)
        for n in range(1, 4):
            kv_y(hh, n).start()
        for dz in range(1, 4):
            kv_z(hh, dz).wait_send()

    def kv_finish(hh):
        for n in range(1, 4):
            kv_y(hh, n).wait_recv()
        same = kv_out[hh, rows(s * 128, 128), :].astype(F32) + kv_fin[hh, 2].astype(F32)
        other = kv_fin[hh, 1].astype(F32) + kv_fin[hh, 3].astype(F32)
        hc = cols(core * 256 + hh * HD, HD)
        dk_ref[:, hc] = same[:, :HD].astype(BF)
        dv_ref[:, hc] = same[:, HD:].astype(BF)
        hc = cols((1 - core) * 256 + hh * HD, HD)
        dk_ref[:, hc] = other[:, :HD].astype(BF)
        dv_ref[:, hc] = other[:, HD:].astype(BF)
        for n in range(1, 4):
            kv_y(hh, n).wait_send()

    gw_send = pltpu.make_async_remote_copy(
        src_ref=gw_out.at[1], dst_ref=gw_par, send_sem=fs.at[0, 0], recv_sem=fr.at[0, 0],
        device_id=near(2), device_id_type=MESH)

    def gw_reduce(which, write):
        def got_one(i, c):
            got(GW, 2 * i + which, gw_in.at[2 * i + which - 2])
            return c

        lax.fori_loop(1, 4, got_one, 0)

        def add(b, c):
            rr = rows(b * 64, 64)
            total = gw_out[which, rr, :].astype(F32)
            for i in range(3):
                total += gw_in[2 * i + which, rr, :].astype(F32)
            write(rr, total)
            return c

        lax.fori_loop(0, 8, add, 0)

    def gw_part():
        def write(rr, total):
            gw_out[1, rr, :] = total.astype(BF)

        gw_reduce(1, write)
        gw_send.start()

    def gw_finish():
        gw_send.wait_recv()

        def write(rr, total):
            gw_ref[rr, :] = (gate * (total + gw_par[rr, :].astype(F32))).astype(BF)

        gw_reduce(0, write)
        gw_send.wait_send()

        def gw_left(i, c):
            sent(GW, i, gw_out.at[i])
            return c

        lax.fori_loop(2, CH, gw_left, 0)

    def backward(j):
        hh = j // 2
        ah = (j + 1 + z // 2) % 2
        hc = cols(hh * HD, HD)
        hr = rows(hh * HD, HD)
        first = j % 2 == 0

        @pl.when(first)
        def _():
            dq_acc[...] = jnp.zeros_like(dq_acc)
            own = ht[rows(core * 256 + hh * HD, HD), :].astype(F32)
            delta[...] = jnp.sum(gh2[hr, :].astype(F32) * own, axis=0, keepdims=True)

        def step(b, c):
            rr = rows(ah * 1024 + b * 256, 256)
            kk = kvb[rr, hc]
            vv = kvb[rr, cols(256 + hh * HD, HD)]
            qv = q2[:, hc]
            gv = gh2[hr, :]
            score = dot(kk, qv, NT)
            logs = lse[hh]
            probs = []
            for m in range(2):
                row = ah * 8 + b * 2 + m
                val = masked(score[m * 128 : (m + 1) * 128], row, slice(None))
                probs.append(jnp.exp2(val * C2 - logs))
            prob = jnp.concatenate(probs, axis=0)
            dp = dot(vv, gv, NN)
            dsc = (prob * (dp - delta[...])).astype(BF)
            kv_out[hh, rr, pl.ds(HD, HD)] = dot(prob.astype(BF), gv, NT).astype(BF)
            kv_out[hh, rr, pl.ds(0, HD)] = (SCALE * dot(dsc, qv, NN)).astype(BF)
            dq_acc[...] += dot(kk, dsc, TN)
            return c

        lax.fori_loop(0, 4, step, 0)

        for b in range(2):
            dz = (ah * 2 + b - z + 4) % 4

            @pl.when(dz > 0)
            def _():
                kv_z(hh, dz).start()

        @pl.when(j % 2 == 1)
        def _():
            full = SCALE * dq_acc[...]
            for u in range(2):
                piece = full[:, u * TOK : (u + 1) * TOK].T.astype(BF)

                @pl.when(core == u)
                def _():
                    dq_ref[:, cols(core * 256 + hh * HD, HD)] = piece

                @pl.when(core != u)
                def _():
                    dq_out[:, hc] = piece

    mine_rows = rows(core * 256, 256)
    ht_send = extra(2, ht.at[mine_rows, :], ht.at[mine_rows, :])
    their_rows = rows((1 - core) * 256, 256)
    gh_send = extra(3, gh_own.at[their_rows, :], gh2.at[:, cols(core * TOK, TOK)])
    dq_send = extra(4, dq_out, dq_in)

    def heads_first():
        q_copy.wait()
        other_q = q2.at[rows((1 - core) * TOK, TOK), :]
        extra(0, other_q, other_q).wait_recv()
        other_m = mask2.at[:, cols((1 - core) * TOK, TOK)]
        extra(1, other_m, other_m).wait_recv()
        for dz in range(1, 4):
            kv_far(dz, (z - dz + 4) % 4).wait_recv()

    def on_first(i, fn):
        @pl.when(i == 0)
        def _():
            fn()

    def stage_fw(j):
        on_first(j, heads_first)
        forward(j)

    def gh_got():
        other = gh2.at[:, cols((1 - core) * TOK, TOK)]
        extra(3, other, other).wait_recv()

    def stage_bw(j):
        on_first(j, gh_got)
        backward(j)

    def stage_hr():
        extra(2, ht.at[their_rows, :], ht.at[their_rows, :]).wait_recv()
        hrow[...] = ht[:, cols(core * TOK, TOK)].astype(F32).T.astype(BF)
        q_send.wait_send()
        m_send.wait_send()
        ht_send.wait_send()
        for n in range(1, 4):
            for copy_ in kv_near(n, rows(s * 128, 128)):
                copy_.wait_send()
            kv_far(n, z).wait_send()

    def stage_gh():
        gh_own[...] = (gate * gh_acc[...]).astype(BF)
        gh2[:, cols(core * TOK, TOK)] = gh_own[mine_rows, :]
        gh_send.start()

    def stage_df():
        dq_send.wait_recv()
        dq_ref[:, cols((1 - core) * 256, 256)] = dq_in[...]
        dq_send.wait_send()
        gh_send.wait_send()

    once = {
        "L0": prepare, "K0": kv_share, "K1": kv_spread, "HX": ht_send.start, "HR": stage_hr, "GH": stage_gh,
        "GP": gw_part, "GF": gw_finish, "DQ": dq_send.start, "DF": stage_df,
    }
    each = {
        "A": stage_a, "B": stage_b, "C": stage_c, "D": stage_d, "X": stage_x2, "E": stage_e, "F": stage_f,
        "LA": stage_la, "LB": stage_lb, "LC": stage_lc, "LD": stage_ld,
        "FW": stage_fw, "BW": stage_bw, "KR": kv_reduce, "KF": kv_finish,
    }
    w_tick = min(ticks[0] for name, ticks, _ in PLAN if name == "E")

    def packed(ticks, low):
        return jnp.int32(sum(1 << (n - low) for n in ticks if low <= n < low + 30))

    def tick(g, state):
        after = []
        for (name, ticks, idx), (bits, order) in zip(PLAN, state):
            for low in range(30, TICKS, 30):
                bits = jnp.where(g == low, packed(ticks, low), bits)
            hit = bits % 2 == 1
            if name == "E":

                @pl.when(g == w_tick)
                def _():
                    w_copy.wait()

            @pl.when(hit)
            def _():
                if name in once:
                    once[name]()
                else:
                    each[name](order % 8)

            after.append((bits // 2, jnp.where(hit, order // 8, order)))
        return tuple(after)

    start = tuple(
        (packed(ticks, 0), jnp.int32(sum(i << (3 * n) for n, i in enumerate(idx)))) for _, ticks, idx in PLAN
    )
    lax.fori_loop(0, TICKS, tick, start)


def hand_over(*refs):
    given, results, sems = refs[:5], refs[5:10], refs[10]
    outs = [pltpu.make_async_copy(given[n], results[n], sems.at[n]) for n in range(5)]
    for c in outs:
        c.start()
    for c in outs:
        c.wait()


def per_device(queries, audio_keys, audio_values, out_weight, mix_gate, block_mask, cotangent):
    hbm = pl.BlockSpec(memory_space=pl.ANY)
    vmem = pl.BlockSpec(memory_space=pltpu.VMEM)
    dma = pltpu.SemaphoreType.DMA
    results = pl.pallas_call(
        kernel,
        out_shape=(
            pltpu.VMEM((64, 8192), BF),
            pltpu.VMEM((TOK, 512), BF),
            pltpu.VMEM((128, 512), BF),
            pltpu.VMEM((128, 512), BF),
            pltpu.VMEM((512, 512), BF),
        ),
        in_specs=[hbm, hbm, hbm, hbm, vmem, pl.BlockSpec(memory_space=pltpu.SMEM), hbm],
        out_specs=[vmem] * 5,
        scratch_shapes=[
            pltpu.VMEM((512, 8192), BF),
            pltpu.VMEM((CH, TOK, WC), BF),
            pltpu.VMEM((CH, TOK, HALF), BF),
            pltpu.VMEM((AUD, 512), BF),
            pltpu.VMEM((2 * TOK, 256), BF),
            pltpu.VMEM((16, 2 * TOK), F32),
            pltpu.VMEM((512, 2 * TOK), BF),
            pltpu.VMEM((TOK, 512), BF),
            pltpu.VMEM((512, TOK), F32),
            pltpu.VMEM((512, TOK), BF),
            pltpu.VMEM((256, 2 * TOK), BF),
            pltpu.VMEM((AUD, TOK), F32),
            pltpu.VMEM((AUD, TOK), BF),
            pltpu.VMEM((2, 1, 2 * TOK), F32),
            pltpu.VMEM((1, 2 * TOK), F32),
            pltpu.VMEM((HD, 2 * TOK), F32),
            pltpu.VMEM((TOK, 256), BF),
            pltpu.VMEM((TOK, 256), BF),
            pltpu.VMEM((CH, 64, WC), BF),
            pltpu.VMEM((CH, 64, WC), BF),
            pltpu.VMEM((CH, 128, WC), BF),
            pltpu.VMEM((CH, 128, WC), BF),
            pltpu.VMEM((CH, 64, WC), BF),
            pltpu.VMEM((3, 4, 64, WC), BF),
            pltpu.VMEM((CH, 512, HALF), BF),
            pltpu.VMEM((CH - 2, 512, HALF), BF),
            pltpu.VMEM((512, HALF), BF),
            pltpu.VMEM((2, AUD, 256), BF),
            pltpu.VMEM((2, 3, 512, 256), BF),
            pltpu.VMEM((2, 4, 128, 256), BF),
            dma((KINDS, CH)), dma((KINDS, CH)),
            dma((4, 2)), dma((4, 2)),
            dma((4,)), dma((4,)),
            dma((2, 4)), dma((2, 4)),
            dma((2, 4)), dma((2, 4)),
            dma((5,)), dma((5,)),
            dma((CH + 4,)),
        ],
        compiler_params=pltpu.CompilerParams(
            collective_id=0, has_side_effects=True, vmem_limit_bytes=58 * 2**20
        ),
        cost_estimate=pl.CostEstimate(flops=20 * 10**9, bytes_accessed=16 * 2**20, transcendentals=8 * 2**20),
    )(queries, audio_keys, audio_values, out_weight, mix_gate.reshape(1, 1), block_mask, cotangent)
    results = [pltpu.with_memory_space_constraint(r, pltpu.VMEM) for r in results]
    return pl.pallas_call(
        hand_over,
        out_shape=tuple(jax.ShapeDtypeStruct(r.shape, r.dtype) for r in results),
        in_specs=[vmem] * 5,
        out_specs=[hbm] * 5,
        scratch_shapes=[dma((5,))],
    )(*results)


def solution(mesh):
    in_specs = (
        P("seq", "tp"),
        P("seq", "tp"),
        P("seq", "tp"),
        P("tp", None),
        P(),
        P("seq", None),
        P(("seq", "tp"), None),
    )
    out_specs = (
        P(("seq", "tp"), None),
        P("seq", "tp"),
        P("seq", "tp"),
        P("seq", "tp"),
        P("tp", "seq"),
    )
    return jax.shard_map(
        per_device, mesh=mesh, in_specs=in_specs, out_specs=out_specs, check_vma=False
    )
```

```python
import jax
import jax.numpy as jnp
from jax import lax
from jax.experimental import pallas as pl
from jax.experimental.pallas import tpu as pltpu
from jax.sharding import PartitionSpec as P

HD = 128
BLK = 128
CH = 8
WC = 1024
HALF = 512
TOK = 512
AUD = 2048
SCALE = HD ** (-0.5)
C2 = SCALE * 1.4426950408889634
NEG = -1e30
BF = jnp.bfloat16
F32 = jnp.float32
MESH = pl.DeviceIdType.MESH

NT = (((1,), (1,)), ((), ()))
NN = (((1,), (0,)), ((), ()))
TN = (((0,), (0,)), ((), ()))

AGY, AGP, AGM, AFP, AFM, SIB, GW, F1, F2, R1, R2, YX, YP, YM, YF, P0 = range(16)
R3, R4 = P0 + 4, P0 + 5
KINDS = P0 + 6
GATHER_X = (3, 5)
SCATTER_Y = (1, 3, 5)
TICKS = 54
PLAN = (
    ('F', (18, 19, 22, 24, 28, 29, 30, 36), (5, 7, 3, 2, 0, 6, 1, 4)),
    ('GP', (32,), (0,)),
    ('B', (0, 1, 7, 8, 9, 10, 11, 15), (3, 5, 4, 2, 7, 0, 1, 6)),
    ('D', (9, 10, 16, 17, 23, 24, 26, 28), (5, 3, 2, 7, 0, 4, 6, 1)),
    ('GH', (29,), (0,)),
    ('KF', (47, 48), (1, 0)),
    ('X', (15, 17), (5, 3)),
    ('E', (15, 19, 20, 22, 24, 25, 27, 28), (5, 7, 2, 3, 0, 4, 6, 1)),
    ('K0', (0,), (0,)),
    ('LB', (30, 31, 32, 33, 37, 38, 39, 40), (5, 2, 7, 0, 3, 6, 1, 4)),
    ('C', (4, 6, 9, 10, 11, 18, 20, 21), (3, 5, 2, 7, 4, 0, 6, 1)),
    ('LA', (18, 22, 23, 26, 28, 29, 31, 36), (5, 7, 3, 2, 0, 6, 1, 4)),
    ('A', (0, 1, 2, 3, 4, 5, 8, 9), (4, 2, 0, 7, 1, 3, 5, 6)),
    ('BW', (31, 33, 34, 35), (0, 1, 2, 3)),
    ('DQ', (40,), (0,)),
    ('L0', (7,), (0,)),
    ('FW', (11, 12, 13, 14), (0, 1, 2, 3)),
    ('LC', (36, 40, 41, 42, 43, 44, 45, 46), (7, 0, 5, 2, 1, 6, 3, 4)),
    ('KR', (39, 45), (0, 1)),
    ('LD', (45, 46, 48, 49, 50, 51, 52, 53), (0, 5, 1, 6, 7, 2, 4, 3)),
    ('HR', (17,), (0,)),
    ('GF', (53,), (0,)),
    ('HX', (14,), (0,)),
    ('K1', (5,), (0,)),
    ('DF', (43,), (0,)),
)


def dot(a, b, dims):
    return lax.dot_general(a, b, dims, preferred_element_type=F32)


def kernel(
    q_hbm, k_hbm, v_hbm, w_hbm, gate_ref, mask_ref, cot_hbm,
    layer_ref, dq_ref, dk_ref, dv_ref, gw_ref,
    w, cot, cot_sib, kvb, q2, mask2, ht, hrow, gh_acc, gh_own, gh2,
    sc, pb, lse, delta, dq_acc, dq_out, dq_in, f1b, f2b, r1b, r2b, yr, p4b, gw_out, gw_in, gw_par, kv_out, kv_in, kv_fin,
    ss, rs, ps, pr, zs, zr, ds_, dr, fs, fr, es, er, ls,
):
    s = lax.axis_index("seq")
    t = lax.axis_index("tp")
    core = s % 2
    z = s // 4
    yl = (s // 2) % 2
    x = t // 2
    yh = t % 2
    xn, xb, xf = (x + 1) % 4, (x + 3) % 4, (x + 2) % 4
    sib = (s + 1 - 2 * core, t)
    nxt = (s, xn * 2 + yh)
    prv = (s, xb * 2 + yh)
    par = (s, x * 2 + 1 - yh)

    def zdev(dz):
        return (((z + dz) % 4) * 4 + yl * 2 + core, t)

    def near(n):
        return (z * 4 + ((yl + n // 2) % 2) * 2 + (core + n) % 2, t)

    def rows(start, size):
        return pl.ds(pl.multiple_of(start, size), size)

    def cols(start, size):
        return pl.ds(pl.multiple_of(start, 128), size)

    def chunk(i):
        m = i // 2
        zz = ((z // 2 + m // 2) % 2) * 2 + (z + m) % 2
        return zz * 2 + (yl + i) % 2

    def copy(kind, i, src, dst, dev):
        return pltpu.make_async_remote_copy(
            src_ref=src, dst_ref=dst, send_sem=ss.at[kind, i], recv_sem=rs.at[kind, i],
            device_id=dev, device_id_type=MESH,
        )

    def got(kind, i, dst):
        copy(kind, i, dst, dst, nxt).wait_recv()

    def sent(kind, i, src):
        copy(kind, i, src, src, nxt).wait_send()

    barrier = pltpu.get_barrier_semaphore()
    for dev in (nxt, prv, par):
        pl.semaphore_signal(barrier, inc=1, device_id=dev, device_id_type=MESH)

    for n in range(1, 4):
        pl.semaphore_signal(barrier, inc=1, device_id=near(n), device_id_type=MESH)
        pl.semaphore_signal(barrier, inc=1, device_id=zdev(n), device_id_type=MESH)

    def own_piece(i):
        return pltpu.make_async_copy(
            cot_hbm.at[:, cols(chunk(i) * WC, WC)], cot.at[i, rows(t * 64, 64), :], ls.at[i]
        )

    def start_piece(i, c):
        own_piece(i).start()
        return c

    w_copy = pltpu.make_async_copy(w_hbm, w, ls.at[CH])
    my_heads = cols(core * 256, 256)
    k_copy = pltpu.make_async_copy(k_hbm.at[:, my_heads], kvb.at[rows(s * 128, 128), pl.ds(0, 256)], ls.at[CH + 1])
    v_copy = pltpu.make_async_copy(v_hbm.at[:, my_heads], kvb.at[rows(s * 128, 128), pl.ds(256, 256)], ls.at[CH + 2])
    q_copy = pltpu.make_async_copy(q_hbm.at[:, my_heads], q2.at[rows(core * TOK, TOK), :], ls.at[CH + 3])

    pl.semaphore_wait(barrier, 9)

    def stage_a(i):
        copy(AGY, i, cot_hbm.at[:, cols(chunk(i) * WC, WC)], cot.at[i, rows(t * 64, 64), :], par).start()

    def piece_x(i):
        src = cot_hbm.at[:, cols(chunk(i) * WC, WC)]
        dst = cot.at[i, rows(t * 64, 64), :]
        copy(AGP, i, src, dst, nxt).start()
        copy(AGM, i, src, dst, prv).start()


    def extra(n, src, dst):
        return pltpu.make_async_remote_copy(
            src_ref=src, dst_ref=dst, send_sem=es.at[n], recv_sem=er.at[n], device_id=sib, device_id_type=MESH
        )

    other_heads = cols((1 - core) * 256, 256)
    q_send = extra(0, q_hbm.at[:, other_heads], q2.at[rows(core * TOK, TOK), :])
    my_mask = mask2.at[:, cols(core * TOK, TOK)]
    m_send = extra(1, my_mask, my_mask)

    def prepare():
        gh_acc[...] = jnp.zeros_like(gh_acc)
        for tb in range(TOK // BLK):
            for ab in range(AUD // BLK):
                seen = jnp.full((1, BLK), mask_ref[tb, ab].astype(F32))
                mask2[pl.ds(ab, 1), cols(core * TOK + tb * BLK, BLK)] = seen
        q_send.start()
        m_send.start()

    def kv_near(n, src_rows):
        heads = cols(((core + n) % 2) * 256, 256)
        return [
            pltpu.make_async_remote_copy(
                src_ref=src.at[:, heads], dst_ref=kvb.at[src_rows, pl.ds(part * 256, 256)],
                send_sem=ps.at[n, part], recv_sem=pr.at[n, part], device_id=near(n), device_id_type=MESH)
            for part, src in enumerate((k_hbm, v_hbm))
        ]

    def kv_far(dz, zz):
        block = kvb.at[rows(zz * 512, 512), :]
        return pltpu.make_async_remote_copy(
            src_ref=block, dst_ref=block, send_sem=zs.at[dz], recv_sem=zr.at[dz],
            device_id=zdev(dz), device_id_type=MESH)

    def kv_share():
        for n in range(1, 4):
            for copy_ in kv_near(n, rows(s * 128, 128)):
                copy_.start()

        for c in (k_copy, v_copy):
            c.start()
        lax.fori_loop(0, CH, start_piece, 0)
        for c in (q_copy, w_copy):
            c.start()

    def kv_spread():
        k_copy.wait()
        v_copy.wait()
        for n in range(1, 4):
            src = z * 4 + ((yl + n // 2) % 2) * 2 + (core + n) % 2
            for copy_ in kv_near(n, rows(src * 128, 128)):
                copy_.wait_recv()
        for dz in (1, 3, 2):
            kv_far(dz, z).start()

    gate = jnp.tanh(gate_ref[...])

    def stage_b1(i):
        own_piece(i).wait()
        got(AGY, i, cot.at[i, rows((x * 2 + 1 - yh) * 64, 64), :])
        block = cot.at[i, rows(x * 128, 128), :]
        copy(AGP, i, block, block, nxt).start()
        copy(AGM, i, block, block, prv).start()

    def stage_c1(i):
        got(AGP, i, cot.at[i, rows(xb * 128, 128), :])
        top = cot.at[i, rows(xb * 128, 64), :]
        copy(AFP, i, top, top, nxt).start()
        got(AGM, i, cot.at[i, rows(xn * 128, 128), :])
        low = cot.at[i, rows(xn * 128 + 64, 64), :]
        copy(AFM, i, low, low, prv).start()

    def stage_d1(i):
        got(AFP, i, cot.at[i, rows(xf * 128, 64), :])
        got(AFM, i, cot.at[i, rows(xf * 128 + 64, 64), :])
        share(i)

    def share(i):
        copy(SIB, i, cot.at[i, :, cols((1 - core) * HALF, HALF)], cot_sib.at[i], sib).start()

    def to_partner(kind, i, xx):
        block = cot.at[i, rows(xx * 128 + yh * 64, 64), :]
        copy(kind, i, block, block, par).start()

    def stage_c2(i):
        got(AGP, i, cot.at[i, rows(xb * 128 + yh * 64, 64), :])
        top = cot.at[i, rows(xb * 128 + yh * 64, 32), :]
        copy(AFP, i, top, top, nxt).start()
        got(AGM, i, cot.at[i, rows(xn * 128 + yh * 64, 64), :])
        low = cot.at[i, rows(xn * 128 + yh * 64 + 32, 32), :]
        copy(AFM, i, low, low, prv).start()
        to_partner(YP, i, xb)
        to_partner(YM, i, xn)

    def stage_d2(i):
        got(AFP, i, cot.at[i, rows(xf * 128 + yh * 64, 32), :])
        got(AFM, i, cot.at[i, rows(xf * 128 + yh * 64 + 32, 32), :])
        to_partner(YF, i, xf)

    def stage_x2(i):
        own_piece(i).wait()
        for kind, xx in ((AGY, x), (YP, xb), (YM, xn), (YF, xf)):
            got(kind, i, cot.at[i, rows(xx * 128 + (1 - yh) * 64, 64), :])
        share(i)

    def either(first, second, cond):
        def stage(i):
            @pl.when(cond(i))
            def _():
                first(i)

            @pl.when(jnp.logical_not(cond(i)))
            def _():
                second(i)

        return stage

    def member(i, chosen):
        hit = i < 0
        for n in chosen:
            hit = jnp.logical_or(hit, i == n)
        return hit

    def gathers_x(i):
        return member(i, GATHER_X)

    stage_b = either(piece_x, stage_b1, gathers_x)
    stage_c = either(stage_c2, stage_c1, gathers_x)
    stage_d = either(stage_d2, stage_d1, gathers_x)

    def gather_sent(i):
        @pl.when(gathers_x(i))
        def _():
            for kind in (AGP, AGM, YP, YM, YF):
                sent(kind, i, cot.at[i, rows(x * 128, 64), :])
            for kind in (AFP, AFM):
                sent(kind, i, cot.at[i, rows(x * 128, 32), :])

        @pl.when(jnp.logical_not(gathers_x(i)))
        def _():
            for kind in (AGP, AGM):
                sent(kind, i, cot.at[i, rows(x * 128, 128), :])
            for kind in (AFP, AFM):
                sent(kind, i, cot.at[i, rows(x * 128, 64), :])

    def stage_e(i):
        cc = cols(chunk(i) * WC, WC)
        for part in range(2):
            rr = pl.ds(part * 256, 256)
            gh_acc[rr, :] += dot(w[rr, cc], cot[i], NT)

    def stage_f(i):
        got(SIB, i, cot_sib.at[i])
        mine = cols(core * TOK, TOK)
        theirs = cols((1 - core) * TOK, TOK)
        for part in range(2):
            rr = pl.ds(part * 256, 256)
            val = dot(ht[rr, mine], cot[i, :, cols(core * HALF, HALF)], NN) + dot(ht[rr, theirs], cot_sib[i], NN)
            gw_out[i, rr, :] = val.astype(BF)

        @pl.when(i > 1)
        def _():
            zz = chunk(i) // 2
            copy(GW, i, gw_out.at[i], gw_in.at[i - 2], (zz * 4 + yl * 2 + core, t)).start()

    def product(i):
        gather_sent(i)
        sent(SIB, i, cot_sib.at[i])
        for part in range(2):
            cc = cols(chunk(i) * WC + part * HALF, HALF)
            cot[i, :, pl.ds(part * HALF, HALF)] = dot(hrow[...], w[:, cc], NN).astype(BF)

    def stage_la1(i):
        product(i)
        copy(F1, i, cot.at[i, rows(xf * 128, 64), :], f1b.at[i], nxt).start()
        copy(F2, i, cot.at[i, rows(xf * 128 + 64, 64), :], f2b.at[i], prv).start()

    def stage_lb1(i):
        top, low = pl.ds(0, 64), pl.ds(64, 64)
        copy(R3, i, cot.at[i, rows(xn * 128 + 64, 64), :], r1b.at[i, low, :], nxt).start()
        copy(R4, i, cot.at[i, rows(xb * 128, 64), :], r2b.at[i, top, :], prv).start()
        got(F1, i, f1b.at[i])
        rr = rows(xn * 128, 64)
        cot[i, rr, :] = (cot[i, rr, :].astype(F32) + f1b[i].astype(F32)).astype(BF)
        copy(R1, i, cot.at[i, rr, :], r1b.at[i, top, :], nxt).start()
        got(F2, i, f2b.at[i])
        rr = rows(xb * 128 + 64, 64)
        cot[i, rr, :] = (cot[i, rr, :].astype(F32) + f2b[i].astype(F32)).astype(BF)
        copy(R2, i, cot.at[i, rr, :], r2b.at[i, low, :], prv).start()

    def reduced(i, which):
        rr = rows(which * 64, 64)
        return (
            cot[i, rows(x * 128 + which * 64, 64), :].astype(F32)
            + r1b[i, rr, :].astype(F32)
            + r2b[i, rr, :].astype(F32)
        )

    def stage_lc1(i):
        top, low = pl.ds(0, 64), pl.ds(64, 64)
        got(R1, i, r1b.at[i, top, :])
        got(R3, i, r1b.at[i, low, :])
        got(R2, i, r2b.at[i, low, :])
        got(R4, i, r2b.at[i, top, :])
        rr = rows(x * 128 + (1 - yh) * 64, 64)
        cot[i, rr, :] = reduced(i, 1 - yh).astype(BF)
        copy(YX, i, cot.at[i, rr, :], yr.at[i], par).start()

    def stage_ld1(i):
        got(YX, i, yr.at[i])
        total = reduced(i, yh) + yr[i].astype(F32)
        layer_ref[:, cols(chunk(i) * WC, WC)] = (gate * total).astype(BF)

    def slot(i):
        return sum((i > n).astype(jnp.int32) for n in SCATTER_Y)

    def stage_la2(i):
        product(i)
        for n in range(4):
            copy(P0 + n, i, cot.at[i, rows(n * 128 + (1 - yh) * 64, 64), :], p4b.at[slot(i), n], par).start()

    def add_partner(i, xx):
        rr = rows(xx * 128 + yh * 64, 64)
        return cot[i, rr, :].astype(F32) + p4b[slot(i), xx].astype(F32)

    def stage_lb2(i):
        for n in range(4):
            got(P0 + n, i, p4b.at[slot(i), n])
        rr = rows(xf * 128 + yh * 64, 64)
        cot[i, rr, :] = add_partner(i, xf).astype(BF)
        copy(F1, i, cot.at[i, rows(xf * 128 + yh * 64, 32), :], f1b.at[i, pl.ds(0, 32), :], nxt).start()
        copy(F2, i, cot.at[i, rows(xf * 128 + yh * 64 + 32, 32), :], f2b.at[i, pl.ds(0, 32), :], prv).start()

    def stage_lc2(i):
        top, low = pl.ds(0, 32), pl.ds(0, 64)
        got(F1, i, f1b.at[i, top, :])
        val = add_partner(i, xn)
        cot[i, rows(xn * 128 + yh * 64, 32), :] = (val[:32] + f1b[i, top, :].astype(F32)).astype(BF)
        cot[i, rows(xn * 128 + yh * 64 + 32, 32), :] = val[32:].astype(BF)
        copy(R1, i, cot.at[i, rows(xn * 128 + yh * 64, 64), :], r1b.at[i, low, :], nxt).start()
        got(F2, i, f2b.at[i, top, :])
        val = add_partner(i, xb)
        cot[i, rows(xb * 128 + yh * 64, 32), :] = val[:32].astype(BF)
        cot[i, rows(xb * 128 + yh * 64 + 32, 32), :] = (val[32:] + f2b[i, top, :].astype(F32)).astype(BF)
        copy(R2, i, cot.at[i, rows(xb * 128 + yh * 64, 64), :], r2b.at[i, low, :], prv).start()

    def stage_ld2(i):
        low = pl.ds(0, 64)
        got(R1, i, r1b.at[i, low, :])
        got(R2, i, r2b.at[i, low, :])
        total = add_partner(i, x) + r1b[i, low, :].astype(F32) + r2b[i, low, :].astype(F32)
        layer_ref[:, cols(chunk(i) * WC, WC)] = (gate * total).astype(BF)

    def chunk_sent(i):
        sent(AGY, i, cot.at[i, rows(x * 128, 64), :])

        @pl.when(scatters_y(i))
        def _():
            for n in range(4):
                sent(P0 + n, i, p4b.at[slot(i), n])
            for kind in (F1, F2):
                sent(kind, i, cot.at[i, rows(x * 128, 32), :])
            for kind in (R1, R2):
                sent(kind, i, cot.at[i, rows(x * 128, 64), :])

        @pl.when(jnp.logical_not(scatters_y(i)))
        def _():
            sent(F1, i, f1b.at[i])
            sent(F2, i, f2b.at[i])
            for kind in (R1, R2, R3, R4):
                sent(kind, i, cot.at[i, rows(x * 128, 64), :])
            sent(YX, i, yr.at[i])

    def scatters_y(i):
        return member(i, SCATTER_Y)

    stage_la = either(stage_la2, stage_la1, scatters_y)
    stage_lb = either(stage_lb2, stage_lb1, scatters_y)
    stage_lc = either(stage_lc2, stage_lc1, scatters_y)
    stage_ld_ = either(stage_ld2, stage_ld1, scatters_y)

    def stage_ld(i):
        stage_ld_(i)
        chunk_sent(i)

    def masked(score, row, tok):
        return jnp.where(mask2[pl.ds(row, 1), tok] > 0, score, NEG)

    def forward(j):
        hh, u = j // 2, j % 2
        hc = cols(hh * HD, HD)
        vc = cols(256 + hh * HD, HD)
        tok = cols(u * TOK, TOK)
        qv = q2[rows(u * TOK, TOK), hc]

        def scores(ab, best):
            part = dot(kvb[rows(ab * 256, 256), hc], qv, NT)
            for b in range(2):
                val = masked(part[b * 128 : (b + 1) * 128], ab * 2 + b, tok)
                sc[rows(ab * 256 + b * 128, 128), :] = val
                best = jnp.maximum(best, jnp.max(val, axis=0, keepdims=True))
            return best

        best = lax.fori_loop(0, AUD // 256, scores, jnp.full((1, TOK), NEG, F32))

        def weigh(ab, total):
            rr = rows(ab * 256, 256)
            val = jnp.exp2((sc[rr, :] - best) * C2)
            pb[rr, :] = val.astype(BF)
            return total + jnp.sum(val, axis=0, keepdims=True)

        total = lax.fori_loop(0, AUD // 256, weigh, jnp.zeros((1, TOK), F32))
        out = dot(kvb[:, vc], pb[...], TN)
        ht[rows(core * 256 + hh * HD, HD), tok] = (out / total).astype(BF)
        lse[hh, :, tok] = best * C2 + jnp.log2(total)

    def kv_z(hh, dz):
        return pltpu.make_async_remote_copy(
            src_ref=kv_out.at[hh, rows(((z + dz) % 4) * 512, 512), :], dst_ref=kv_in.at[hh, dz - 1],
            send_sem=ds_.at[hh, dz], recv_sem=dr.at[hh, dz], device_id=zdev(dz), device_id_type=MESH)

    def kv_y(hh, n):
        src = ((yl + n // 2) % 2) * 2 + (core + n) % 2
        return pltpu.make_async_remote_copy(
            src_ref=kv_out.at[hh, rows(z * 512 + src * 128, 128), :], dst_ref=kv_fin.at[hh, n],
            send_sem=fs.at[hh, n], recv_sem=fr.at[hh, n], device_id=near(n), device_id_type=MESH)

    def kv_reduce(hh):
        for dz in range(1, 4):
            kv_z(hh, dz).wait_recv()
        for b in range(4):
            total = kv_out[hh, rows(z * 512 + b * 128, 128), :].astype(F32)
            for dz in range(3):
                total += kv_in[hh, dz, b * 128 : (b + 1) * 128, :].astype(F32)
            kv_out[hh, rows(z * 512 + b * 128, 128), :] = total.astype(BF)
        for n in range(1, 4):
            kv_y(hh, n).start()
        for dz in range(1, 4):
            kv_z(hh, dz).wait_send()

    def kv_finish(hh):
        for n in range(1, 4):
            kv_y(hh, n).wait_recv()
        same = kv_out[hh, rows(s * 128, 128), :].astype(F32) + kv_fin[hh, 2].astype(F32)
        other = kv_fin[hh, 1].astype(F32) + kv_fin[hh, 3].astype(F32)
        hc = cols(core * 256 + hh * HD, HD)
        dk_ref[:, hc] = same[:, :HD].astype(BF)
        dv_ref[:, hc] = same[:, HD:].astype(BF)
        hc = cols((1 - core) * 256 + hh * HD, HD)
        dk_ref[:, hc] = other[:, :HD].astype(BF)
        dv_ref[:, hc] = other[:, HD:].astype(BF)
        for n in range(1, 4):
            kv_y(hh, n).wait_send()

    gw_send = pltpu.make_async_remote_copy(
        src_ref=gw_out.at[1], dst_ref=gw_par, send_sem=fs.at[0, 0], recv_sem=fr.at[0, 0],
        device_id=near(2), device_id_type=MESH)

    def gw_reduce(which, write):
        def got_one(i, c):
            got(GW, 2 * i + which, gw_in.at[2 * i + which - 2])
            return c

        lax.fori_loop(1, 4, got_one, 0)

        def add(b, c):
            rr = rows(b * 64, 64)
            total = gw_out[which, rr, :].astype(F32)
            for i in range(3):
                total += gw_in[2 * i + which, rr, :].astype(F32)
            write(rr, total)
            return c

        lax.fori_loop(0, 8, add, 0)

    def gw_part():
        def write(rr, total):
            gw_out[1, rr, :] = total.astype(BF)

        gw_reduce(1, write)
        gw_send.start()

    def gw_finish():
        gw_send.wait_recv()

        def write(rr, total):
            gw_ref[rr, :] = (gate * (total + gw_par[rr, :].astype(F32))).astype(BF)

        gw_reduce(0, write)
        gw_send.wait_send()

        def gw_left(i, c):
            sent(GW, i, gw_out.at[i])
            return c

        lax.fori_loop(2, CH, gw_left, 0)

    def backward(j):
        hh = j // 2
        ah = (j + 1 + z // 2) % 2
        hc = cols(hh * HD, HD)
        hr = rows(hh * HD, HD)
        first = j % 2 == 0

        @pl.when(first)
        def _():
            dq_acc[...] = jnp.zeros_like(dq_acc)
            own = ht[rows(core * 256 + hh * HD, HD), :].astype(F32)
            delta[...] = jnp.sum(gh2[hr, :].astype(F32) * own, axis=0, keepdims=True)

        def step(b, c):
            rr = rows(ah * 1024 + b * 256, 256)
            kk = kvb[rr, hc]
            vv = kvb[rr, cols(256 + hh * HD, HD)]
            qv = q2[:, hc]
            gv = gh2[hr, :]
            score = dot(kk, qv, NT)
            logs = lse[hh]
            probs = []
            for m in range(2):
                row = ah * 8 + b * 2 + m
                val = masked(score[m * 128 : (m + 1) * 128], row, slice(None))
                probs.append(jnp.exp2(val * C2 - logs))
            prob = jnp.concatenate(probs, axis=0)
            dp = dot(vv, gv, NN)
            dsc = (prob * (dp - delta[...])).astype(BF)
            kv_out[hh, rr, pl.ds(HD, HD)] = dot(prob.astype(BF), gv, NT).astype(BF)
            kv_out[hh, rr, pl.ds(0, HD)] = (SCALE * dot(dsc, qv, NN)).astype(BF)
            dq_acc[...] += dot(kk, dsc, TN)
            return c

        lax.fori_loop(0, 4, step, 0)

        for b in range(2):
            dz = (ah * 2 + b - z + 4) % 4

            @pl.when(dz > 0)
            def _():
                kv_z(hh, dz).start()

        @pl.when(j % 2 == 1)
        def _():
            full = SCALE * dq_acc[...]
            for u in range(2):
                piece = full[:, u * TOK : (u + 1) * TOK].T.astype(BF)

                @pl.when(core == u)
                def _():
                    dq_ref[:, cols(core * 256 + hh * HD, HD)] = piece

                @pl.when(core != u)
                def _():
                    dq_out[:, hc] = piece

    mine_rows = rows(core * 256, 256)
    ht_send = extra(2, ht.at[mine_rows, :], ht.at[mine_rows, :])
    their_rows = rows((1 - core) * 256, 256)
    gh_send = extra(3, gh_own.at[their_rows, :], gh2.at[:, cols(core * TOK, TOK)])
    dq_send = extra(4, dq_out, dq_in)

    def heads_first():
        q_copy.wait()
        other_q = q2.at[rows((1 - core) * TOK, TOK), :]
        extra(0, other_q, other_q).wait_recv()
        other_m = mask2.at[:, cols((1 - core) * TOK, TOK)]
        extra(1, other_m, other_m).wait_recv()
        for dz in range(1, 4):
            kv_far(dz, (z - dz + 4) % 4).wait_recv()

    def on_first(i, fn):
        @pl.when(i == 0)
        def _():
            fn()

    def stage_fw(j):
        on_first(j, heads_first)
        forward(j)

    def gh_got():
        other = gh2.at[:, cols((1 - core) * TOK, TOK)]
        extra(3, other, other).wait_recv()

    def stage_bw(j):
        on_first(j, gh_got)
        backward(j)

    def stage_hr():
        extra(2, ht.at[their_rows, :], ht.at[their_rows, :]).wait_recv()
        hrow[...] = ht[:, cols(core * TOK, TOK)].astype(F32).T.astype(BF)
        q_send.wait_send()
        m_send.wait_send()
        ht_send.wait_send()
        for n in range(1, 4):
            for copy_ in kv_near(n, rows(s * 128, 128)):
                copy_.wait_send()
            kv_far(n, z).wait_send()

    def stage_gh():
        gh_own[...] = (gate * gh_acc[...]).astype(BF)
        gh2[:, cols(core * TOK, TOK)] = gh_own[mine_rows, :]
        gh_send.start()

    def stage_df():
        dq_send.wait_recv()
        dq_ref[:, cols((1 - core) * 256, 256)] = dq_in[...]
        dq_send.wait_send()
        gh_send.wait_send()

    once = {
        "L0": prepare, "K0": kv_share, "K1": kv_spread, "HX": ht_send.start, "HR": stage_hr, "GH": stage_gh,
        "GP": gw_part, "GF": gw_finish, "DQ": dq_send.start, "DF": stage_df,
    }
    each = {
        "A": stage_a, "B": stage_b, "C": stage_c, "D": stage_d, "X": stage_x2, "E": stage_e, "F": stage_f,
        "LA": stage_la, "LB": stage_lb, "LC": stage_lc, "LD": stage_ld,
        "FW": stage_fw, "BW": stage_bw, "KR": kv_reduce, "KF": kv_finish,
    }
    w_tick = min(ticks[0] for name, ticks, _ in PLAN if name == "E")

    def packed(ticks, low):
        return jnp.int32(sum(1 << (n - low) for n in ticks if low <= n < low + 30))

    def tick(g, state):
        after = []
        for (name, ticks, idx), (bits, order) in zip(PLAN, state):
            for low in range(30, TICKS, 30):
                bits = jnp.where(g == low, packed(ticks, low), bits)
            hit = bits % 2 == 1
            if name == "E":

                @pl.when(g == w_tick)
                def _():
                    w_copy.wait()

            @pl.when(hit)
            def _():
                if name in once:
                    once[name]()
                else:
                    each[name](order % 8)

            after.append((bits // 2, jnp.where(hit, order // 8, order)))
        return tuple(after)

    start = tuple(
        (packed(ticks, 0), jnp.int32(sum(i << (3 * n) for n, i in enumerate(idx)))) for _, ticks, idx in PLAN
    )
    lax.fori_loop(0, TICKS, tick, start)


def hand_over(*refs):
    given, results, sems = refs[:5], refs[5:10], refs[10]
    outs = [pltpu.make_async_copy(given[n], results[n], sems.at[n]) for n in range(5)]
    for c in outs:
        c.start()
    for c in outs:
        c.wait()


def per_device(queries, audio_keys, audio_values, out_weight, mix_gate, block_mask, cotangent):
    hbm = pl.BlockSpec(memory_space=pl.ANY)
    vmem = pl.BlockSpec(memory_space=pltpu.VMEM)
    dma = pltpu.SemaphoreType.DMA
    results = pl.pallas_call(
        kernel,
        out_shape=(
            pltpu.VMEM((64, 8192), BF),
            pltpu.VMEM((TOK, 512), BF),
            pltpu.VMEM((128, 512), BF),
            pltpu.VMEM((128, 512), BF),
            pltpu.VMEM((512, 512), BF),
        ),
        in_specs=[hbm, hbm, hbm, hbm, vmem, pl.BlockSpec(memory_space=pltpu.SMEM), hbm],
        out_specs=[vmem] * 5,
        scratch_shapes=[
            pltpu.VMEM((512, 8192), BF),
            pltpu.VMEM((CH, TOK, WC), BF),
            pltpu.VMEM((CH, TOK, HALF), BF),
            pltpu.VMEM((AUD, 512), BF),
            pltpu.VMEM((2 * TOK, 256), BF),
            pltpu.VMEM((16, 2 * TOK), F32),
            pltpu.VMEM((512, 2 * TOK), BF),
            pltpu.VMEM((TOK, 512), BF),
            pltpu.VMEM((512, TOK), F32),
            pltpu.VMEM((512, TOK), BF),
            pltpu.VMEM((256, 2 * TOK), BF),
            pltpu.VMEM((AUD, TOK), F32),
            pltpu.VMEM((AUD, TOK), BF),
            pltpu.VMEM((2, 1, 2 * TOK), F32),
            pltpu.VMEM((1, 2 * TOK), F32),
            pltpu.VMEM((HD, 2 * TOK), F32),
            pltpu.VMEM((TOK, 256), BF),
            pltpu.VMEM((TOK, 256), BF),
            pltpu.VMEM((CH, 64, WC), BF),
            pltpu.VMEM((CH, 64, WC), BF),
            pltpu.VMEM((CH, 128, WC), BF),
            pltpu.VMEM((CH, 128, WC), BF),
            pltpu.VMEM((CH, 64, WC), BF),
            pltpu.VMEM((3, 4, 64, WC), BF),
            pltpu.VMEM((CH, 512, HALF), BF),
            pltpu.VMEM((CH - 2, 512, HALF), BF),
            pltpu.VMEM((512, HALF), BF),
            pltpu.VMEM((2, AUD, 256), BF),
            pltpu.VMEM((2, 3, 512, 256), BF),
            pltpu.VMEM((2, 4, 128, 256), BF),
            dma((KINDS, CH)), dma((KINDS, CH)),
            dma((4, 2)), dma((4, 2)),
            dma((4,)), dma((4,)),
            dma((2, 4)), dma((2, 4)),
            dma((2, 4)), dma((2, 4)),
            dma((5,)), dma((5,)),
            dma((CH + 4,)),
        ],
        compiler_params=pltpu.CompilerParams(
            collective_id=0, has_side_effects=True, vmem_limit_bytes=58 * 2**20
        ),
        cost_estimate=pl.CostEstimate(flops=20 * 10**9, bytes_accessed=16 * 2**20, transcendentals=8 * 2**20),
    )(queries, audio_keys, audio_values, out_weight, mix_gate.reshape(1, 1), block_mask, cotangent)
    results = [pltpu.with_memory_space_constraint(r, pltpu.VMEM) for r in results]
    return pl.pallas_call(
        hand_over,
        out_shape=tuple(jax.ShapeDtypeStruct(r.shape, r.dtype) for r in results),
        in_specs=[vmem] * 5,
        out_specs=[hbm] * 5,
        scratch_shapes=[dma((5,))],
    )(*results)


def solution(mesh):
    in_specs = (
        P("seq", "tp"),
        P("seq", "tp"),
        P("seq", "tp"),
        P("tp", None),
        P(),
        P("seq", None),
        P(("seq", "tp"), None),
    )
    out_specs = (
        P(("seq", "tp"), None),
        P("seq", "tp"),
        P("seq", "tp"),
        P("seq", "tp"),
        P("tp", "seq"),
    )
    return jax.shard_map(
        per_device, mesh=mesh, in_specs=in_specs, out_specs=out_specs, check_vma=False
    )
```
